32 devices in a mesh: tm: 8 (over z, x), row: 2 (over y), col: 2 (over core).
Axes of the slice: x: 2, y: 2, z: 4, core: 2. Of those that a mesh axis runs over, the one named last changes fastest.
Arguments:
- features: bfloat16 [16, 12, 32, 512], P('tm', 'row', 'col'), may hold values from -16 to 16, as said below
- gn1_gain: float32 [512], replicated, may hold values from 0.1 to 1.9
- gn1_bias: float32 [512], replicated, may hold values from -3 to 3
- conv1_weight: bfloat16 [27, 512, 256], P(None, ('row', 'col')), may hold values from -0.0546875 to 0.0546875
- conv1_bias: float32 [256], replicated, may hold values from -3 to 3
- skip_weight: bfloat16 [1, 512, 256], P(None, ('row', 'col')), may hold values from -0.25 to 0.25
- gn2_gain: float32 [256], replicated, may hold values from 0.1 to 1.9
- gn2_bias: float32 [256], replicated, may hold values from -3 to 3
- conv2_weight: bfloat16 [27, 256, 256], P(None, ('row', 'col')), may hold values from -0.078125 to 0.078125
- conv2_bias: float32 [256], replicated, may hold values from -3 to 3
Outputs:
- block_out: bfloat16 [16, 12, 32, 256], P('tm', 'row', 'col')
The draws below stay inside these ranges and needn't reach their ends.
Inputs may be any that keep to these rules, and one draw needn't show every extreme that they name: Latent features of the decoder, of mixed scales over frames, positions and channels.
All inputs are finite; a program needn't handle non-finite values.
Results may differ from the reference program's by a relative error of at most 0.0065.
Values may be sent and summed in bfloat16 or wider, within the bound.
A program may use at most 64 MiB of HBM per device.

```python
import jax
import jax.numpy as jnp
from jax import lax

C_IN = 512
C_OUT = 256
GROUPS = 32
NT = 16
NH = 12
NW = 32


def draw_features(key, part):
    key = jax.random.fold_in(key, 11)
    keys = jax.random.split(key, 8)
    frame = jnp.arange(NT, dtype=jnp.float32) / float(max(NT - 1, 1))
    rise = jnp.exp(jnp.log(3.0) * frame) * jnp.exp(jax.random.uniform(keys[0], (NT,), jnp.float32, -0.2, 0.2))
    rows = jnp.exp(jax.random.uniform(keys[1], (NH,), jnp.float32, 0.0, jnp.log(3.0)))
    halves = jnp.arange(NW, dtype=jnp.int32) * 2 // NW
    pick = jax.random.randint(keys[6], (), 0, 2, dtype=jnp.int32)
    step = jnp.where(halves == pick, 2.5, 1.0).astype(jnp.float32)
    cols = jnp.exp(jax.random.uniform(keys[2], (NW,), jnp.float32, 0.0, jnp.log(3.0))) * step
    offsets = 0.8 * jax.random.normal(keys[7], (2, C_IN), jnp.float32)
    placed = jnp.where(halves[:, None] == 0, offsets[0][None, :], offsets[1][None, :])
    chan = jnp.exp(jax.random.uniform(keys[3], (C_IN,), jnp.float32, 0.0, jnp.log(10.0)))
    noise = jnp.clip(jax.random.normal(keys[4], (NT, NH, NW, C_IN), jnp.float32), -4.0, 4.0)
    noise = noise + placed[None, None, :, :]
    scale = 0.035 * rise[:, None, None, None] * rows[None, :, None, None] * cols[None, None, :, None] * chan
    return jnp.clip(scale * noise, -16.0, 16.0).astype(jnp.bfloat16)


def shard_levels(stream_key, extent, cuts, least, high):
    level = 1.0
    for axis_at, shards_of in cuts:
        draws = jax.random.uniform(jax.random.fold_in(jax.random.fold_in(stream_key, 6), axis_at), (shards_of,), jnp.float32, least / len(cuts), high / len(cuts))
        level = level * jnp.repeat(jnp.exp(draws), extent[axis_at] // shards_of).reshape((-1,) + (1,) * (len(extent) - 1 - axis_at))
    return level


def bell_draw(rng, extent, width, limit, pieces=(), held_as=jnp.bfloat16):
    array = width * jax.random.normal(rng, extent, jnp.float32)
    if pieces:
        array = array * shard_levels(rng, extent, pieces, -0.22, 0.18)
    return jnp.clip(array, -limit, limit).astype(held_as)


def setup_inputs(seed: int = 0) -> dict:
    arg_keys = jax.random.split(jax.random.key(seed), 11)
    features = draw_features(jax.random.fold_in(arg_keys[10], 71), 0)
    gn1_gain = jnp.clip(1.0 + 0.18 * jax.random.normal(arg_keys[1], (C_IN,), jnp.float32), 0.1, 1.9)
    gn1_bias = bell_draw(arg_keys[2], (C_IN,), 0.5, 3.0, (), jnp.float32)
    conv1_weight = bell_draw(arg_keys[3], (27, C_IN, C_OUT), (27 * C_IN) ** -0.5, 0.0546875, ((1, 4),))
    conv1_bias = bell_draw(arg_keys[4], (C_OUT,), 0.5, 3.0, (), jnp.float32)
    skip_weight = bell_draw(arg_keys[5], (1, C_IN, C_OUT), C_IN ** -0.5, 0.25, ((1, 4),))
    gn2_gain = jnp.clip(1.0 + 0.18 * jax.random.normal(arg_keys[6], (C_OUT,), jnp.float32), 0.1, 1.9)
    gn2_bias = bell_draw(arg_keys[7], (C_OUT,), 0.5, 3.0, (), jnp.float32)
    conv2_weight = bell_draw(arg_keys[8], (27, C_OUT, C_OUT), (27 * C_OUT) ** -0.5, 0.078125, ((1, 4),))
    conv2_bias = bell_draw(arg_keys[9], (C_OUT,), 0.5, 3.0, (), jnp.float32)
    return dict(features=features, gn1_gain=gn1_gain, gn1_bias=gn1_bias, conv1_weight=conv1_weight, conv1_bias=conv1_bias, skip_weight=skip_weight, gn2_gain=gn2_gain, gn2_bias=gn2_bias, conv2_weight=conv2_weight, conv2_bias=conv2_bias)


def group_silu(values, gain, shift):
    chans = values.shape[-1]
    grouped = values.reshape(-1, GROUPS, chans // GROUPS)
    mean = lax.optimization_barrier(jnp.mean(grouped, axis=(0, 2)))
    centred = grouped - mean[None, :, None]
    spread = lax.optimization_barrier(jnp.mean(centred * centred, axis=(0, 2)))
    normed = centred * jax.lax.rsqrt(spread + 1e-06)[None, :, None]
    normed = normed.reshape(values.shape) * gain + shift
    return jax.nn.silu(normed).astype(jnp.bfloat16)

def causal_conv(field, weight):
    frames, rows, cols, chans = field.shape
    padded = jnp.pad(field, ((2, 0), (1, 1), (1, 1), (0, 0)), mode='edge')
    total = jnp.zeros((frames * rows * cols, weight.shape[2]), jnp.float32)
    for tap in range(27):
        dt, dy, dx = (tap // 9, tap // 3 % 3, tap % 3)
        window = padded[dt:dt + frames, dy:dy + rows, dx:dx + cols].reshape(-1, chans)
        total = total + jnp.dot(window, weight[tap], preferred_element_type=jnp.float32)
    return total

def reference(features, gn1_gain, gn1_bias, conv1_weight, conv1_bias, skip_weight, gn2_gain, gn2_bias, conv2_weight, conv2_bias):
    hidden1 = group_silu(features.astype(jnp.float32), gn1_gain, gn1_bias)
    middle = causal_conv(hidden1, conv1_weight) + conv1_bias
    middle = middle.reshape(NT, NH, NW, C_OUT)
    hidden2 = group_silu(middle, gn2_gain, gn2_bias)
    second = causal_conv(hidden2, conv2_weight) + conv2_bias
    shortcut = jnp.dot(features.reshape(-1, C_IN), skip_weight[0], preferred_element_type=jnp.float32)
    return (shortcut + second).astype(jnp.bfloat16).reshape(NT, NH, NW, C_OUT)
```

```python
import functools

import jax
import jax.numpy as jnp
from jax import lax
from jax.experimental import pallas as pl
from jax.experimental.pallas import tpu as pltpu
from jax.sharding import PartitionSpec as P

GROUPS = 32


def passed_along(block, axis, distance):
    devices = range(lax.axis_size(axis))
    route = [(i - distance, i) for i in devices if i - distance in devices]
    return lax.ppermute(block, axis, route)


def with_halo(array, sides, width):
    for axis, dim in sides:
        size, length = (lax.axis_size(axis), array.shape[dim])
        up = [(i, (i + 1) % size) for i in range(size - 1)]
        down = [(j, i) for i, j in up]
        last = lax.slice_in_dim(array, length - width, length, axis=dim)
        leading = lax.slice_in_dim(array, 0, width, axis=dim)
        before = lax.ppermute(last, axis, up)
        after = lax.ppermute(leading, axis, down)
        array = jnp.concatenate([before, array, after], axis=dim)
    return array


def group_silu(values, gain, shift, groups, total_rows):
    chans = values.shape[-1]
    per_group = chans // groups
    grouped = values.reshape(-1, groups, per_group)
    count = float(total_rows * per_group)
    mean = lax.psum(jnp.sum(grouped, axis=(0, 2)), ("tm", "row", "col")) / count
    centred = grouped - mean[None, :, None]
    spread = lax.psum(jnp.sum(centred * centred, axis=(0, 2)), ("tm", "row", "col")) / count
    normed = (grouped - mean[None, :, None]) * lax.rsqrt(spread + 1e-06)[None, :, None]
    normed = normed.reshape(values.shape) * gain + shift
    return jax.nn.silu(normed).astype(jnp.bfloat16)


def conv_taps(padded, weight, frames, rows, cols):
    chans = padded.shape[3]
    total = jnp.zeros((frames * rows * cols, weight.shape[2]), jnp.float32)
    for dt in range(3):
        pieces = []
        for tap in range(9):
            dy, dx = (tap // 3, tap % 3)
            pieces.append(
                padded[dt : dt + frames, dy : dy + rows, dx : dx + cols].reshape(-1, chans)
            )
        stacked = jnp.concatenate(pieces, axis=1)
        flat_weight = weight[9 * dt : 9 * dt + 9].reshape(9 * chans, weight.shape[2])
        total = total + jnp.dot(stacked, flat_weight, preferred_element_type=jnp.float32)
    return total


def time_edge(earlier, volume):
    first_twice = jnp.concatenate([volume[:1], volume[:1]], axis=0)
    earlier = jnp.where(lax.axis_index("tm") == 0, first_twice, earlier)
    return jnp.concatenate([earlier, volume], axis=0)


def edge_rows(padded):
    place = lax.axis_index("row")
    last = lax.axis_size("row") - 1
    top = jnp.where(place == 0, padded[:, 1:2], padded[:, 0:1])
    bottom = jnp.where(place == last, padded[:, -2:-1], padded[:, -1:])
    return jnp.concatenate([top, padded[:, 1:-1], bottom], axis=1)


def edge_cols(padded):
    place = lax.axis_index("col")
    last = lax.axis_size("col") - 1
    left = jnp.where(place == 0, padded[:, :, 1:2], padded[:, :, 0:1])
    right = jnp.where(place == last, padded[:, :, -2:-1], padded[:, :, -1:])
    return jnp.concatenate([left, padded[:, :, 1:-1], right], axis=2)


def per_device_gathered(
    features,
    gn1_gain,
    gn1_bias,
    conv1_weight,
    conv1_bias,
    skip_weight,
    gn2_gain,
    gn2_bias,
    conv2_weight,
    conv2_bias,
):
    frames, rows, cols, chans_in = features.shape
    chans_out = conv1_weight.shape[2]
    groups = GROUPS
    nrow = lax.axis_size("row")
    ncol = lax.axis_size("col")
    total_rows = lax.axis_size("tm") * nrow * ncol * frames * rows * cols
    flat_features = features.reshape(-1, chans_in)
    hidden1 = group_silu(features.astype(jnp.float32), gn1_gain, gn1_bias, groups, total_rows)
    earlier = passed_along(hidden1, "tm", 1)
    extended = time_edge(earlier, hidden1)
    padded = with_halo(extended, (("row", 1), ("col", 2)), 1)
    padded = edge_cols(edge_rows(padded))
    window = padded
    first = conv_taps(
        window, lax.all_gather(conv1_weight, ("row", "col"), axis=1, tiled=True), frames, rows, cols
    )
    second = jnp.dot(
        flat_features,
        lax.all_gather(skip_weight, ("row", "col"), axis=1, tiled=True)[0],
        preferred_element_type=jnp.float32,
    )
    middle = (first + conv1_bias).reshape(frames, rows, cols, chans_out)
    hidden2 = group_silu(middle, gn2_gain, gn2_bias, groups, total_rows)
    earlier_mid = passed_along(hidden2, "tm", 1)
    extended_mid = time_edge(earlier_mid, hidden2)
    padded_mid = with_halo(extended_mid, (("row", 1), ("col", 2)), 1)
    padded_mid = edge_cols(edge_rows(padded_mid))
    window = padded_mid
    conv_second = conv_taps(
        window, lax.all_gather(conv2_weight, ("row", "col"), axis=1, tiled=True), frames, rows, cols
    )
    block_out = (second + conv_second + conv2_bias).astype(jnp.bfloat16)
    return block_out.reshape(frames, rows, cols, chans_out)


MESH = pl.DeviceIdType.MESH
LANES = 128


def lane_of(shape):
    return lax.broadcasted_iota(jnp.int32, shape, len(shape) - 1)


def silu(a):
    half = 0.5 * a
    return half + half * jnp.tanh(half)


def lane_stats(x):
    mean = jnp.sum(x, axis=0, keepdims=True) * (1.0 / x.shape[0])
    spread = jnp.sum((x - mean) ** 2, axis=0, keepdims=True)
    row = lax.broadcasted_iota(jnp.int32, (8, LANES), 0)
    return jnp.where(row == 0, mean, jnp.where(row == 1, spread, 0.0))


def group_stats(stats, same, lanes, count):
    devices = stats.shape[0]
    means, spreads = stats[:, 0:1, :], stats[:, 1:2, :]
    mean = jnp.sum(means, axis=0) * (1.0 / devices)
    spread = jnp.sum(spreads, axis=0) + count * jnp.sum((means - mean[None]) ** 2, axis=0)
    mean = jnp.broadcast_to(mean, (8, LANES))
    group_mean = (
        jnp.dot(mean, same, precision=lax.Precision.HIGHEST, preferred_element_type=jnp.float32)
        * (1.0 / lanes)
    )
    spread = spread + (count * devices) * (mean - group_mean) ** 2
    total = jnp.dot(
        spread, same, precision=lax.Precision.HIGHEST, preferred_element_type=jnp.float32
    )
    inv = lax.rsqrt(total * (1.0 / (count * devices * lanes)) + 1e-6)
    return group_mean[0:1], inv[0:1]


def side_shifts(h, cols):
    col = lax.broadcasted_iota(jnp.int32, h.shape, 0) & (cols - 1)
    length = h.shape[0]
    left = jnp.where(col == 0, h, pltpu.roll(h, 1, 0))
    right = jnp.where(col == cols - 1, h, pltpu.roll(h, length - 1, 0))
    return left, right


def block_kernel(
    sizes,
    feat, gain1, shift1, w1, bias1, wskip, gain2, shift2, w2, bias2,
    out,
    xall, w1v, wsv, wa, wb, xp1, xp2, part1, send1, recv1, stat1, stat2,
    midbf, prevbf, scut, part2, send2, recv2,
    w_sem, own_sem, fs_sem, fr_sem, fps_sem, fpr_sem,
    s1s_sem, s1r_sem, s2s_sem, s2r_sem, r1s_sem, r1r_sem, r2s_sem, r2r_sem,
    ps_sem, pr_sem,
):
    slabs, nrow, ncol, rows, cols, per1, per2 = sizes
    n = nrow * ncol
    height, width = nrow * rows, ncol * cols
    area = height * width
    t = lax.axis_index("tm")
    r = lax.axis_index("row")
    c = lax.axis_index("col")
    me = r * ncol + c

    def place(i):
        return lax.div(i, ncol), lax.rem(i, ncol)

    def ident(ti, i):
        ri, ci = place(i)
        return {"tm": ti, "row": ri, "col": ci}

    def member(delta):
        return lax.rem(me + delta, n)

    def slab(delta):
        return lax.rem(t + delta, slabs)

    loads = [
        pltpu.make_async_copy(w1, w1v, w_sem.at[0]),
        pltpu.make_async_copy(wskip, wsv, w_sem.at[1]),
    ]
    for dt in range(3):
        lo = dt * per2
        loads.append(
            pltpu.make_async_copy(w2.at[dt], wa.at[:, lo : lo + per2, :], w_sem.at[2 + dt])
        )
        loads.append(
            pltpu.make_async_copy(
                w2.at[dt], wb.at[:, lo + per2 : lo + 2 * per2, :], w_sem.at[5 + dt]
            )
        )

    def window(frame0, i):
        ri, ci = place(i)
        top = ri * rows
        left = pl.multiple_of(ci * cols, cols)
        return xall.at[frame0 : frame0 + 2, pl.ds(top, rows), pl.ds(left, cols), :]

    def chunk(i):
        return feat.at[:, :, :, pl.ds(pl.multiple_of(i * LANES, LANES), LANES)]

    own = pltpu.make_async_copy(chunk(me), window(2, me), own_sem)
    own.start()

    barrier = pltpu.get_barrier_semaphore()
    for delta in range(1, n):
        pl.semaphore_signal(barrier, inc=1, device_id=ident(t, member(delta)), device_id_type=MESH)
    for delta in range(1, slabs):
        pl.semaphore_signal(barrier, inc=1, device_id=ident(slab(delta), me), device_id_type=MESH)

    @pl.when(t > 0)
    def _():
        for delta in range(1, n):
            pl.semaphore_signal(
                barrier, inc=1, device_id=ident(t - 1, member(delta)), device_id_type=MESH
            )

    pl.semaphore_wait(barrier, jnp.where(t < slabs - 1, 2 * (n - 1), n - 1) + slabs - 1)

    def feat_copy(source, target):
        return pltpu.make_async_remote_copy(
            src_ref=chunk(target), dst_ref=window(2, source),
            send_sem=fs_sem.at[target], recv_sem=fr_sem.at[source],
            device_id=ident(t, target), device_id_type=MESH,
        )

    def feat_next(source, target, to):
        return pltpu.make_async_remote_copy(
            src_ref=chunk(target), dst_ref=window(0, source),
            send_sem=fps_sem.at[target], recv_sem=fpr_sem.at[source],
            device_id=ident(to, target), device_id_type=MESH,
        )

    for delta in range(1, n):
        feat_copy(me, member(delta)).start()

    @pl.when(t < slabs - 1)
    def _():
        for delta in range(n):
            feat_next(me, member(delta), t + 1).start()

    for load in loads:
        load.start()
    wa[:, 3 * per2 :, :] = jnp.zeros((9, 4 * per2 - 3 * per2, wa.shape[2]), wa.dtype)
    wb[:, :per2, :] = jnp.zeros((9, per2, wb.shape[2]), wb.dtype)

    lane = lane_of((8, LANES))
    lane_in = lax.broadcasted_iota(jnp.int32, (LANES, LANES), 0)
    lane_to = lane_of((LANES, LANES))
    size1 = per1 // (GROUPS // n)
    size2 = per2 // (GROUPS // n)
    same1 = (lane_in // size1 == lane_to // size1).astype(jnp.float32)
    same2 = ((lane_in % per2) // size2 == (lane_to % per2) // size2).astype(jnp.float32)

    def own_full(ref):
        result = ref[0:1, 0:LANES]
        for d in range(1, n):
            result = jnp.where(me == d, ref[0:1, d * LANES : (d + 1) * LANES], result)
        return result

    def own_twice(ref):
        result = jnp.zeros((8, LANES), jnp.float32)
        for d in range(n):
            k = d // 2 * LANES
            seg = jnp.broadcast_to(ref[0:1, k : k + LANES], (8, LANES))
            turned = pltpu.roll(seg, per2, 1)
            twice = jnp.where((lane < per2) == (d % 2 == 0), seg, turned)
            result = jnp.where(me == d, twice, result)
        return result[0:1]

    g1, b1 = own_full(gain1), own_full(shift1)
    g2, b2, c1 = own_twice(gain2), own_twice(shift2), own_twice(bias1)

    def stat_copy(buf, source, target, ssem, rsem):
        return pltpu.make_async_remote_copy(
            src_ref=buf.at[source], dst_ref=buf.at[source],
            send_sem=ssem.at[target], recv_sem=rsem.at[source],
            device_id=ident(target, me), device_id_type=MESH,
        )

    own.wait()
    for delta in range(1, n):
        feat_copy(member(delta), me).wait_recv()
    raw = xall[2:4].reshape(2 * area, LANES).astype(jnp.float32)
    stat1[t] = lane_stats(raw)
    for delta in range(1, slabs):
        stat_copy(stat1, t, slab(delta), s1s_sem, s1r_sem).start()

    loads[1].wait()
    for f in range(2):
        x = xall[2 + f].reshape(area, LANES)
        scut[f] = jnp.dot(x, wsv[...], preferred_element_type=jnp.float32)

    @pl.when(t > 0)
    def _():
        for delta in range(n):
            feat_next(member(delta), me, t).wait_recv()

    @pl.when(t == 0)
    def _():
        xall[0] = xall[2]
        xall[1] = xall[2]

    for delta in range(1, slabs):
        stat_copy(stat1, slab(delta), t, s1s_sem, s1r_sem).wait_recv()
    mean, inv = group_stats(stat1[...], same1, size1, float(2 * area))
    scale = inv * g1
    for f in range(4):
        x = xall[f].reshape(area, LANES).astype(jnp.float32)
        h = silu((x - mean) * scale + b1)
        left, right = side_shifts(h, width)
        for dx, part in enumerate((left, h, right)):
            part = part.astype(jnp.bfloat16).reshape(height, width, LANES)
            lanes = slice(dx * LANES, (dx + 1) * LANES)
            xp1[f, 1 : height + 1, :, lanes] = part
            xp1[f, 0, :, lanes] = part[0]
            xp1[f, height + 1, :, lanes] = part[height - 1]

    loads[0].wait()
    depth = 9 * LANES
    firsts = []
    for f in range(2):
        total = None
        for dt in range(3):
            lhs = jnp.concatenate(
                [xp1[f + dt, dy : dy + height].reshape(area, 3 * LANES) for dy in range(3)], axis=1
            )
            term = jnp.dot(
                lhs, w1v[dt * depth : (dt + 1) * depth, :], preferred_element_type=jnp.float32
            )
            total = term if total is None else total + term
        firsts.append(total)
    wide = lane_of((area, LANES))
    for d in range(n):
        k = d // 2 * LANES
        one, two = firsts[0][:, k : k + LANES], firsts[1][:, k : k + LANES]
        if d % 2 == 0:
            packed = jnp.where(wide < per2, one, pltpu.roll(two, per2, 1))
        else:
            packed = jnp.where(wide < per2, pltpu.roll(one, per2, 1), two)
        part1[d] = packed
        send1[d] = packed.astype(jnp.bfloat16)

    def sum_copy(src, dst, source, target, ssem, rsem):
        return pltpu.make_async_remote_copy(
            src_ref=src.at[target], dst_ref=dst.at[source],
            send_sem=ssem.at[target], recv_sem=rsem.at[source],
            device_id=ident(t, target), device_id_type=MESH,
        )

    for delta in range(1, n):
        sum_copy(send1, recv1, me, member(delta), r1s_sem, r1r_sem).start()
    middle = part1[me] + c1
    for delta in range(1, n):
        source = member(delta)
        sum_copy(send1, recv1, source, me, r1s_sem, r1r_sem).wait_recv()
        middle = middle + recv1[source].astype(jnp.float32)

    midbf[...] = middle.astype(jnp.bfloat16)

    def mid_copy(to):
        return pltpu.make_async_remote_copy(
            src_ref=midbf, dst_ref=prevbf, send_sem=ps_sem, recv_sem=pr_sem,
            device_id=ident(to, me), device_id_type=MESH,
        )

    stat2[t] = lane_stats(middle)
    for delta in range(1, slabs):
        stat_copy(stat2, t, slab(delta), s2s_sem, s2r_sem).start()

    @pl.when(t < slabs - 1)
    def _():
        mid_copy(t + 1).start()

    part1[0] = middle

    @pl.when(t > 0)
    def _():
        mid_copy(t).wait_recv()
        part1[1] = prevbf[...].astype(jnp.float32)

    @pl.when(t == 0)
    def _():
        part1[1] = jnp.where(wide < per2, middle, pltpu.roll(middle, per2, 1))

    for delta in range(1, slabs):
        stat_copy(stat2, slab(delta), t, s2s_sem, s2r_sem).wait_recv()
    mean, inv = group_stats(stat2[...], same2, 2 * size2, float(area))
    scale = inv * g2
    for i in range(2):
        h = silu((part1[1 - i] - mean) * scale + b2)
        left, right = side_shifts(h, width)
        for dx, part in enumerate((left, h, right)):
            part = part.astype(jnp.bfloat16).reshape(height, width, LANES)
            lanes = slice((2 * dx + i) * LANES, (2 * dx + i + 1) * LANES)
            xp2[1 : height + 1, :, lanes] = part
            xp2[0, :, lanes] = part[0]
            xp2[height + 1, :, lanes] = part[height - 1]

    for load in loads[2:]:
        load.wait()
    for f, weight in enumerate((wa, wb)):
        total = scut[f]
        for dy in range(3):
            lhs = xp2[dy : dy + height].reshape(area, 6 * LANES)
            rhs = weight[3 * dy : 3 * dy + 3].reshape(6 * LANES, weight.shape[2])
            total = total + jnp.dot(lhs, rhs, preferred_element_type=jnp.float32)
        total = total.reshape(height, width, weight.shape[2])
        for d in range(n):
            ri, ci = d // ncol, d % ncol
            piece = total[ri * rows : (ri + 1) * rows, ci * cols : (ci + 1) * cols]
            part2[d, f] = piece
            send2[d, f] = piece.astype(jnp.bfloat16)

    for delta in range(1, n):
        sum_copy(send2, recv2, me, member(delta), r2s_sem, r2r_sem).start()
    result = part2[me] + bias2[...].reshape(1, 1, 1, -1)
    for delta in range(1, n):
        source = member(delta)
        sum_copy(send2, recv2, source, me, r2s_sem, r2r_sem).wait_recv()
        result = result + recv2[source].astype(jnp.float32)
    out[...] = result.astype(out.dtype)

    for delta in range(1, n):
        target = member(delta)
        feat_copy(me, target).wait_send()
        sum_copy(send1, recv1, me, target, r1s_sem, r1r_sem).wait_send()
        sum_copy(send2, recv2, me, target, r2s_sem, r2r_sem).wait_send()
    for delta in range(1, slabs):
        stat_copy(stat1, t, slab(delta), s1s_sem, s1r_sem).wait_send()
        stat_copy(stat2, t, slab(delta), s2s_sem, s2r_sem).wait_send()

    @pl.when(t < slabs - 1)
    def _():
        for delta in range(n):
            feat_next(me, member(delta), t + 1).wait_send()
        mid_copy(t + 1).wait_send()


def per_device(
    features,
    gn1_gain,
    gn1_bias,
    conv1_weight,
    conv1_bias,
    skip_weight,
    gn2_gain,
    gn2_bias,
    conv2_weight,
    conv2_bias,
):
    frames, rows, cols, chans_in = features.shape
    per1, per2 = conv1_weight.shape[1], conv2_weight.shape[1]
    chans_out = conv1_weight.shape[2]
    slabs, nrow, ncol = (lax.axis_size(a) for a in ("tm", "row", "col"))
    n = nrow * ncol
    height, width = nrow * rows, ncol * cols
    area = height * width
    fits = frames == 2 and per1 == LANES and 2 * per2 == LANES and cols % 16 == 0
    fits = fits and width & (width - 1) == 0 and GROUPS % n == 0
    if not fits:
        return per_device_gathered(
            features, gn1_gain, gn1_bias, conv1_weight, conv1_bias, skip_weight,
            gn2_gain, gn2_bias, conv2_weight, conv2_bias,
        )
    bf16, f32 = jnp.bfloat16, jnp.float32
    vmem, dma = pltpu.VMEM, pltpu.SemaphoreType.DMA
    scratch = [
        vmem((4, height, width, LANES), bf16),
        vmem((27 * per1, chans_out), bf16),
        vmem((per1, chans_out), bf16),
        vmem((9, 4 * per2, chans_out), bf16),
        vmem((9, 4 * per2, chans_out), bf16),
        vmem((4, height + 2, width, 3 * LANES), bf16),
        vmem((height + 2, width, 6 * LANES), bf16),
        vmem((n, area, LANES), f32),
        vmem((n, area, LANES), bf16),
        vmem((n, area, LANES), bf16),
        vmem((slabs, 8, LANES), f32),
        vmem((slabs, 8, LANES), f32),
        vmem((area, LANES), bf16),
        vmem((area, LANES), bf16),
        vmem((2, area, chans_out), f32),
        vmem((n, 2, rows, cols, chans_out), f32),
        vmem((n, 2, rows, cols, chans_out), bf16),
        vmem((n, 2, rows, cols, chans_out), bf16),
        dma((8,)), dma, dma((n,)), dma((n,)), dma((n,)), dma((n,)),
        dma((slabs,)), dma((slabs,)), dma((slabs,)), dma((slabs,)),
        dma((n,)), dma((n,)), dma((n,)), dma((n,)),
        dma, dma,
    ]
    anywhere = pl.BlockSpec(memory_space=pl.ANY)
    inside = pl.BlockSpec(memory_space=pltpu.VMEM)
    sizes = (slabs, nrow, ncol, rows, cols, per1, per2)
    flops = 2 * 2 * area * chans_out * (28 * per1 + 27 * per2)
    return pl.pallas_call(
        functools.partial(block_kernel, sizes),
        out_shape=jax.ShapeDtypeStruct((frames, rows, cols, chans_out), bf16),
        in_specs=[
            anywhere, inside, inside, anywhere, inside, anywhere, inside, inside, anywhere, inside,
        ],
        out_specs=inside,
        scratch_shapes=scratch,
        compiler_params=pltpu.CompilerParams(
            collective_id=0, has_side_effects=True, vmem_limit_bytes=48 * 1024 * 1024
        ),
        cost_estimate=pl.CostEstimate(
            flops=flops, bytes_accessed=4 * 1024 * 1024, transcendentals=6 * area * LANES
        ),
        name="residual_block",
    )(
        features,
        gn1_gain.reshape(1, -1),
        gn1_bias.reshape(1, -1),
        conv1_weight.reshape(27 * per1, chans_out),
        conv1_bias.reshape(1, -1),
        skip_weight.reshape(per1, chans_out),
        gn2_gain.reshape(1, -1),
        gn2_bias.reshape(1, -1),
        conv2_weight.reshape(3, 9, per2, chans_out),
        conv2_bias.reshape(1, -1),
    )


def solution(mesh):
    in_specs = (
        P("tm", "row", "col", None),
        P(),
        P(),
        P(None, ("row", "col"), None),
        P(),
        P(None, ("row", "col"), None),
        P(),
        P(),
        P(None, ("row", "col"), None),
        P(),
    )
    out_specs = P("tm", "row", "col", None)
    return jax.shard_map(
        per_device, mesh=mesh, in_specs=in_specs, out_specs=out_specs, check_vma=False
    )
```

```python
import functools

import jax
import jax.numpy as jnp
from jax import lax
from jax.experimental import pallas as pl
from jax.experimental.pallas import tpu as pltpu
from jax.sharding import PartitionSpec as P

GROUPS = 32


def passed_along(block, axis, distance):
    devices = range(lax.axis_size(axis))
    route = [(i - distance, i) for i in devices if i - distance in devices]
    return lax.ppermute(block, axis, route)


def with_halo(array, sides, width):
    for axis, dim in sides:
        size, length = (lax.axis_size(axis), array.shape[dim])
        up = [(i, (i + 1) % size) for i in range(size - 1)]
        down = [(j, i) for i, j in up]
        last = lax.slice_in_dim(array, length - width, length, axis=dim)
        leading = lax.slice_in_dim(array, 0, width, axis=dim)
        before = lax.ppermute(last, axis, up)
        after = lax.ppermute(leading, axis, down)
        array = jnp.concatenate([before, array, after], axis=dim)
    return array


def group_silu(values, gain, shift, groups, total_rows):
    chans = values.shape[-1]
    per_group = chans // groups
    grouped = values.reshape(-1, groups, per_group)
    count = float(total_rows * per_group)
    mean = lax.psum(jnp.sum(grouped, axis=(0, 2)), ("tm", "row", "col")) / count
    centred = grouped - mean[None, :, None]
    spread = lax.psum(jnp.sum(centred * centred, axis=(0, 2)), ("tm", "row", "col")) / count
    normed = (grouped - mean[None, :, None]) * lax.rsqrt(spread + 1e-06)[None, :, None]
    normed = normed.reshape(values.shape) * gain + shift
    return jax.nn.silu(normed).astype(jnp.bfloat16)


def conv_taps(padded, weight, frames, rows, cols):
    chans = padded.shape[3]
    total = jnp.zeros((frames * rows * cols, weight.shape[2]), jnp.float32)
    for dt in range(3):
        pieces = []
        for tap in range(9):
            dy, dx = (tap // 3, tap % 3)
            pieces.append(
                padded[dt : dt + frames, dy : dy + rows, dx : dx + cols].reshape(-1, chans)
            )
        stacked = jnp.concatenate(pieces, axis=1)
        flat_weight = weight[9 * dt : 9 * dt + 9].reshape(9 * chans, weight.shape[2])
        total = total + jnp.dot(stacked, flat_weight, preferred_element_type=jnp.float32)
    return total


def time_edge(earlier, volume):
    first_twice = jnp.concatenate([volume[:1], volume[:1]], axis=0)
    earlier = jnp.where(lax.axis_index("tm") == 0, first_twice, earlier)
    return jnp.concatenate([earlier, volume], axis=0)


def edge_rows(padded):
    place = lax.axis_index("row")
    last = lax.axis_size("row") - 1
    top = jnp.where(place == 0, padded[:, 1:2], padded[:, 0:1])
    bottom = jnp.where(place == last, padded[:, -2:-1], padded[:, -1:])
    return jnp.concatenate([top, padded[:, 1:-1], bottom], axis=1)


def edge_cols(padded):
    place = lax.axis_index("col")
    last = lax.axis_size("col") - 1
    left = jnp.where(place == 0, padded[:, :, 1:2], padded[:, :, 0:1])
    right = jnp.where(place == last, padded[:, :, -2:-1], padded[:, :, -1:])
    return jnp.concatenate([left, padded[:, :, 1:-1], right], axis=2)


def per_device_gathered(
    features,
    gn1_gain,
    gn1_bias,
    conv1_weight,
    conv1_bias,
    skip_weight,
    gn2_gain,
    gn2_bias,
    conv2_weight,
    conv2_bias,
):
    frames, rows, cols, chans_in = features.shape
    chans_out = conv1_weight.shape[2]
    groups = GROUPS
    nrow = lax.axis_size("row")
    ncol = lax.axis_size("col")
    total_rows = lax.axis_size("tm") * nrow * ncol * frames * rows * cols
    flat_features = features.reshape(-1, chans_in)
    hidden1 = group_silu(features.astype(jnp.float32), gn1_gain, gn1_bias, groups, total_rows)
    earlier = passed_along(hidden1, "tm", 1)
    extended = time_edge(earlier, hidden1)
    padded = with_halo(extended, (("row", 1), ("col", 2)), 1)
    padded = edge_cols(edge_rows(padded))
    window = padded
    first = conv_taps(
        window, lax.all_gather(conv1_weight, ("row", "col"), axis=1, tiled=True), frames, rows, cols
    )
    second = jnp.dot(
        flat_features,
        lax.all_gather(skip_weight, ("row", "col"), axis=1, tiled=True)[0],
        preferred_element_type=jnp.float32,
    )
    middle = (first + conv1_bias).reshape(frames, rows, cols, chans_out)
    hidden2 = group_silu(middle, gn2_gain, gn2_bias, groups, total_rows)
    earlier_mid = passed_along(hidden2, "tm", 1)
    extended_mid = time_edge(earlier_mid, hidden2)
    padded_mid = with_halo(extended_mid, (("row", 1), ("col", 2)), 1)
    padded_mid = edge_cols(edge_rows(padded_mid))
    window = padded_mid
    conv_second = conv_taps(
        window, lax.all_gather(conv2_weight, ("row", "col"), axis=1, tiled=True), frames, rows, cols
    )
    block_out = (second + conv_second + conv2_bias).astype(jnp.bfloat16)
    return block_out.reshape(frames, rows, cols, chans_out)


MESH = pl.DeviceIdType.MESH
LANES = 128


def lane_of(shape):
    return lax.broadcasted_iota(jnp.int32, shape, len(shape) - 1)


def silu(a):
    half = 0.5 * a
    return half + half * jnp.tanh(half)


def lane_stats(x):
    mean = jnp.sum(x, axis=0, keepdims=True) * (1.0 / x.shape[0])
    spread = jnp.sum((x - mean) ** 2, axis=0, keepdims=True)
    row = lax.broadcasted_iota(jnp.int32, (8, LANES), 0)
    return jnp.where(row == 0, mean, jnp.where(row == 1, spread, 0.0))


def group_stats(stats, same, lanes, count):
    devices = stats.shape[0]
    means, spreads = stats[:, 0:1, :], stats[:, 1:2, :]
    mean = jnp.sum(means, axis=0) * (1.0 / devices)
    spread = jnp.sum(spreads, axis=0) + count * jnp.sum((means - mean[None]) ** 2, axis=0)
    mean = jnp.broadcast_to(mean, (8, LANES))
    group_mean = (
        jnp.dot(mean, same, precision=lax.Precision.HIGHEST, preferred_element_type=jnp.float32)
        * (1.0 / lanes)
    )
    spread = spread + (count * devices) * (mean - group_mean) ** 2
    total = jnp.dot(
        spread, same, precision=lax.Precision.HIGHEST, preferred_element_type=jnp.float32
    )
    inv = lax.rsqrt(total * (1.0 / (count * devices * lanes)) + 1e-6)
    return group_mean[0:1], inv[0:1]


def side_shifts(h, cols):
    col = lax.broadcasted_iota(jnp.int32, h.shape, 0) & (cols - 1)
    length = h.shape[0]
    left = jnp.where(col == 0, h, pltpu.roll(h, 1, 0))
    right = jnp.where(col == cols - 1, h, pltpu.roll(h, length - 1, 0))
    return left, right


def block_kernel(
    sizes,
    feat, gain1_hbm, shift1_hbm, w1, bias1_hbm, wskip, gain2_hbm, shift2_hbm, w2, bias2_hbm,
    out,
    gain1, shift1, bias1, gain2, shift2, bias2, xall, w1v, wsv, wa, wb, xp1, xp2, acc, part1, send1, recv1, stat1, stat2,
    mids, midbf, prevbf, scut, part2, send2, recv2,
    w_sem, p_sem, own_sem, fs_sem, fr_sem, fps_sem, fpr_sem,
    s1s_sem, s1r_sem, s2s_sem, s2r_sem, r1s_sem, r1r_sem, r2s_sem, r2r_sem,
    ps_sem, pr_sem,
):
    slabs, nrow, ncol, rows, cols, per1, per2 = sizes
    n = nrow * ncol
    height, width = nrow * rows, ncol * cols
    area = height * width
    t = lax.axis_index("tm")
    r = lax.axis_index("row")
    c = lax.axis_index("col")
    me = r * ncol + c

    def place(i):
        return lax.div(i, ncol), lax.rem(i, ncol)

    def ident(ti, i):
        ri, ci = place(i)
        return {"tm": ti, "row": ri, "col": ci}

    def member(delta):
        return lax.rem(r + delta // ncol, nrow) * ncol + lax.rem(c + delta % ncol, ncol)

    def slab(delta):
        return lax.rem(t + delta, slabs)

    loads = [
        pltpu.make_async_copy(w1, w1v, w_sem.at[0]),
        pltpu.make_async_copy(wskip, wsv, w_sem.at[1]),
    ]
    for dt in range(3):
        lo = dt * per2
        loads.append(
            pltpu.make_async_copy(w2.at[dt], wa.at[:, lo : lo + per2, :], w_sem.at[2 + dt])
        )
        loads.append(
            pltpu.make_async_copy(
                w2.at[dt], wb.at[:, lo + per2 : lo + 2 * per2, :], w_sem.at[5 + dt]
            )
        )

    params = [
        pltpu.make_async_copy(source, target, p_sem.at[i])
        for i, (source, target) in enumerate(
            (
                (gain1_hbm, gain1), (shift1_hbm, shift1), (bias1_hbm, bias1),
                (gain2_hbm, gain2), (shift2_hbm, shift2), (bias2_hbm, bias2),
            )
        )
    ]

    def window(frame0, i):
        ri, ci = place(i)
        top = ri * rows
        left = pl.multiple_of(ci * cols, cols)
        return xall.at[frame0 : frame0 + 2, pl.ds(top, rows), pl.ds(left, cols), :]

    def chunk(i):
        return feat.at[:, :, :, pl.ds(pl.multiple_of(i * LANES, LANES), LANES)]

    own = pltpu.make_async_copy(chunk(me), window(2, me), own_sem)
    own.start()

    barrier = pltpu.get_barrier_semaphore()
    for delta in range(1, n):
        pl.semaphore_signal(barrier, inc=1, device_id=ident(t, member(delta)), device_id_type=MESH)
    for delta in range(1, slabs):
        pl.semaphore_signal(barrier, inc=1, device_id=ident(slab(delta), me), device_id_type=MESH)

    @pl.when(t > 0)
    def _():
        for delta in range(1, n):
            pl.semaphore_signal(
                barrier, inc=1, device_id=ident(t - 1, member(delta)), device_id_type=MESH
            )

    for load in params + loads:
        load.start()
    wa[:, 3 * per2 :, :] = jnp.zeros((9, 4 * per2 - 3 * per2, wa.shape[2]), wa.dtype)
    wb[:, :per2, :] = jnp.zeros((9, per2, wb.shape[2]), wb.dtype)
    pl.semaphore_wait(barrier, jnp.where(t < slabs - 1, 2 * (n - 1), n - 1) + slabs - 1)

    def feat_copy(source, target):
        return pltpu.make_async_remote_copy(
            src_ref=chunk(target), dst_ref=window(2, source),
            send_sem=fs_sem.at[target], recv_sem=fr_sem.at[source],
            device_id=ident(t, target), device_id_type=MESH,
        )

    def feat_next(source, target, to):
        return pltpu.make_async_remote_copy(
            src_ref=chunk(target), dst_ref=window(0, source),
            send_sem=fps_sem.at[target], recv_sem=fpr_sem.at[source],
            device_id=ident(to, target), device_id_type=MESH,
        )

    for delta in reversed(range(1, n)):
        feat_copy(me, member(delta)).start()

    @pl.when(t < slabs - 1)
    def _():
        for delta in reversed(range(n)):
            feat_next(me, member(delta), t + 1).start()

    lane = lane_of((8, LANES))
    lane_in = lax.broadcasted_iota(jnp.int32, (LANES, LANES), 0)
    lane_to = lane_of((LANES, LANES))
    size1 = per1 // (GROUPS // n)
    size2 = per2 // (GROUPS // n)
    same1 = (lane_in // size1 == lane_to // size1).astype(jnp.float32)
    same2 = ((lane_in % per2) // size2 == (lane_to % per2) // size2).astype(jnp.float32)

    def own_full(ref):
        result = ref[0:1, 0:LANES]
        for d in range(1, n):
            result = jnp.where(me == d, ref[0:1, d * LANES : (d + 1) * LANES], result)
        return result

    def own_twice(ref):
        result = jnp.zeros((8, LANES), jnp.float32)
        for d in range(n):
            k = d // 2 * LANES
            seg = jnp.broadcast_to(ref[0:1, k : k + LANES], (8, LANES))
            turned = pltpu.roll(seg, per2, 1)
            twice = jnp.where((lane < per2) == (d % 2 == 0), seg, turned)
            result = jnp.where(me == d, twice, result)
        return result[0:1]

    for load in params:
        load.wait()
    g1, b1 = own_full(gain1), own_full(shift1)
    g2, b2, c1 = own_twice(gain2), own_twice(shift2), own_twice(bias1)

    def stat_copy(buf, source, target, ssem, rsem):
        return pltpu.make_async_remote_copy(
            src_ref=buf.at[source], dst_ref=buf.at[source],
            send_sem=ssem.at[target], recv_sem=rsem.at[source],
            device_id=ident(target, me), device_id_type=MESH,
        )

    own.wait()
    for delta in range(1, n):
        feat_copy(member(delta), me).wait_recv()
    raw = xall[2:4].reshape(2 * area, LANES).astype(jnp.float32)
    stat1[t] = lane_stats(raw)
    for delta in range(1, slabs):
        stat_copy(stat1, t, slab(delta), s1s_sem, s1r_sem).start()

    loads[1].wait()
    for f in range(2):
        x = xall[2 + f].reshape(area, LANES)
        scut[f] = jnp.dot(x, wsv[...], preferred_element_type=jnp.float32)

    for delta in range(1, slabs):
        stat_copy(stat1, slab(delta), t, s1s_sem, s1r_sem).wait_recv()
    mean, inv = group_stats(stat1[...], same1, size1, float(2 * area))
    scale = inv * g1

    def normalise(f):
        x = xall[f].reshape(area, LANES).astype(jnp.float32)
        h = silu((x - mean) * scale + b1)
        left, right = side_shifts(h, width)
        for dx, part in enumerate((left, h, right)):
            part = part.astype(jnp.bfloat16).reshape(height, width, LANES)
            lanes = slice(dx * LANES, (dx + 1) * LANES)
            xp1[f, 1 : height + 1, :, lanes] = part
            xp1[f, 0, :, lanes] = part[0]
            xp1[f, height + 1, :, lanes] = part[height - 1]

    depth = 9 * LANES
    tall = height // 2
    half = tall * width

    def conv1(dt, s):
        rows_in = [xp1[dt : dt + 2, s * tall + dy : (s + 1) * tall + dy] for dy in range(3)]
        lhs = jnp.concatenate([x.reshape(2 * half, 3 * LANES) for x in rows_in], axis=1)
        rhs = w1v[dt * depth : (dt + 1) * depth, :]
        return jnp.dot(lhs, rhs, preferred_element_type=jnp.float32)

    normalise(2)
    normalise(3)
    loads[0].wait()
    for s in range(2):
        acc[s] = conv1(2, s)

    @pl.when(t > 0)
    def _():
        for delta in range(n):
            feat_next(member(delta), me, t).wait_recv()

    @pl.when(t == 0)
    def _():
        xall[0] = xall[2]
        xall[1] = xall[2]

    normalise(0)
    normalise(1)

    def piece_copy(src, dst, source, target, s, ssem, rsem):
        return pltpu.make_async_remote_copy(
            src_ref=src.at[s, target], dst_ref=dst.at[s, source],
            send_sem=ssem.at[s, target], recv_sem=rsem.at[s, source],
            device_id=ident(t, target), device_id_type=MESH,
        )

    wide = lane_of((half, LANES))
    for s in range(2):
        total = acc[s] + conv1(1, s) + conv1(0, s)
        for d in range(n):
            k = d // 2 * LANES
            one, two = total[:half, k : k + LANES], total[half:, k : k + LANES]
            if d % 2 == 0:
                packed = jnp.where(wide < per2, one, pltpu.roll(two, per2, 1))
            else:
                packed = jnp.where(wide < per2, pltpu.roll(one, per2, 1), two)
            part1[s, d] = packed
            send1[s, d] = packed.astype(jnp.bfloat16)
        for delta in reversed(range(1, n)):
            piece_copy(send1, recv1, me, member(delta), s, r1s_sem, r1r_sem).start()

    def mid_copy(to, s):
        return pltpu.make_async_remote_copy(
            src_ref=midbf.at[s], dst_ref=prevbf.at[s],
            send_sem=ps_sem.at[s], recv_sem=pr_sem.at[s],
            device_id=ident(to, me), device_id_type=MESH,
        )

    for s in range(2):
        middle = part1[s, me] + c1
        for delta in range(1, n):
            source = member(delta)
            piece_copy(send1, recv1, source, me, s, r1s_sem, r1r_sem).wait_recv()
            middle = middle + recv1[s, source].astype(jnp.float32)
        midbf[s] = middle.astype(jnp.bfloat16)
        mids[1, s] = middle

        @pl.when(t < slabs - 1)
        def _():
            mid_copy(t + 1, s).start()

    stat2[t] = lane_stats(mids[1].reshape(area, LANES))
    for delta in range(1, slabs):
        stat_copy(stat2, t, slab(delta), s2s_sem, s2r_sem).start()

    @pl.when(t > 0)
    def _():
        for s in range(2):
            mid_copy(t, s).wait_recv()
            mids[0, s] = prevbf[s].astype(jnp.float32)

    @pl.when(t == 0)
    def _():
        for s in range(2):
            middle = mids[1, s]
            mids[0, s] = jnp.where(wide < per2, middle, pltpu.roll(middle, per2, 1))

    for delta in range(1, slabs):
        stat_copy(stat2, slab(delta), t, s2s_sem, s2r_sem).wait_recv()
    mean, inv = group_stats(stat2[...], same2, 2 * size2, float(area))
    scale = inv * g2
    for i in range(2):
        h = silu((mids[i].reshape(area, LANES) - mean) * scale + b2)
        left, right = side_shifts(h, width)
        for dx, part in enumerate((left, h, right)):
            part = part.astype(jnp.bfloat16).reshape(height, width, LANES)
            lanes = slice((2 * dx + i) * LANES, (2 * dx + i + 1) * LANES)
            xp2[1 : height + 1, :, lanes] = part
            xp2[0, :, lanes] = part[0]
            xp2[height + 1, :, lanes] = part[height - 1]

    for load in loads[2:]:
        load.wait()
    for f, weight in enumerate((wa, wb)):
        total = scut[f]
        for dy in range(3):
            lhs = xp2[dy : dy + height].reshape(area, 6 * LANES)
            rhs = weight[3 * dy : 3 * dy + 3].reshape(6 * LANES, weight.shape[2])
            total = total + jnp.dot(lhs, rhs, preferred_element_type=jnp.float32)
        total = total.reshape(height, width, weight.shape[2])
        for d in range(n):
            ri, ci = d // ncol, d % ncol
            piece = total[ri * rows : (ri + 1) * rows, ci * cols : (ci + 1) * cols]
            part2[f, d] = piece
            send2[f, d] = piece.astype(jnp.bfloat16)
        for delta in reversed(range(1, n)):
            piece_copy(send2, recv2, me, member(delta), f, r2s_sem, r2r_sem).start()

    last = bias2[...].reshape(1, 1, -1)
    for f in range(2):
        result = part2[f, me] + last
        for delta in range(1, n):
            source = member(delta)
            piece_copy(send2, recv2, source, me, f, r2s_sem, r2r_sem).wait_recv()
            result = result + recv2[f, source].astype(jnp.float32)
        out[f] = result.astype(out.dtype)

    for delta in range(1, n):
        target = member(delta)
        feat_copy(me, target).wait_send()
        for s in range(2):
            piece_copy(send1, recv1, me, target, s, r1s_sem, r1r_sem).wait_send()
            piece_copy(send2, recv2, me, target, s, r2s_sem, r2r_sem).wait_send()
    for delta in range(1, slabs):
        stat_copy(stat1, t, slab(delta), s1s_sem, s1r_sem).wait_send()
        stat_copy(stat2, t, slab(delta), s2s_sem, s2r_sem).wait_send()

    @pl.when(t < slabs - 1)
    def _():
        for delta in range(n):
            feat_next(me, member(delta), t + 1).wait_send()
        for s in range(2):
            mid_copy(t + 1, s).wait_send()


def per_device(
    features,
    gn1_gain,
    gn1_bias,
    conv1_weight,
    conv1_bias,
    skip_weight,
    gn2_gain,
    gn2_bias,
    conv2_weight,
    conv2_bias,
):
    frames, rows, cols, chans_in = features.shape
    per1, per2 = conv1_weight.shape[1], conv2_weight.shape[1]
    chans_out = conv1_weight.shape[2]
    slabs, nrow, ncol = (lax.axis_size(a) for a in ("tm", "row", "col"))
    n = nrow * ncol
    height, width = nrow * rows, ncol * cols
    area = height * width
    fits = frames == 2 and per1 == LANES and 2 * per2 == LANES and cols % 16 == 0
    fits = fits and width & (width - 1) == 0 and GROUPS % n == 0 and height % 2 == 0
    if not fits:
        return per_device_gathered(
            features, gn1_gain, gn1_bias, conv1_weight, conv1_bias, skip_weight,
            gn2_gain, gn2_bias, conv2_weight, conv2_bias,
        )
    bf16, f32 = jnp.bfloat16, jnp.float32
    vmem, dma = pltpu.VMEM, pltpu.SemaphoreType.DMA
    half = area // 2
    scratch = [
        vmem((1, chans_in), f32),
        vmem((1, chans_in), f32),
        vmem((1, chans_out), f32),
        vmem((1, chans_out), f32),
        vmem((1, chans_out), f32),
        vmem((1, chans_out), f32),
        vmem((4, height, width, LANES), bf16),
        vmem((27 * per1, chans_out), bf16),
        vmem((per1, chans_out), bf16),
        vmem((9, 4 * per2, chans_out), bf16),
        vmem((9, 4 * per2, chans_out), bf16),
        vmem((4, height + 2, width, 3 * LANES), bf16),
        vmem((height + 2, width, 6 * LANES), bf16),
        vmem((2, area, chans_out), f32),
        vmem((2, n, half, LANES), f32),
        vmem((2, n, half, LANES), bf16),
        vmem((2, n, half, LANES), bf16),
        vmem((slabs, 8, LANES), f32),
        vmem((slabs, 8, LANES), f32),
        vmem((2, 2, half, LANES), f32),
        vmem((2, half, LANES), bf16),
        vmem((2, half, LANES), bf16),
        vmem((2, area, chans_out), f32),
        vmem((2, n, rows, cols, chans_out), f32),
        vmem((2, n, rows, cols, chans_out), bf16),
        vmem((2, n, rows, cols, chans_out), bf16),
        dma((8,)), dma((6,)), dma, dma((n,)), dma((n,)), dma((n,)), dma((n,)),
        dma((slabs,)), dma((slabs,)), dma((slabs,)), dma((slabs,)),
        dma((2, n)), dma((2, n)), dma((2, n)), dma((2, n)),
        dma((2,)), dma((2,)),
    ]
    stays = pl.BlockSpec(memory_space=pltpu.HBM)
    inside = pl.BlockSpec(memory_space=pltpu.VMEM)
    sizes = (slabs, nrow, ncol, rows, cols, per1, per2)
    flops = 2 * 2 * area * chans_out * (28 * per1 + 27 * per2)
    return pl.pallas_call(
        functools.partial(block_kernel, sizes),
        out_shape=jax.ShapeDtypeStruct((frames, rows, cols, chans_out), bf16),
        in_specs=[stays] * 10,
        out_specs=inside,
        scratch_shapes=scratch,
        compiler_params=pltpu.CompilerParams(
            collective_id=0, has_side_effects=True, vmem_limit_bytes=64 * 1024 * 1024
        ),
        cost_estimate=pl.CostEstimate(
            flops=flops, bytes_accessed=4 * 1024 * 1024, transcendentals=6 * area * LANES
        ),
        name="residual_block",
    )(
        features,
        gn1_gain.reshape(1, -1),
        gn1_bias.reshape(1, -1),
        conv1_weight.reshape(27 * per1, chans_out),
        conv1_bias.reshape(1, -1),
        skip_weight.reshape(per1, chans_out),
        gn2_gain.reshape(1, -1),
        gn2_bias.reshape(1, -1),
        conv2_weight.reshape(3, 9, per2, chans_out),
        conv2_bias.reshape(1, -1),
    )


def solution(mesh):
    in_specs = (
        P("tm", "row", "col", None),
        P(),
        P(),
        P(None, ("row", "col"), None),
        P(),
        P(None, ("row", "col"), None),
        P(),
        P(),
        P(None, ("row", "col"), None),
        P(),
    )
    out_specs = P("tm", "row", "col", None)
    return jax.shard_map(
        per_device, mesh=mesh, in_specs=in_specs, out_specs=out_specs, check_vma=False
    )
```

```python
import functools

import jax
import jax.numpy as jnp
from jax import lax
from jax.experimental import pallas as pl
from jax.experimental.pallas import tpu as pltpu
from jax.sharding import PartitionSpec as P

GROUPS = 32


def passed_along(block, axis, distance):
    devices = range(lax.axis_size(axis))
    route = [(i - distance, i) for i in devices if i - distance in devices]
    return lax.ppermute(block, axis, route)


def with_halo(array, sides, width):
    for axis, dim in sides:
        size, length = (lax.axis_size(axis), array.shape[dim])
        up = [(i, (i + 1) % size) for i in range(size - 1)]
        down = [(j, i) for i, j in up]
        last = lax.slice_in_dim(array, length - width, length, axis=dim)
        leading = lax.slice_in_dim(array, 0, width, axis=dim)
        before = lax.ppermute(last, axis, up)
        after = lax.ppermute(leading, axis, down)
        array = jnp.concatenate([before, array, after], axis=dim)
    return array


def group_silu(values, gain, shift, groups, total_rows):
    chans = values.shape[-1]
    per_group = chans // groups
    grouped = values.reshape(-1, groups, per_group)
    count = float(total_rows * per_group)
    mean = lax.psum(jnp.sum(grouped, axis=(0, 2)), ("tm", "row", "col")) / count
    centred = grouped - mean[None, :, None]
    spread = lax.psum(jnp.sum(centred * centred, axis=(0, 2)), ("tm", "row", "col")) / count
    normed = (grouped - mean[None, :, None]) * lax.rsqrt(spread + 1e-06)[None, :, None]
    normed = normed.reshape(values.shape) * gain + shift
    return jax.nn.silu(normed).astype(jnp.bfloat16)


def conv_taps(padded, weight, frames, rows, cols):
    chans = padded.shape[3]
    total = jnp.zeros((frames * rows * cols, weight.shape[2]), jnp.float32)
    for dt in range(3):
        pieces = []
        for tap in range(9):
            dy, dx = (tap // 3, tap % 3)
            pieces.append(
                padded[dt : dt + frames, dy : dy + rows, dx : dx + cols].reshape(-1, chans)
            )
        stacked = jnp.concatenate(pieces, axis=1)
        flat_weight = weight[9 * dt : 9 * dt + 9].reshape(9 * chans, weight.shape[2])
        total = total + jnp.dot(stacked, flat_weight, preferred_element_type=jnp.float32)
    return total


def time_edge(earlier, volume):
    first_twice = jnp.concatenate([volume[:1], volume[:1]], axis=0)
    earlier = jnp.where(lax.axis_index("tm") == 0, first_twice, earlier)
    return jnp.concatenate([earlier, volume], axis=0)


def edge_rows(padded):
    place = lax.axis_index("row")
    last = lax.axis_size("row") - 1
    top = jnp.where(place == 0, padded[:, 1:2], padded[:, 0:1])
    bottom = jnp.where(place == last, padded[:, -2:-1], padded[:, -1:])
    return jnp.concatenate([top, padded[:, 1:-1], bottom], axis=1)


def edge_cols(padded):
    place = lax.axis_index("col")
    last = lax.axis_size("col") - 1
    left = jnp.where(place == 0, padded[:, :, 1:2], padded[:, :, 0:1])
    right = jnp.where(place == last, padded[:, :, -2:-1], padded[:, :, -1:])
    return jnp.concatenate([left, padded[:, :, 1:-1], right], axis=2)


def per_device_gathered(
    features,
    gn1_gain,
    gn1_bias,
    conv1_weight,
    conv1_bias,
    skip_weight,
    gn2_gain,
    gn2_bias,
    conv2_weight,
    conv2_bias,
):
    frames, rows, cols, chans_in = features.shape
    chans_out = conv1_weight.shape[2]
    groups = GROUPS
    nrow = lax.axis_size("row")
    ncol = lax.axis_size("col")
    total_rows = lax.axis_size("tm") * nrow * ncol * frames * rows * cols
    flat_features = features.reshape(-1, chans_in)
    hidden1 = group_silu(features.astype(jnp.float32), gn1_gain, gn1_bias, groups, total_rows)
    earlier = passed_along(hidden1, "tm", 1)
    extended = time_edge(earlier, hidden1)
    padded = with_halo(extended, (("row", 1), ("col", 2)), 1)
    padded = edge_cols(edge_rows(padded))
    window = padded
    first = conv_taps(
        window, lax.all_gather(conv1_weight, ("row", "col"), axis=1, tiled=True), frames, rows, cols
    )
    second = jnp.dot(
        flat_features,
        lax.all_gather(skip_weight, ("row", "col"), axis=1, tiled=True)[0],
        preferred_element_type=jnp.float32,
    )
    middle = (first + conv1_bias).reshape(frames, rows, cols, chans_out)
    hidden2 = group_silu(middle, gn2_gain, gn2_bias, groups, total_rows)
    earlier_mid = passed_along(hidden2, "tm", 1)
    extended_mid = time_edge(earlier_mid, hidden2)
    padded_mid = with_halo(extended_mid, (("row", 1), ("col", 2)), 1)
    padded_mid = edge_cols(edge_rows(padded_mid))
    window = padded_mid
    conv_second = conv_taps(
        window, lax.all_gather(conv2_weight, ("row", "col"), axis=1, tiled=True), frames, rows, cols
    )
    block_out = (second + conv_second + conv2_bias).astype(jnp.bfloat16)
    return block_out.reshape(frames, rows, cols, chans_out)


MESH = pl.DeviceIdType.MESH
LANES = 128


def lane_of(shape):
    return lax.broadcasted_iota(jnp.int32, shape, len(shape) - 1)


def silu(a):
    half = 0.5 * a
    return half + half * jnp.tanh(half)


def lane_stats(x):
    mean = jnp.sum(x, axis=0, keepdims=True) * (1.0 / x.shape[0])
    spread = jnp.sum((x - mean) ** 2, axis=0, keepdims=True)
    row = lax.broadcasted_iota(jnp.int32, (8, LANES), 0)
    return jnp.where(row == 0, mean, jnp.where(row == 1, spread, 0.0))


def group_stats(means, spreads, same, lanes, count):
    parts = means.shape[0]
    mean = jnp.sum(means, axis=0) * (1.0 / parts)
    spread = jnp.sum(spreads, axis=0) + count * jnp.sum((means - mean[None]) ** 2, axis=0)
    mean = jnp.broadcast_to(mean, (8, LANES))
    group_mean = (
        jnp.dot(mean, same, precision=lax.Precision.HIGHEST, preferred_element_type=jnp.float32)
        * (1.0 / lanes)
    )
    spread = spread + (count * parts) * (mean - group_mean) ** 2
    total = jnp.dot(
        spread, same, precision=lax.Precision.HIGHEST, preferred_element_type=jnp.float32
    )
    inv = lax.rsqrt(total * (1.0 / (count * parts * lanes)) + 1e-6)
    return group_mean[0:1], inv[0:1]


def side_shifts(h, cols):
    col = lax.broadcasted_iota(jnp.int32, h.shape, 0) & (cols - 1)
    length = h.shape[0]
    left = jnp.where(col == 0, h, pltpu.roll(h, 1, 0))
    right = jnp.where(col == cols - 1, h, pltpu.roll(h, length - 1, 0))
    return left, right


def block_kernel(
    sizes,
    feat, gain1_hbm, shift1_hbm, w1, bias1_hbm, wskip, gain2_hbm, shift2_hbm, w2, bias2_hbm,
    out,
    gain1, shift1, bias1, gain2, shift2, bias2, featv, xall, w1v, wsv, wcat, xp1, xp2,
    acc, part1, send1, recv1, sum1, send1b, recv1b, stat0, statg, stat2,
    mids, midbf, prevbf, scut, part2, send2, recv2, sum2, send2b, recv2b,
    w_sem, p_sem, own_sem, fs_sem, fr_sem, fps_sem, fpr_sem,
    s1s_sem, s1r_sem, sgs_sem, sgr_sem, s2s_sem, s2r_sem,
    r1s_sem, r1r_sem, r1bs_sem, r1br_sem, r2s_sem, r2r_sem, r2bs_sem, r2br_sem,
    ps_sem, pr_sem,
):
    slabs, nrow, ncol, rows, cols, per1, per2 = sizes
    n = nrow * ncol
    height, width = nrow * rows, ncol * cols
    area = height * width
    t = lax.axis_index("tm")
    r = lax.axis_index("row")
    c = lax.axis_index("col")
    me = r * ncol + c

    def place(i):
        return lax.div(i, ncol), lax.rem(i, ncol)

    def ident(ti, i):
        ri, ci = place(i)
        return {"tm": ti, "row": ri, "col": ci}

    def member(delta):
        return lax.rem(r + delta // ncol, nrow) * ncol + lax.rem(c + delta % ncol, ncol)

    def slab(delta):
        return lax.rem(t + delta, slabs)

    loads = [
        pltpu.make_async_copy(w1, w1v, w_sem.at[0]),
        pltpu.make_async_copy(wskip, wsv, w_sem.at[1]),
    ]
    for i, (f, p, place_in, dt) in enumerate(
        ((0, 0, 0, 0), (0, 0, 1, 1), (0, 1, 0, 2), (1, 0, 1, 0), (1, 1, 0, 1), (1, 1, 1, 2))
    ):
        lo = place_in * per2
        loads.append(
            pltpu.make_async_copy(
                w2.at[dt], wcat.at[f, p, :, lo : lo + per2, :], w_sem.at[2 + i]
            )
        )
    params = [
        pltpu.make_async_copy(source, target, p_sem.at[i])
        for i, (source, target) in enumerate(
            (
                (gain1_hbm, gain1), (shift1_hbm, shift1), (bias1_hbm, bias1),
                (gain2_hbm, gain2), (shift2_hbm, shift2), (bias2_hbm, bias2),
            )
        )
    ]

    def window(frame0, i):
        ri, ci = place(i)
        top = ri * rows
        left = pl.multiple_of(ci * cols, cols)
        return xall.at[frame0 : frame0 + 2, pl.ds(top, rows), pl.ds(left, cols), :]

    def chunk(i):
        return feat.at[:, :, :, pl.ds(pl.multiple_of(i * LANES, LANES), LANES)]

    whole = pltpu.make_async_copy(feat, featv, own_sem.at[1])
    whole.start()
    own = pltpu.make_async_copy(chunk(me), window(2, me), own_sem.at[0])
    own.start()

    barrier = pltpu.get_barrier_semaphore()
    for delta in range(1, n):
        pl.semaphore_signal(barrier, inc=1, device_id=ident(t, member(delta)), device_id_type=MESH)
    for delta in range(1, slabs):
        pl.semaphore_signal(barrier, inc=1, device_id=ident(slab(delta), me), device_id_type=MESH)

    @pl.when(t > 0)
    def _():
        for delta in range(1, n):
            pl.semaphore_signal(
                barrier, inc=1, device_id=ident(t - 1, member(delta)), device_id_type=MESH
            )

    for load in params + loads:
        load.start()
    blank = jnp.zeros((9, per2, wcat.shape[4]), wcat.dtype)
    wcat[0, 1, :, per2:, :] = blank
    wcat[1, 0, :, :per2, :] = blank

    row8 = lax.broadcasted_iota(jnp.int32, (2 * n, LANES), 0)
    spots = float(2 * rows * cols)
    whole.wait()
    x = featv[...].reshape(2 * rows * cols, n * LANES).astype(jnp.float32)
    lane_mean = jnp.sum(x, axis=0, keepdims=True) * (1.0 / spots)
    lane_spread = jnp.sum((x - lane_mean) ** 2, axis=0, keepdims=True)
    tile = jnp.zeros((2 * n, LANES), jnp.float32)
    for d in range(n):
        at = slice(d * LANES, (d + 1) * LANES)
        tile = jnp.where(row8 == d, lane_mean[:, at], tile)
        tile = jnp.where(row8 == n + d, lane_spread[:, at], tile)
    stat0[t] = tile

    pl.semaphore_wait(barrier, jnp.where(t < slabs - 1, 2 * (n - 1), n - 1) + slabs - 1)

    def stat_copy(buf, source, target, ssem, rsem):
        return pltpu.make_async_remote_copy(
            src_ref=buf.at[source], dst_ref=buf.at[source],
            send_sem=ssem.at[target], recv_sem=rsem.at[source],
            device_id=ident(target, me), device_id_type=MESH,
        )

    def share_copy(source, target):
        return pltpu.make_async_remote_copy(
            src_ref=statg.at[source], dst_ref=statg.at[source],
            send_sem=sgs_sem.at[target], recv_sem=sgr_sem.at[source],
            device_id=ident(t, target), device_id_type=MESH,
        )

    for delta in reversed(range(1, slabs)):
        stat_copy(stat0, t, slab(delta), s1s_sem, s1r_sem).start()

    def feat_copy(source, target):
        return pltpu.make_async_remote_copy(
            src_ref=chunk(target), dst_ref=window(2, source),
            send_sem=fs_sem.at[target], recv_sem=fr_sem.at[source],
            device_id=ident(t, target), device_id_type=MESH,
        )

    def feat_next(source, target, to):
        return pltpu.make_async_remote_copy(
            src_ref=chunk(target), dst_ref=window(0, source),
            send_sem=fps_sem.at[target], recv_sem=fpr_sem.at[source],
            device_id=ident(to, target), device_id_type=MESH,
        )

    for delta in reversed(range(1, n)):
        feat_copy(me, member(delta)).start()

    @pl.when(t < slabs - 1)
    def _():
        for delta in reversed(range(n)):
            feat_next(me, member(delta), t + 1).start()

    lane = lane_of((8, LANES))
    lane_in = lax.broadcasted_iota(jnp.int32, (LANES, LANES), 0)
    lane_to = lane_of((LANES, LANES))
    size1 = per1 // (GROUPS // n)
    size2 = per2 // (GROUPS // n)
    same1 = (lane_in // size1 == lane_to // size1).astype(jnp.float32)
    same2 = ((lane_in % per2) // size2 == (lane_to % per2) // size2).astype(jnp.float32)

    def own_full(ref):
        result = ref[0:1, 0:LANES]
        for d in range(1, n):
            result = jnp.where(me == d, ref[0:1, d * LANES : (d + 1) * LANES], result)
        return result

    def own_twice(ref):
        result = jnp.zeros((8, LANES), jnp.float32)
        for d in range(n):
            k = d // 2 * LANES
            seg = jnp.broadcast_to(ref[0:1, k : k + LANES], (8, LANES))
            turned = pltpu.roll(seg, per2, 1)
            twice = jnp.where((lane < per2) == (d % 2 == 0), seg, turned)
            result = jnp.where(me == d, twice, result)
        return result[0:1]

    for load in params:
        load.wait()
    g1, b1 = own_full(gain1), own_full(shift1)
    g2, b2, c1 = own_twice(gain2), own_twice(shift2), own_twice(bias1)

    for delta in range(1, slabs):
        stat_copy(stat0, slab(delta), t, s1s_sem, s1r_sem).wait_recv()
    stats = stat0[...]
    total = jnp.sum(stats, axis=0)
    mean = total * (1.0 / slabs)
    off = spots * jnp.sum((stats - mean[None]) ** 2, axis=0)
    statg[me] = jnp.where(row8 < n, mean, total + pltpu.roll(off, n, 0))
    for delta in reversed(range(1, n)):
        share_copy(me, member(delta)).start()

    own.wait()
    for delta in range(1, n):
        feat_copy(member(delta), me).wait_recv()
    loads[1].wait()
    for f in range(2):
        x = xall[2 + f].reshape(area, LANES)
        scut[f] = jnp.dot(x, wsv[...], preferred_element_type=jnp.float32)

    for delta in range(1, n):
        share_copy(member(delta), me).wait_recv()
    stats = statg[...]
    pick = lax.broadcasted_iota(jnp.int32, stats.shape, 1)
    means = jnp.sum(jnp.where(pick == me, stats, 0.0), axis=1, keepdims=True)
    spreads = jnp.sum(jnp.where(pick == n + me, stats, 0.0), axis=1, keepdims=True)
    mean, inv = group_stats(means, spreads, same1, size1, spots * slabs)
    scale = inv * g1

    def normalise(f):
        x = xall[f].reshape(area, LANES).astype(jnp.float32)
        h = silu((x - mean) * scale + b1)
        left, right = side_shifts(h, width)
        for dx, part in enumerate((left, h, right)):
            part = part.astype(jnp.bfloat16).reshape(height, width, LANES)
            lanes = slice(dx * LANES, (dx + 1) * LANES)
            xp1[f, 1 : height + 1, :, lanes] = part
            xp1[f, 0, :, lanes] = part[0]
            xp1[f, height + 1, :, lanes] = part[height - 1]

    depth = 9 * LANES
    tall = height // 2
    half = tall * width

    def conv1(dt, s):
        rows_in = [xp1[dt : dt + 2, s * tall + dy : (s + 1) * tall + dy] for dy in range(3)]
        lhs = jnp.concatenate([x.reshape(2 * half, 3 * LANES) for x in rows_in], axis=1)
        rhs = w1v[dt * depth : (dt + 1) * depth, :]
        return jnp.dot(lhs, rhs, preferred_element_type=jnp.float32)

    normalise(2)
    normalise(3)
    loads[0].wait()
    for s in range(2):
        acc[s] = conv1(2, s)

    @pl.when(t > 0)
    def _():
        for delta in range(n):
            feat_next(member(delta), me, t).wait_recv()

    @pl.when(t == 0)
    def _():
        xall[0] = xall[2]
        xall[1] = xall[2]

    normalise(0)
    normalise(1)

    def core_copy(src, dst, source, target, s, ssem, rsem):
        return pltpu.make_async_remote_copy(
            src_ref=src.at[s, target], dst_ref=dst.at[s, source],
            send_sem=ssem.at[s, target], recv_sem=rsem.at[s, source],
            device_id={"tm": t, "row": r, "col": target}, device_id_type=MESH,
        )

    def row_copy(src, dst, source, target, s, ssem, rsem):
        return pltpu.make_async_remote_copy(
            src_ref=src.at[s, target], dst_ref=dst.at[s, source],
            send_sem=ssem.at[s, target], recv_sem=rsem.at[s, source],
            device_id={"tm": t, "row": target, "col": c}, device_id_type=MESH,
        )

    cores = [lax.rem(c + delta, ncol) for delta in range(1, ncol)]
    others = [lax.rem(r + delta, nrow) for delta in range(1, nrow)]

    def to_cores(stage, s):
        send, recv, ssem, rsem = stage
        for core in cores:
            core_copy(send, recv, c, core, s, ssem, rsem).start()

    def to_rows(stage, part, total, stage_b, s):
        send, recv, ssem, rsem = stage
        send_b, recv_b, ssem_b, rsem_b = stage_b
        summed = part[s, c]
        for core in cores:
            core_copy(send, recv, core, c, s, ssem, rsem).wait_recv()
            summed = summed + recv[s, core].astype(jnp.float32)
        total[s] = summed
        send_b[s] = summed.astype(jnp.bfloat16)
        for other in others:
            row_copy(send_b, recv_b, r, other, s, ssem_b, rsem_b).start()

    def from_rows(total, stage_b, s):
        send_b, recv_b, ssem_b, rsem_b = stage_b
        result = total[s, r]
        for other in others:
            row_copy(send_b, recv_b, other, r, s, ssem_b, rsem_b).wait_recv()
            result = result + recv_b[s, other].astype(jnp.float32)
        return result

    first = (send1, recv1, r1s_sem, r1r_sem)
    first_b = (send1b, recv1b, r1bs_sem, r1br_sem)
    second = (send2, recv2, r2s_sem, r2r_sem)
    second_b = (send2b, recv2b, r2bs_sem, r2br_sem)

    wide = lane_of((half, LANES))
    for s in range(2):
        total = acc[s] + conv1(1, s) + conv1(0, s)
        for d in range(n):
            k = d // 2 * LANES
            one, two = total[:half, k : k + LANES], total[half:, k : k + LANES]
            if d % 2 == 0:
                packed = jnp.where(wide < per2, one, pltpu.roll(two, per2, 1))
            else:
                packed = jnp.where(wide < per2, pltpu.roll(one, per2, 1), two)
            part1[s, d % ncol, d // ncol] = packed
            send1[s, d % ncol, d // ncol] = packed.astype(jnp.bfloat16)
        to_cores(first, s)
    for s in range(2):
        to_rows(first, part1, sum1, first_b, s)

    def mid_copy(to, s):
        return pltpu.make_async_remote_copy(
            src_ref=midbf.at[s], dst_ref=prevbf.at[s],
            send_sem=ps_sem.at[s], recv_sem=pr_sem.at[s],
            device_id=ident(to, me), device_id_type=MESH,
        )

    def pass_on(s):
        @pl.when(t < slabs - 1)
        def _():
            mid_copy(t + 1, s).start()

    for s in range(2):
        middle = from_rows(sum1, first_b, s) + c1
        midbf[s] = middle.astype(jnp.bfloat16)
        mids[1, s] = middle
        if s == 0:
            pass_on(0)

    stat2[t] = lane_stats(mids[1].reshape(area, LANES))
    for delta in reversed(range(1, slabs)):
        stat_copy(stat2, t, slab(delta), s2s_sem, s2r_sem).start()
    pass_on(1)

    for delta in range(1, slabs):
        stat_copy(stat2, slab(delta), t, s2s_sem, s2r_sem).wait_recv()
    stats = stat2[...]
    mean, inv = group_stats(stats[:, 0:1], stats[:, 1:2], same2, 2 * size2, float(area))
    scale = inv * g2

    def normalise_mid(i):
        h = silu((mids[i].reshape(area, LANES) - mean) * scale + b2)
        left, right = side_shifts(h, width)
        for dx, part in enumerate((left, h, right)):
            part = part.astype(jnp.bfloat16).reshape(height, width, LANES)
            lanes = slice(dx * LANES, (dx + 1) * LANES)
            xp2[i, 1 : height + 1, :, lanes] = part
            xp2[i, 0, :, lanes] = part[0]
            xp2[i, height + 1, :, lanes] = part[height - 1]

    def conv2(f, i):
        rows_in = [xp2[i, dy : dy + height].reshape(area, 3 * LANES) for dy in range(3)]
        rhs = wcat[f, i].reshape(9 * LANES, wcat.shape[4])
        return jnp.dot(
            jnp.concatenate(rows_in, axis=1), rhs, preferred_element_type=jnp.float32
        )

    normalise_mid(1)
    for load in loads[2:]:
        load.wait()
    for f in range(2):
        scut[f] = scut[f] + conv2(f, 1)

    @pl.when(t > 0)
    def _():
        for s in range(2):
            mid_copy(t, s).wait_recv()
            mids[0, s] = prevbf[s].astype(jnp.float32)

    @pl.when(t == 0)
    def _():
        for s in range(2):
            middle = mids[1, s]
            mids[0, s] = jnp.where(wide < per2, middle, pltpu.roll(middle, per2, 1))

    normalise_mid(0)
    for f in range(2):
        total = (scut[f] + conv2(f, 0)).reshape(nrow, rows, width, wcat.shape[4])
        for ci in range(ncol):
            piece = total[:, :, ci * cols : (ci + 1) * cols]
            part2[f, ci] = piece
            send2[f, ci] = piece.astype(jnp.bfloat16)
        to_cores(second, f)
    for f in range(2):
        to_rows(second, part2, sum2, second_b, f)
    last = bias2[...].reshape(1, 1, -1)
    for f in range(2):
        out[f] = (from_rows(sum2, second_b, f) + last).astype(out.dtype)

    for delta in range(1, n):
        target = member(delta)
        feat_copy(me, target).wait_send()
        share_copy(me, target).wait_send()
    for s in range(2):
        for send, recv, ssem, rsem in (first, second):
            for core in cores:
                core_copy(send, recv, c, core, s, ssem, rsem).wait_send()
        for send, recv, ssem, rsem in (first_b, second_b):
            for other in others:
                row_copy(send, recv, r, other, s, ssem, rsem).wait_send()
    for delta in range(1, slabs):
        stat_copy(stat0, t, slab(delta), s1s_sem, s1r_sem).wait_send()
        stat_copy(stat2, t, slab(delta), s2s_sem, s2r_sem).wait_send()

    @pl.when(t < slabs - 1)
    def _():
        for delta in range(n):
            feat_next(me, member(delta), t + 1).wait_send()
        for s in range(2):
            mid_copy(t + 1, s).wait_send()


def per_device(
    features,
    gn1_gain,
    gn1_bias,
    conv1_weight,
    conv1_bias,
    skip_weight,
    gn2_gain,
    gn2_bias,
    conv2_weight,
    conv2_bias,
):
    frames, rows, cols, chans_in = features.shape
    per1, per2 = conv1_weight.shape[1], conv2_weight.shape[1]
    chans_out = conv1_weight.shape[2]
    slabs, nrow, ncol = (lax.axis_size(a) for a in ("tm", "row", "col"))
    n = nrow * ncol
    height, width = nrow * rows, ncol * cols
    area = height * width
    fits = frames == 2 and per1 == LANES and 2 * per2 == LANES and cols % 16 == 0
    fits = fits and n == 4 and width & (width - 1) == 0 and GROUPS % n == 0 and height % 2 == 0
    if not fits:
        return per_device_gathered(
            features, gn1_gain, gn1_bias, conv1_weight, conv1_bias, skip_weight,
            gn2_gain, gn2_bias, conv2_weight, conv2_bias,
        )
    bf16, f32 = jnp.bfloat16, jnp.float32
    vmem, dma = pltpu.VMEM, pltpu.SemaphoreType.DMA
    half = area // 2
    scratch = [
        vmem((1, chans_in), f32),
        vmem((1, chans_in), f32),
        vmem((1, chans_out), f32),
        vmem((1, chans_out), f32),
        vmem((1, chans_out), f32),
        vmem((1, chans_out), f32),
        vmem((frames, rows, cols, chans_in), bf16),
        vmem((4, height, width, LANES), bf16),
        vmem((27 * per1, chans_out), bf16),
        vmem((per1, chans_out), bf16),
        vmem((2, 2, 9, 2 * per2, chans_out), bf16),
        vmem((4, height + 2, width, 3 * LANES), bf16),
        vmem((2, height + 2, width, 3 * LANES), bf16),
        vmem((2, area, chans_out), f32),
        vmem((2, ncol, nrow, half, LANES), f32),
        vmem((2, ncol, nrow, half, LANES), bf16),
        vmem((2, ncol, nrow, half, LANES), bf16),
        vmem((2, nrow, half, LANES), f32),
        vmem((2, nrow, half, LANES), bf16),
        vmem((2, nrow, half, LANES), bf16),
        vmem((slabs, 2 * n, LANES), f32),
        vmem((n, 2 * n, LANES), f32),
        vmem((slabs, 8, LANES), f32),
        vmem((2, 2, half, LANES), f32),
        vmem((2, half, LANES), bf16),
        vmem((2, half, LANES), bf16),
        vmem((2, area, chans_out), f32),
        vmem((2, ncol, nrow, rows, cols, chans_out), f32),
        vmem((2, ncol, nrow, rows, cols, chans_out), bf16),
        vmem((2, ncol, nrow, rows, cols, chans_out), bf16),
        vmem((2, nrow, rows, cols, chans_out), f32),
        vmem((2, nrow, rows, cols, chans_out), bf16),
        vmem((2, nrow, rows, cols, chans_out), bf16),
        dma((8,)), dma((6,)), dma((2,)), dma((n,)), dma((n,)), dma((n,)), dma((n,)),
        dma((slabs,)), dma((slabs,)), dma((n,)), dma((n,)), dma((slabs,)), dma((slabs,)),
        dma((2, ncol)), dma((2, ncol)), dma((2, nrow)), dma((2, nrow)),
        dma((2, ncol)), dma((2, ncol)), dma((2, nrow)), dma((2, nrow)),
        dma((2,)), dma((2,)),
    ]
    stays = pl.BlockSpec(memory_space=pltpu.HBM)
    inside = pl.BlockSpec(memory_space=pltpu.VMEM)
    sizes = (slabs, nrow, ncol, rows, cols, per1, per2)
    flops = 2 * 2 * area * chans_out * (28 * per1 + 27 * per2)
    return pl.pallas_call(
        functools.partial(block_kernel, sizes),
        out_shape=jax.ShapeDtypeStruct((frames, rows, cols, chans_out), bf16),
        in_specs=[stays] * 10,
        out_specs=inside,
        scratch_shapes=scratch,
        compiler_params=pltpu.CompilerParams(
            collective_id=0, has_side_effects=True, vmem_limit_bytes=64 * 1024 * 1024
        ),
        cost_estimate=pl.CostEstimate(
            flops=flops, bytes_accessed=4 * 1024 * 1024, transcendentals=6 * area * LANES
        ),
        name="residual_block",
    )(
        features,
        gn1_gain.reshape(1, -1),
        gn1_bias.reshape(1, -1),
        conv1_weight.reshape(27 * per1, chans_out),
        conv1_bias.reshape(1, -1),
        skip_weight.reshape(per1, chans_out),
        gn2_gain.reshape(1, -1),
        gn2_bias.reshape(1, -1),
        conv2_weight.reshape(3, 9, per2, chans_out),
        conv2_bias.reshape(1, -1),
    )


def solution(mesh):
    in_specs = (
        P("tm", "row", "col", None),
        P(),
        P(),
        P(None, ("row", "col"), None),
        P(),
        P(None, ("row", "col"), None),
        P(),
        P(),
        P(None, ("row", "col"), None),
        P(),
    )
    out_specs = P("tm", "row", "col", None)
    return jax.shard_map(
        per_device, mesh=mesh, in_specs=in_specs, out_specs=out_specs, check_vma=False
    )
```

```python
import functools

import jax
import jax.numpy as jnp
from jax import lax
from jax.experimental import pallas as pl
from jax.experimental.pallas import tpu as pltpu
from jax.sharding import PartitionSpec as P

GROUPS = 32


def passed_along(block, axis, distance):
    devices = range(lax.axis_size(axis))
    route = [(i - distance, i) for i in devices if i - distance in devices]
    return lax.ppermute(block, axis, route)


def with_halo(array, sides, width):
    for axis, dim in sides:
        size, length = (lax.axis_size(axis), array.shape[dim])
        up = [(i, (i + 1) % size) for i in range(size - 1)]
        down = [(j, i) for i, j in up]
        last = lax.slice_in_dim(array, length - width, length, axis=dim)
        leading = lax.slice_in_dim(array, 0, width, axis=dim)
        before = lax.ppermute(last, axis, up)
        after = lax.ppermute(leading, axis, down)
        array = jnp.concatenate([before, array, after], axis=dim)
    return array


def group_silu(values, gain, shift, groups, total_rows):
    chans = values.shape[-1]
    per_group = chans // groups
    grouped = values.reshape(-1, groups, per_group)
    count = float(total_rows * per_group)
    mean = lax.psum(jnp.sum(grouped, axis=(0, 2)), ("tm", "row", "col")) / count
    centred = grouped - mean[None, :, None]
    spread = lax.psum(jnp.sum(centred * centred, axis=(0, 2)), ("tm", "row", "col")) / count
    normed = (grouped - mean[None, :, None]) * lax.rsqrt(spread + 1e-06)[None, :, None]
    normed = normed.reshape(values.shape) * gain + shift
    return jax.nn.silu(normed).astype(jnp.bfloat16)


def conv_taps(padded, weight, frames, rows, cols):
    chans = padded.shape[3]
    total = jnp.zeros((frames * rows * cols, weight.shape[2]), jnp.float32)
    for dt in range(3):
        pieces = []
        for tap in range(9):
            dy, dx = (tap // 3, tap % 3)
            pieces.append(
                padded[dt : dt + frames, dy : dy + rows, dx : dx + cols].reshape(-1, chans)
            )
        stacked = jnp.concatenate(pieces, axis=1)
        flat_weight = weight[9 * dt : 9 * dt + 9].reshape(9 * chans, weight.shape[2])
        total = total + jnp.dot(stacked, flat_weight, preferred_element_type=jnp.float32)
    return total


def time_edge(earlier, volume):
    first_twice = jnp.concatenate([volume[:1], volume[:1]], axis=0)
    earlier = jnp.where(lax.axis_index("tm") == 0, first_twice, earlier)
    return jnp.concatenate([earlier, volume], axis=0)


def edge_rows(padded):
    place = lax.axis_index("row")
    last = lax.axis_size("row") - 1
    top = jnp.where(place == 0, padded[:, 1:2], padded[:, 0:1])
    bottom = jnp.where(place == last, padded[:, -2:-1], padded[:, -1:])
    return jnp.concatenate([top, padded[:, 1:-1], bottom], axis=1)


def edge_cols(padded):
    place = lax.axis_index("col")
    last = lax.axis_size("col") - 1
    left = jnp.where(place == 0, padded[:, :, 1:2], padded[:, :, 0:1])
    right = jnp.where(place == last, padded[:, :, -2:-1], padded[:, :, -1:])
    return jnp.concatenate([left, padded[:, :, 1:-1], right], axis=2)


def per_device_gathered(
    features,
    gn1_gain,
    gn1_bias,
    conv1_weight,
    conv1_bias,
    skip_weight,
    gn2_gain,
    gn2_bias,
    conv2_weight,
    conv2_bias,
):
    frames, rows, cols, chans_in = features.shape
    chans_out = conv1_weight.shape[2]
    groups = GROUPS
    nrow = lax.axis_size("row")
    ncol = lax.axis_size("col")
    total_rows = lax.axis_size("tm") * nrow * ncol * frames * rows * cols
    flat_features = features.reshape(-1, chans_in)
    hidden1 = group_silu(features.astype(jnp.float32), gn1_gain, gn1_bias, groups, total_rows)
    earlier = passed_along(hidden1, "tm", 1)
    extended = time_edge(earlier, hidden1)
    padded = with_halo(extended, (("row", 1), ("col", 2)), 1)
    padded = edge_cols(edge_rows(padded))
    window = padded
    first = conv_taps(
        window, lax.all_gather(conv1_weight, ("row", "col"), axis=1, tiled=True), frames, rows, cols
    )
    second = jnp.dot(
        flat_features,
        lax.all_gather(skip_weight, ("row", "col"), axis=1, tiled=True)[0],
        preferred_element_type=jnp.float32,
    )
    middle = (first + conv1_bias).reshape(frames, rows, cols, chans_out)
    hidden2 = group_silu(middle, gn2_gain, gn2_bias, groups, total_rows)
    earlier_mid = passed_along(hidden2, "tm", 1)
    extended_mid = time_edge(earlier_mid, hidden2)
    padded_mid = with_halo(extended_mid, (("row", 1), ("col", 2)), 1)
    padded_mid = edge_cols(edge_rows(padded_mid))
    window = padded_mid
    conv_second = conv_taps(
        window, lax.all_gather(conv2_weight, ("row", "col"), axis=1, tiled=True), frames, rows, cols
    )
    block_out = (second + conv_second + conv2_bias).astype(jnp.bfloat16)
    return block_out.reshape(frames, rows, cols, chans_out)


MESH = pl.DeviceIdType.MESH
LANES = 128


def lane_of(shape):
    return lax.broadcasted_iota(jnp.int32, shape, len(shape) - 1)


def silu(a):
    half = 0.5 * a
    return half + half * jnp.tanh(half)


def lane_stats(x):
    mean = jnp.sum(x, axis=0, keepdims=True) * (1.0 / x.shape[0])
    spread = jnp.sum((x - mean) ** 2, axis=0, keepdims=True)
    row = lax.broadcasted_iota(jnp.int32, (8, LANES), 0)
    return jnp.where(row == 0, mean, jnp.where(row == 1, spread, 0.0))


def group_stats(means, spreads, same, lanes, count):
    parts = means.shape[0]
    mean = jnp.sum(means, axis=0) * (1.0 / parts)
    spread = jnp.sum(spreads, axis=0) + count * jnp.sum((means - mean[None]) ** 2, axis=0)
    mean = jnp.broadcast_to(mean, (8, LANES))
    group_mean = (
        jnp.dot(mean, same, precision=lax.Precision.HIGHEST, preferred_element_type=jnp.float32)
        * (1.0 / lanes)
    )
    spread = spread + (count * parts) * (mean - group_mean) ** 2
    total = jnp.dot(
        spread, same, precision=lax.Precision.HIGHEST, preferred_element_type=jnp.float32
    )
    inv = lax.rsqrt(total * (1.0 / (count * parts * lanes)) + 1e-6)
    return group_mean[0:1], inv[0:1]


def side_shifts(h, cols):
    col = lax.broadcasted_iota(jnp.int32, h.shape, 0) & (cols - 1)
    length = h.shape[0]
    left = jnp.where(col == 0, h, pltpu.roll(h, 1, 0))
    right = jnp.where(col == cols - 1, h, pltpu.roll(h, length - 1, 0))
    return left, right


def block_kernel(
    sizes,
    feat, gain1_hbm, shift1_hbm, w1, bias1_hbm, wskip, gain2_hbm, shift2_hbm, w2, bias2_hbm,
    out,
    gain1, shift1, bias1, gain2, shift2, bias2, featv, xall, w1v, wsv, wcat, xp1, xp2,
    acc, part1, send1, recv1, sum1, send1b, recv1b, stat0, other0, statg, stat2,
    mids, midbf, prevbf, scut, part2, send2, recv2, sum2, send2b, recv2b,
    w_sem, p_sem, own_sem, fs_sem, fr_sem, fps_sem, fpr_sem,
    s1s_sem, s1r_sem, sgs_sem, sgr_sem, s2s_sem, s2r_sem,
    r1s_sem, r1r_sem, r1bs_sem, r1br_sem, r2s_sem, r2r_sem, r2bs_sem, r2br_sem,
    ps_sem, pr_sem,
):
    slabs, nrow, ncol, rows, cols, per1, per2 = sizes
    n = nrow * ncol
    height, width = nrow * rows, ncol * cols
    area = height * width
    t = lax.axis_index("tm")
    r = lax.axis_index("row")
    c = lax.axis_index("col")
    me = r * ncol + c

    def place(i):
        return lax.div(i, ncol), lax.rem(i, ncol)

    def ident(ti, i):
        ri, ci = place(i)
        return {"tm": ti, "row": ri, "col": ci}

    def member(delta):
        return lax.rem(r + delta // ncol, nrow) * ncol + lax.rem(c + delta % ncol, ncol)

    def slab(delta):
        return lax.rem(t + delta, slabs)

    bits = [1 << k for k in range(slabs.bit_length() - 1)]

    def across(bit):
        return t + bit - 2 * bit * lax.rem(lax.div(t, bit), 2)

    loads = [
        pltpu.make_async_copy(w1, w1v, w_sem.at[0]),
        pltpu.make_async_copy(wskip, wsv, w_sem.at[1]),
    ]
    for i, (f, p, place_in, dt) in enumerate(
        ((0, 0, 0, 0), (0, 0, 1, 1), (0, 1, 0, 2), (1, 0, 1, 0), (1, 1, 0, 1), (1, 1, 1, 2))
    ):
        lo = place_in * per2
        loads.append(
            pltpu.make_async_copy(
                w2.at[dt], wcat.at[f, p, :, lo : lo + per2, :], w_sem.at[2 + i]
            )
        )
    params = [
        pltpu.make_async_copy(source, target, p_sem.at[i])
        for i, (source, target) in enumerate(
            (
                (gain1_hbm, gain1), (shift1_hbm, shift1), (bias1_hbm, bias1),
                (gain2_hbm, gain2), (shift2_hbm, shift2), (bias2_hbm, bias2),
            )
        )
    ]

    def window(frame0, i):
        ri, ci = place(i)
        top = ri * rows
        left = pl.multiple_of(ci * cols, cols)
        return xall.at[frame0 : frame0 + 2, pl.ds(top, rows), pl.ds(left, cols), :]

    def chunk(i):
        return feat.at[:, :, :, pl.ds(pl.multiple_of(i * LANES, LANES), LANES)]

    whole = pltpu.make_async_copy(feat, featv, own_sem.at[1])
    whole.start()
    own = pltpu.make_async_copy(chunk(me), window(2, me), own_sem.at[0])
    own.start()

    barrier = pltpu.get_barrier_semaphore()
    for delta in range(1, n):
        pl.semaphore_signal(barrier, inc=1, device_id=ident(t, member(delta)), device_id_type=MESH)
    for bit in bits:
        pl.semaphore_signal(barrier, inc=1, device_id=ident(across(bit), me), device_id_type=MESH)

    @pl.when(t > 0)
    def _():
        for delta in range(n):
            pl.semaphore_signal(
                barrier, inc=1, device_id=ident(t - 1, member(delta)), device_id_type=MESH
            )

    for load in params + loads:
        load.start()
    blank = jnp.zeros((9, per2, wcat.shape[4]), wcat.dtype)
    wcat[0, 1, :, per2:, :] = blank
    wcat[1, 0, :, :per2, :] = blank

    row8 = lax.broadcasted_iota(jnp.int32, (2 * n, LANES), 0)
    spots = float(2 * rows * cols)
    whole.wait()
    x = featv[...].reshape(2 * rows * cols, n * LANES).astype(jnp.float32)
    lane_mean = jnp.sum(x, axis=0, keepdims=True) * (1.0 / spots)
    lane_spread = jnp.sum((x - lane_mean) ** 2, axis=0, keepdims=True)
    tile = jnp.zeros((2 * n, LANES), jnp.float32)
    for d in range(n):
        at = slice(d * LANES, (d + 1) * LANES)
        tile = jnp.where(row8 == d, lane_mean[:, at], tile)
        tile = jnp.where(row8 == n + d, lane_spread[:, at], tile)
    stat0[0] = tile

    pl.semaphore_wait(barrier, jnp.where(t < slabs - 1, 2 * n - 1, n - 1) + len(bits))

    def stat_copy(buf, source, target, ssem, rsem):
        return pltpu.make_async_remote_copy(
            src_ref=buf.at[source], dst_ref=buf.at[source],
            send_sem=ssem.at[target], recv_sem=rsem.at[source],
            device_id=ident(target, me), device_id_type=MESH,
        )

    def share_copy(source, target):
        return pltpu.make_async_remote_copy(
            src_ref=statg.at[source], dst_ref=statg.at[source],
            send_sem=sgs_sem.at[target], recv_sem=sgr_sem.at[source],
            device_id=ident(t, target), device_id_type=MESH,
        )

    def swap_copy(k):
        return pltpu.make_async_remote_copy(
            src_ref=stat0.at[k], dst_ref=other0.at[k],
            send_sem=s1s_sem.at[k], recv_sem=s1r_sem.at[k],
            device_id=ident(across(bits[k]), me), device_id_type=MESH,
        )

    def swap(k):
        swap_copy(k).wait_recv()
        mine, theirs = stat0[k], other0[k]
        off = (mine - theirs) ** 2 * (spots * bits[k] * 0.5)
        total = mine + theirs
        joined = jnp.where(row8 < n, 0.5 * total, total + pltpu.roll(off, n, 0))
        if k + 1 < len(bits):
            stat0[k + 1] = joined
            swap_copy(k + 1).start()
        else:
            statg[me] = joined

    swap_copy(0).start()

    def feat_copy(source, target):
        return pltpu.make_async_remote_copy(
            src_ref=chunk(target), dst_ref=window(2, source),
            send_sem=fs_sem.at[target], recv_sem=fr_sem.at[source],
            device_id=ident(t, target), device_id_type=MESH,
        )

    def feat_next(source, target, to):
        return pltpu.make_async_remote_copy(
            src_ref=chunk(target), dst_ref=window(0, source),
            send_sem=fps_sem.at[target], recv_sem=fpr_sem.at[source],
            device_id=ident(to, target), device_id_type=MESH,
        )

    for delta in reversed(range(1, n)):
        feat_copy(me, member(delta)).start()

    swap(0)

    @pl.when(t < slabs - 1)
    def _():
        for delta in reversed(range(n)):
            feat_next(me, member(delta), t + 1).start()

    lane = lane_of((8, LANES))
    lane_in = lax.broadcasted_iota(jnp.int32, (LANES, LANES), 0)
    lane_to = lane_of((LANES, LANES))
    size1 = per1 // (GROUPS // n)
    size2 = per2 // (GROUPS // n)
    same1 = (lane_in // size1 == lane_to // size1).astype(jnp.float32)
    same2 = ((lane_in % per2) // size2 == (lane_to % per2) // size2).astype(jnp.float32)

    def own_full(ref):
        result = ref[0:1, 0:LANES]
        for d in range(1, n):
            result = jnp.where(me == d, ref[0:1, d * LANES : (d + 1) * LANES], result)
        return result

    def own_twice(ref):
        result = jnp.zeros((8, LANES), jnp.float32)
        for d in range(n):
            k = d // 2 * LANES
            seg = jnp.broadcast_to(ref[0:1, k : k + LANES], (8, LANES))
            turned = pltpu.roll(seg, per2, 1)
            twice = jnp.where((lane < per2) == (d % 2 == 0), seg, turned)
            result = jnp.where(me == d, twice, result)
        return result[0:1]

    for load in params:
        load.wait()
    g1, b1 = own_full(gain1), own_full(shift1)
    g2, b2, c1 = own_twice(gain2), own_twice(shift2), own_twice(bias1)

    for k in range(1, len(bits)):
        swap(k)
    for delta in reversed(range(1, n)):
        share_copy(me, member(delta)).start()

    own.wait()
    for delta in range(1, n):
        feat_copy(member(delta), me).wait_recv()
    loads[1].wait()
    for f in range(2):
        x = xall[2 + f].reshape(area, LANES)
        scut[f] = jnp.dot(x, wsv[...], preferred_element_type=jnp.float32)

    for delta in range(1, n):
        share_copy(member(delta), me).wait_recv()
    stats = statg[...]
    pick = lax.broadcasted_iota(jnp.int32, stats.shape, 1)
    means = jnp.sum(jnp.where(pick == me, stats, 0.0), axis=1, keepdims=True)
    spreads = jnp.sum(jnp.where(pick == n + me, stats, 0.0), axis=1, keepdims=True)
    mean, inv = group_stats(means, spreads, same1, size1, spots * slabs)
    scale = inv * g1

    def normalise(f):
        x = xall[f].reshape(area, LANES).astype(jnp.float32)
        h = silu((x - mean) * scale + b1)
        left, right = side_shifts(h, width)
        for dx, part in enumerate((left, h, right)):
            part = part.astype(jnp.bfloat16).reshape(height, width, LANES)
            lanes = slice(dx * LANES, (dx + 1) * LANES)
            xp1[f, 1 : height + 1, :, lanes] = part
            xp1[f, 0, :, lanes] = part[0]
            xp1[f, height + 1, :, lanes] = part[height - 1]

    depth = 9 * LANES
    tall = height // 2
    half = tall * width

    def conv1(dt, s):
        rows_in = [xp1[dt : dt + 2, s * tall + dy : (s + 1) * tall + dy] for dy in range(3)]
        lhs = jnp.concatenate([x.reshape(2 * half, 3 * LANES) for x in rows_in], axis=1)
        rhs = w1v[dt * depth : (dt + 1) * depth, :]
        return jnp.dot(lhs, rhs, preferred_element_type=jnp.float32)

    normalise(2)
    normalise(3)
    loads[0].wait()
    for s in range(2):
        acc[s] = conv1(2, s)

    @pl.when(t > 0)
    def _():
        for delta in range(n):
            feat_next(member(delta), me, t).wait_recv()

    @pl.when(t == 0)
    def _():
        xall[0] = xall[2]
        xall[1] = xall[2]

    normalise(0)
    normalise(1)

    def core_copy(src, dst, source, target, s, ssem, rsem):
        return pltpu.make_async_remote_copy(
            src_ref=src.at[s, target], dst_ref=dst.at[s, source],
            send_sem=ssem.at[s, target], recv_sem=rsem.at[s, source],
            device_id={"tm": t, "row": r, "col": target}, device_id_type=MESH,
        )

    def row_copy(src, dst, source, target, s, ssem, rsem):
        return pltpu.make_async_remote_copy(
            src_ref=src.at[s, target], dst_ref=dst.at[s, source],
            send_sem=ssem.at[s, target], recv_sem=rsem.at[s, source],
            device_id={"tm": t, "row": target, "col": c}, device_id_type=MESH,
        )

    cores = [lax.rem(c + delta, ncol) for delta in range(1, ncol)]
    others = [lax.rem(r + delta, nrow) for delta in range(1, nrow)]

    def to_cores(stage, s):
        send, recv, ssem, rsem = stage
        for core in cores:
            core_copy(send, recv, c, core, s, ssem, rsem).start()

    def to_rows(stage, part, total, stage_b, s):
        send, recv, ssem, rsem = stage
        send_b, recv_b, ssem_b, rsem_b = stage_b
        summed = part[s, c]
        for core in cores:
            core_copy(send, recv, core, c, s, ssem, rsem).wait_recv()
            summed = summed + recv[s, core].astype(jnp.float32)
        total[s] = summed
        send_b[s] = summed.astype(jnp.bfloat16)
        for other in others:
            row_copy(send_b, recv_b, r, other, s, ssem_b, rsem_b).start()

    def from_rows(total, stage_b, s):
        send_b, recv_b, ssem_b, rsem_b = stage_b
        result = total[s, r]
        for other in others:
            row_copy(send_b, recv_b, other, r, s, ssem_b, rsem_b).wait_recv()
            result = result + recv_b[s, other].astype(jnp.float32)
        return result

    def sent_to_cores(stage):
        send, recv, ssem, rsem = stage
        for s in range(2):
            for core in cores:
                core_copy(send, recv, c, core, s, ssem, rsem).wait_send()

    def sent_to_rows(stage):
        send, recv, ssem, rsem = stage
        for s in range(2):
            for other in others:
                row_copy(send, recv, r, other, s, ssem, rsem).wait_send()

    first = (send1, recv1, r1s_sem, r1r_sem)
    first_b = (send1b, recv1b, r1bs_sem, r1br_sem)
    second = (send2, recv2, r2s_sem, r2r_sem)
    second_b = (send2b, recv2b, r2bs_sem, r2br_sem)

    wide = lane_of((half, LANES))
    for s in range(2):
        total = acc[s] + conv1(1, s) + conv1(0, s)
        for d in range(n):
            k = d // 2 * LANES
            one, two = total[:half, k : k + LANES], total[half:, k : k + LANES]
            if d % 2 == 0:
                packed = jnp.where(wide < per2, one, pltpu.roll(two, per2, 1))
            else:
                packed = jnp.where(wide < per2, pltpu.roll(one, per2, 1), two)
            part1[s, d % ncol, d // ncol] = packed
            send1[s, d % ncol, d // ncol] = packed.astype(jnp.bfloat16)
        to_cores(first, s)
    for s in range(2):
        to_rows(first, part1, sum1, first_b, s)

    for delta in range(1, n):
        feat_copy(me, member(delta)).wait_send()
        share_copy(me, member(delta)).wait_send()
    for k in range(len(bits)):
        swap_copy(k).wait_send()

    @pl.when(t < slabs - 1)
    def _():
        for delta in range(n):
            feat_next(me, member(delta), t + 1).wait_send()

    def mid_copy(to, s):
        return pltpu.make_async_remote_copy(
            src_ref=midbf.at[s], dst_ref=prevbf.at[s],
            send_sem=ps_sem.at[s], recv_sem=pr_sem.at[s],
            device_id=ident(to, me), device_id_type=MESH,
        )

    def pass_on(s):
        @pl.when(t < slabs - 1)
        def _():
            mid_copy(t + 1, s).start()

    for s in range(2):
        middle = from_rows(sum1, first_b, s) + c1
        midbf[s] = middle.astype(jnp.bfloat16)
        mids[1, s] = middle
        if s == 0:
            pass_on(0)

    stat2[t] = lane_stats(mids[1].reshape(area, LANES))
    for delta in reversed(range(1, slabs)):
        stat_copy(stat2, t, slab(delta), s2s_sem, s2r_sem).start()
    pass_on(1)

    for delta in range(1, slabs):
        stat_copy(stat2, slab(delta), t, s2s_sem, s2r_sem).wait_recv()
    sent_to_cores(first)
    sent_to_rows(first_b)
    stats = stat2[...]
    mean, inv = group_stats(stats[:, 0:1], stats[:, 1:2], same2, 2 * size2, float(area))
    scale = inv * g2

    def normalise_mid(i):
        h = silu((mids[i].reshape(area, LANES) - mean) * scale + b2)
        left, right = side_shifts(h, width)
        for dx, part in enumerate((left, h, right)):
            part = part.astype(jnp.bfloat16).reshape(height, width, LANES)
            lanes = slice(dx * LANES, (dx + 1) * LANES)
            xp2[i, 1 : height + 1, :, lanes] = part
            xp2[i, 0, :, lanes] = part[0]
            xp2[i, height + 1, :, lanes] = part[height - 1]

    def conv2(f, i):
        rows_in = [xp2[i, dy : dy + height].reshape(area, 3 * LANES) for dy in range(3)]
        rhs = wcat[f, i].reshape(9 * LANES, wcat.shape[4])
        return jnp.dot(
            jnp.concatenate(rows_in, axis=1), rhs, preferred_element_type=jnp.float32
        )

    normalise_mid(1)
    for load in loads[2:]:
        load.wait()
    for f in range(2):
        scut[f] = scut[f] + conv2(f, 1)

    @pl.when(t > 0)
    def _():
        for s in range(2):
            mid_copy(t, s).wait_recv()
            mids[0, s] = prevbf[s].astype(jnp.float32)

    @pl.when(t == 0)
    def _():
        for s in range(2):
            middle = mids[1, s]
            mids[0, s] = jnp.where(wide < per2, middle, pltpu.roll(middle, per2, 1))

    normalise_mid(0)
    for f in range(2):
        total = (scut[f] + conv2(f, 0)).reshape(nrow, rows, width, wcat.shape[4])
        for ci in range(ncol):
            piece = total[:, :, ci * cols : (ci + 1) * cols]
            part2[f, ci] = piece
            send2[f, ci] = piece.astype(jnp.bfloat16)
        to_cores(second, f)
    for f in range(2):
        to_rows(second, part2, sum2, second_b, f)
    for delta in range(1, slabs):
        stat_copy(stat2, t, slab(delta), s2s_sem, s2r_sem).wait_send()

    @pl.when(t < slabs - 1)
    def _():
        for s in range(2):
            mid_copy(t + 1, s).wait_send()

    sent_to_cores(second)
    last = bias2[...].reshape(1, 1, -1)
    for f in range(2):
        out[f] = (from_rows(sum2, second_b, f) + last).astype(out.dtype)

    sent_to_rows(second_b)


def per_device(
    features,
    gn1_gain,
    gn1_bias,
    conv1_weight,
    conv1_bias,
    skip_weight,
    gn2_gain,
    gn2_bias,
    conv2_weight,
    conv2_bias,
):
    frames, rows, cols, chans_in = features.shape
    per1, per2 = conv1_weight.shape[1], conv2_weight.shape[1]
    chans_out = conv1_weight.shape[2]
    slabs, nrow, ncol = (lax.axis_size(a) for a in ("tm", "row", "col"))
    n = nrow * ncol
    height, width = nrow * rows, ncol * cols
    area = height * width
    fits = frames == 2 and per1 == LANES and 2 * per2 == LANES and cols % 16 == 0
    fits = fits and n == 4 and slabs & (slabs - 1) == 0 and width & (width - 1) == 0 and GROUPS % n == 0 and height % 2 == 0
    if not fits:
        return per_device_gathered(
            features, gn1_gain, gn1_bias, conv1_weight, conv1_bias, skip_weight,
            gn2_gain, gn2_bias, conv2_weight, conv2_bias,
        )
    bf16, f32 = jnp.bfloat16, jnp.float32
    vmem, dma = pltpu.VMEM, pltpu.SemaphoreType.DMA
    half = area // 2
    scratch = [
        vmem((1, chans_in), f32),
        vmem((1, chans_in), f32),
        vmem((1, chans_out), f32),
        vmem((1, chans_out), f32),
        vmem((1, chans_out), f32),
        vmem((1, chans_out), f32),
        vmem((frames, rows, cols, chans_in), bf16),
        vmem((4, height, width, LANES), bf16),
        vmem((27 * per1, chans_out), bf16),
        vmem((per1, chans_out), bf16),
        vmem((2, 2, 9, 2 * per2, chans_out), bf16),
        vmem((4, height + 2, width, 3 * LANES), bf16),
        vmem((2, height + 2, width, 3 * LANES), bf16),
        vmem((2, area, chans_out), f32),
        vmem((2, ncol, nrow, half, LANES), f32),
        vmem((2, ncol, nrow, half, LANES), bf16),
        vmem((2, ncol, nrow, half, LANES), bf16),
        vmem((2, nrow, half, LANES), f32),
        vmem((2, nrow, half, LANES), bf16),
        vmem((2, nrow, half, LANES), bf16),
        vmem((slabs, 2 * n, LANES), f32),
        vmem((slabs, 2 * n, LANES), f32),
        vmem((n, 2 * n, LANES), f32),
        vmem((slabs, 8, LANES), f32),
        vmem((2, 2, half, LANES), f32),
        vmem((2, half, LANES), bf16),
        vmem((2, half, LANES), bf16),
        vmem((2, area, chans_out), f32),
        vmem((2, ncol, nrow, rows, cols, chans_out), f32),
        vmem((2, ncol, nrow, rows, cols, chans_out), bf16),
        vmem((2, ncol, nrow, rows, cols, chans_out), bf16),
        vmem((2, nrow, rows, cols, chans_out), f32),
        vmem((2, nrow, rows, cols, chans_out), bf16),
        vmem((2, nrow, rows, cols, chans_out), bf16),
        dma((8,)), dma((6,)), dma((2,)), dma((n,)), dma((n,)), dma((n,)), dma((n,)),
        dma((slabs,)), dma((slabs,)), dma((n,)), dma((n,)), dma((slabs,)), dma((slabs,)),
        dma((2, ncol)), dma((2, ncol)), dma((2, nrow)), dma((2, nrow)),
        dma((2, ncol)), dma((2, ncol)), dma((2, nrow)), dma((2, nrow)),
        dma((2,)), dma((2,)),
    ]
    stays = pl.BlockSpec(memory_space=pltpu.HBM)
    inside = pl.BlockSpec(memory_space=pltpu.VMEM)
    sizes = (slabs, nrow, ncol, rows, cols, per1, per2)
    flops = 2 * 2 * area * chans_out * (28 * per1 + 27 * per2)
    return pl.pallas_call(
        functools.partial(block_kernel, sizes),
        out_shape=jax.ShapeDtypeStruct((frames, rows, cols, chans_out), bf16),
        in_specs=[stays] * 10,
        out_specs=inside,
        scratch_shapes=scratch,
        compiler_params=pltpu.CompilerParams(
            collective_id=0, has_side_effects=True, vmem_limit_bytes=64 * 1024 * 1024
        ),
        cost_estimate=pl.CostEstimate(
            flops=flops, bytes_accessed=4 * 1024 * 1024, transcendentals=6 * area * LANES
        ),
        name="residual_block",
    )(
        features,
        gn1_gain.reshape(1, -1),
        gn1_bias.reshape(1, -1),
        conv1_weight.reshape(27 * per1, chans_out),
        conv1_bias.reshape(1, -1),
        skip_weight.reshape(per1, chans_out),
        gn2_gain.reshape(1, -1),
        gn2_bias.reshape(1, -1),
        conv2_weight.reshape(3, 9, per2, chans_out),
        conv2_bias.reshape(1, -1),
    )


def solution(mesh):
    in_specs = (
        P("tm", "row", "col", None),
        P(),
        P(),
        P(None, ("row", "col"), None),
        P(),
        P(None, ("row", "col"), None),
        P(),
        P(),
        P(None, ("row", "col"), None),
        P(),
    )
    out_specs = P("tm", "row", "col", None)
    return jax.shard_map(
        per_device, mesh=mesh, in_specs=in_specs, out_specs=out_specs, check_vma=False
    )
```

```python
import functools

import jax
import jax.numpy as jnp
from jax import lax
from jax.experimental import pallas as pl
from jax.experimental.pallas import tpu as pltpu
from jax.sharding import PartitionSpec as P

GROUPS = 32


def passed_along(block, axis, distance):
    devices = range(lax.axis_size(axis))
    route = [(i - distance, i) for i in devices if i - distance in devices]
    return lax.ppermute(block, axis, route)


def with_halo(array, sides, width):
    for axis, dim in sides:
        size, length = (lax.axis_size(axis), array.shape[dim])
        up = [(i, (i + 1) % size) for i in range(size - 1)]
        down = [(j, i) for i, j in up]
        last = lax.slice_in_dim(array, length - width, length, axis=dim)
        leading = lax.slice_in_dim(array, 0, width, axis=dim)
        before = lax.ppermute(last, axis, up)
        after = lax.ppermute(leading, axis, down)
        array = jnp.concatenate([before, array, after], axis=dim)
    return array


def group_silu(values, gain, shift, groups, total_rows):
    chans = values.shape[-1]
    per_group = chans // groups
    grouped = values.reshape(-1, groups, per_group)
    count = float(total_rows * per_group)
    mean = lax.psum(jnp.sum(grouped, axis=(0, 2)), ("tm", "row", "col")) / count
    centred = grouped - mean[None, :, None]
    spread = lax.psum(jnp.sum(centred * centred, axis=(0, 2)), ("tm", "row", "col")) / count
    normed = (grouped - mean[None, :, None]) * lax.rsqrt(spread + 1e-06)[None, :, None]
    normed = normed.reshape(values.shape) * gain + shift
    return jax.nn.silu(normed).astype(jnp.bfloat16)


def conv_taps(padded, weight, frames, rows, cols):
    chans = padded.shape[3]
    total = jnp.zeros((frames * rows * cols, weight.shape[2]), jnp.float32)
    for dt in range(3):
        pieces = []
        for tap in range(9):
            dy, dx = (tap // 3, tap % 3)
            pieces.append(
                padded[dt : dt + frames, dy : dy + rows, dx : dx + cols].reshape(-1, chans)
            )
        stacked = jnp.concatenate(pieces, axis=1)
        flat_weight = weight[9 * dt : 9 * dt + 9].reshape(9 * chans, weight.shape[2])
        total = total + jnp.dot(stacked, flat_weight, preferred_element_type=jnp.float32)
    return total


def time_edge(earlier, volume):
    first_twice = jnp.concatenate([volume[:1], volume[:1]], axis=0)
    earlier = jnp.where(lax.axis_index("tm") == 0, first_twice, earlier)
    return jnp.concatenate([earlier, volume], axis=0)


def edge_rows(padded):
    place = lax.axis_index("row")
    last = lax.axis_size("row") - 1
    top = jnp.where(place == 0, padded[:, 1:2], padded[:, 0:1])
    bottom = jnp.where(place == last, padded[:, -2:-1], padded[:, -1:])
    return jnp.concatenate([top, padded[:, 1:-1], bottom], axis=1)


def edge_cols(padded):
    place = lax.axis_index("col")
    last = lax.axis_size("col") - 1
    left = jnp.where(place == 0, padded[:, :, 1:2], padded[:, :, 0:1])
    right = jnp.where(place == last, padded[:, :, -2:-1], padded[:, :, -1:])
    return jnp.concatenate([left, padded[:, :, 1:-1], right], axis=2)


def per_device_gathered(
    features,
    gn1_gain,
    gn1_bias,
    conv1_weight,
    conv1_bias,
    skip_weight,
    gn2_gain,
    gn2_bias,
    conv2_weight,
    conv2_bias,
):
    frames, rows, cols, chans_in = features.shape
    chans_out = conv1_weight.shape[2]
    groups = GROUPS
    nrow = lax.axis_size("row")
    ncol = lax.axis_size("col")
    total_rows = lax.axis_size("tm") * nrow * ncol * frames * rows * cols
    flat_features = features.reshape(-1, chans_in)
    hidden1 = group_silu(features.astype(jnp.float32), gn1_gain, gn1_bias, groups, total_rows)
    earlier = passed_along(hidden1, "tm", 1)
    extended = time_edge(earlier, hidden1)
    padded = with_halo(extended, (("row", 1), ("col", 2)), 1)
    padded = edge_cols(edge_rows(padded))
    window = padded
    first = conv_taps(
        window, lax.all_gather(conv1_weight, ("row", "col"), axis=1, tiled=True), frames, rows, cols
    )
    second = jnp.dot(
        flat_features,
        lax.all_gather(skip_weight, ("row", "col"), axis=1, tiled=True)[0],
        preferred_element_type=jnp.float32,
    )
    middle = (first + conv1_bias).reshape(frames, rows, cols, chans_out)
    hidden2 = group_silu(middle, gn2_gain, gn2_bias, groups, total_rows)
    earlier_mid = passed_along(hidden2, "tm", 1)
    extended_mid = time_edge(earlier_mid, hidden2)
    padded_mid = with_halo(extended_mid, (("row", 1), ("col", 2)), 1)
    padded_mid = edge_cols(edge_rows(padded_mid))
    window = padded_mid
    conv_second = conv_taps(
        window, lax.all_gather(conv2_weight, ("row", "col"), axis=1, tiled=True), frames, rows, cols
    )
    block_out = (second + conv_second + conv2_bias).astype(jnp.bfloat16)
    return block_out.reshape(frames, rows, cols, chans_out)


MESH = pl.DeviceIdType.MESH
LANES = 128


def lane_of(shape):
    return lax.broadcasted_iota(jnp.int32, shape, len(shape) - 1)


def silu(a):
    half = 0.5 * a
    return half + half * jnp.tanh(half)


def lane_stats(x):
    mean = jnp.sum(x, axis=0, keepdims=True) * (1.0 / x.shape[0])
    spread = jnp.sum((x - mean) ** 2, axis=0, keepdims=True)
    row = lax.broadcasted_iota(jnp.int32, (8, LANES), 0)
    return jnp.where(row == 0, mean, jnp.where(row == 1, spread, 0.0))


def group_stats(means, spreads, same, lanes, count):
    parts = means.shape[0]
    mean = jnp.sum(means, axis=0) * (1.0 / parts)
    spread = jnp.sum(spreads, axis=0) + count * jnp.sum((means - mean[None]) ** 2, axis=0)
    mean = jnp.broadcast_to(mean, (8, LANES))
    group_mean = (
        jnp.dot(mean, same, precision=lax.Precision.HIGHEST, preferred_element_type=jnp.float32)
        * (1.0 / lanes)
    )
    spread = spread + (count * parts) * (mean - group_mean) ** 2
    total = jnp.dot(
        spread, same, precision=lax.Precision.HIGHEST, preferred_element_type=jnp.float32
    )
    inv = lax.rsqrt(total * (1.0 / (count * parts * lanes)) + 1e-6)
    return group_mean[0:1], inv[0:1]


def side_shifts(h, cols):
    col = lax.broadcasted_iota(jnp.int32, h.shape, 0) & (cols - 1)
    length = h.shape[0]
    left = jnp.where(col == 0, h, pltpu.roll(h, 1, 0))
    right = jnp.where(col == cols - 1, h, pltpu.roll(h, length - 1, 0))
    return left, right


def block_kernel(
    sizes,
    feat, gain1_hbm, shift1_hbm, w1, bias1_hbm, wskip, gain2_hbm, shift2_hbm, w2, bias2_hbm,
    out,
    gain1, shift1, bias1, gain2, shift2, bias2, featv, xall, w1v, wsv, wcat, xp1, xp2,
    acc, part1, send1, recv1, sum1, send1b, recv1b, stat0, stat2,
    mids, midbf, prevbf, scut, part2, send2, recv2, sum2, send2b, recv2b,
    w_sem, p_sem, own_sem, fs_sem, fr_sem, fps_sem, fpr_sem,
    s1s_sem, s1r_sem, s2s_sem, s2r_sem,
    r1s_sem, r1r_sem, r1bs_sem, r1br_sem, r2s_sem, r2r_sem, r2bs_sem, r2br_sem,
    ps_sem, pr_sem,
):
    slabs, nrow, ncol, rows, cols, per1, per2 = sizes
    n = nrow * ncol
    height, width = nrow * rows, ncol * cols
    area = height * width
    t = lax.axis_index("tm")
    r = lax.axis_index("row")
    c = lax.axis_index("col")
    me = r * ncol + c

    def place(i):
        return lax.div(i, ncol), lax.rem(i, ncol)

    def ident(ti, i):
        ri, ci = place(i)
        return {"tm": ti, "row": ri, "col": ci}

    def member(delta):
        return lax.rem(r + delta // ncol, nrow) * ncol + lax.rem(c + delta % ncol, ncol)

    def slab(delta):
        return lax.rem(t + delta, slabs)

    everyone = [(dt, di) for dt in range(slabs) for di in range(n) if dt or di]

    loads = [
        pltpu.make_async_copy(w1, w1v, w_sem.at[0]),
        pltpu.make_async_copy(wskip, wsv, w_sem.at[1]),
    ]
    for i, (f, p, place_in, dt) in enumerate(
        ((0, 0, 0, 0), (0, 0, 1, 1), (0, 1, 0, 2), (1, 0, 1, 0), (1, 1, 0, 1), (1, 1, 1, 2))
    ):
        lo = place_in * per2
        loads.append(
            pltpu.make_async_copy(
                w2.at[dt], wcat.at[f, p, :, lo : lo + per2, :], w_sem.at[2 + i]
            )
        )
    params = [
        pltpu.make_async_copy(source, target, p_sem.at[i])
        for i, (source, target) in enumerate(
            (
                (gain1_hbm, gain1), (shift1_hbm, shift1), (bias1_hbm, bias1),
                (gain2_hbm, gain2), (shift2_hbm, shift2), (bias2_hbm, bias2),
            )
        )
    ]

    def window(frame0, i):
        ri, ci = place(i)
        top = ri * rows
        left = pl.multiple_of(ci * cols, cols)
        return xall.at[frame0 : frame0 + 2, pl.ds(top, rows), pl.ds(left, cols), :]

    def chunk(i):
        return feat.at[:, :, :, pl.ds(pl.multiple_of(i * LANES, LANES), LANES)]

    whole = pltpu.make_async_copy(feat, featv, own_sem.at[1])
    whole.start()
    own = pltpu.make_async_copy(chunk(me), window(2, me), own_sem.at[0])
    own.start()

    barrier = pltpu.get_barrier_semaphore()
    for dt, di in everyone:
        pl.semaphore_signal(
            barrier, inc=1, device_id=ident(slab(dt), member(di)), device_id_type=MESH
        )
    for load in params + loads:
        load.start()
    blank = jnp.zeros((9, per2, wcat.shape[4]), wcat.dtype)
    wcat[0, 1, :, per2:, :] = blank
    wcat[1, 0, :, :per2, :] = blank

    row8 = lax.broadcasted_iota(jnp.int32, (2 * n, LANES), 0)
    spots = float(2 * rows * cols)
    whole.wait()
    x = featv[...].reshape(2 * rows * cols, n * LANES).astype(jnp.float32)
    lane_mean = jnp.sum(x, axis=0, keepdims=True) * (1.0 / spots)
    lane_spread = jnp.sum((x - lane_mean) ** 2, axis=0, keepdims=True)
    tile = jnp.zeros((2 * n, LANES), jnp.float32)
    for d in range(n):
        at = slice(d * LANES, (d + 1) * LANES)
        tile = jnp.where(row8 == d, lane_mean[:, at], tile)
        tile = jnp.where(row8 == n + d, lane_spread[:, at], tile)
    here = t * n + me
    stat0[here] = tile

    pl.semaphore_wait(barrier, len(everyone))

    def stat_copy(buf, source, target, ssem, rsem):
        return pltpu.make_async_remote_copy(
            src_ref=buf.at[source], dst_ref=buf.at[source],
            send_sem=ssem.at[target], recv_sem=rsem.at[source],
            device_id=ident(target, me), device_id_type=MESH,
        )

    def tile_copy(source, t_to, to):
        return pltpu.make_async_remote_copy(
            src_ref=stat0.at[source], dst_ref=stat0.at[source],
            send_sem=s1s_sem.at[t_to * n + to], recv_sem=s1r_sem.at[source],
            device_id=ident(t_to, to), device_id_type=MESH,
        )

    for dt, di in reversed(everyone):
        tile_copy(here, slab(dt), member(di)).start()

    def feat_copy(source, target):
        return pltpu.make_async_remote_copy(
            src_ref=chunk(target), dst_ref=window(2, source),
            send_sem=fs_sem.at[target], recv_sem=fr_sem.at[source],
            device_id=ident(t, target), device_id_type=MESH,
        )

    def feat_next(source, target, to):
        return pltpu.make_async_remote_copy(
            src_ref=chunk(target), dst_ref=window(0, source),
            send_sem=fps_sem.at[target], recv_sem=fpr_sem.at[source],
            device_id=ident(to, target), device_id_type=MESH,
        )

    for delta in reversed(range(1, n)):
        feat_copy(me, member(delta)).start()

    @pl.when(t < slabs - 1)
    def _():
        for delta in reversed(range(n)):
            feat_next(me, member(delta), t + 1).start()

    lane = lane_of((8, LANES))
    lane_in = lax.broadcasted_iota(jnp.int32, (LANES, LANES), 0)
    lane_to = lane_of((LANES, LANES))
    size1 = per1 // (GROUPS // n)
    size2 = per2 // (GROUPS // n)
    same1 = (lane_in // size1 == lane_to // size1).astype(jnp.float32)
    same2 = ((lane_in % per2) // size2 == (lane_to % per2) // size2).astype(jnp.float32)

    def own_full(ref):
        result = ref[0:1, 0:LANES]
        for d in range(1, n):
            result = jnp.where(me == d, ref[0:1, d * LANES : (d + 1) * LANES], result)
        return result

    def own_twice(ref):
        result = jnp.zeros((8, LANES), jnp.float32)
        for d in range(n):
            k = d // 2 * LANES
            seg = jnp.broadcast_to(ref[0:1, k : k + LANES], (8, LANES))
            turned = pltpu.roll(seg, per2, 1)
            twice = jnp.where((lane < per2) == (d % 2 == 0), seg, turned)
            result = jnp.where(me == d, twice, result)
        return result[0:1]

    for load in params:
        load.wait()
    g1, b1 = own_full(gain1), own_full(shift1)
    g2, b2, c1 = own_twice(gain2), own_twice(shift2), own_twice(bias1)

    own.wait()
    for delta in range(1, n):
        feat_copy(member(delta), me).wait_recv()
    loads[1].wait()
    for f in range(2):
        x = xall[2 + f].reshape(area, LANES)
        scut[f] = jnp.dot(x, wsv[...], preferred_element_type=jnp.float32)

    for dt, di in everyone:
        tile_copy(slab(dt) * n + member(di), t, me).wait_recv()
    stats = stat0[...]
    pick = lax.broadcasted_iota(jnp.int32, stats.shape, 1)
    means = jnp.sum(jnp.where(pick == me, stats, 0.0), axis=1, keepdims=True)
    spreads = jnp.sum(jnp.where(pick == n + me, stats, 0.0), axis=1, keepdims=True)
    mean, inv = group_stats(means, spreads, same1, size1, spots)
    scale = inv * g1

    def normalise(f):
        x = xall[f].reshape(area, LANES).astype(jnp.float32)
        h = silu((x - mean) * scale + b1)
        left, right = side_shifts(h, width)
        for dx, part in enumerate((left, h, right)):
            part = part.astype(jnp.bfloat16).reshape(height, width, LANES)
            lanes = slice(dx * LANES, (dx + 1) * LANES)
            xp1[f, 1 : height + 1, :, lanes] = part
            xp1[f, 0, :, lanes] = part[0]
            xp1[f, height + 1, :, lanes] = part[height - 1]

    depth = 9 * LANES
    tall = height // 2
    half = tall * width

    def conv1(dt, s):
        rows_in = [xp1[dt : dt + 2, s * tall + dy : (s + 1) * tall + dy] for dy in range(3)]
        lhs = jnp.concatenate([x.reshape(2 * half, 3 * LANES) for x in rows_in], axis=1)
        rhs = w1v[dt * depth : (dt + 1) * depth, :]
        return jnp.dot(lhs, rhs, preferred_element_type=jnp.float32)

    normalise(2)
    normalise(3)
    loads[0].wait()
    for s in range(2):
        acc[s] = conv1(2, s)

    @pl.when(t > 0)
    def _():
        for delta in range(n):
            feat_next(member(delta), me, t).wait_recv()

    @pl.when(t == 0)
    def _():
        xall[0] = xall[2]
        xall[1] = xall[2]

    normalise(0)
    normalise(1)

    def core_copy(src, dst, source, target, s, ssem, rsem):
        return pltpu.make_async_remote_copy(
            src_ref=src.at[s, target], dst_ref=dst.at[s, source],
            send_sem=ssem.at[s, target], recv_sem=rsem.at[s, source],
            device_id={"tm": t, "row": r, "col": target}, device_id_type=MESH,
        )

    def row_copy(src, dst, source, target, s, ssem, rsem):
        return pltpu.make_async_remote_copy(
            src_ref=src.at[s, target], dst_ref=dst.at[s, source],
            send_sem=ssem.at[s, target], recv_sem=rsem.at[s, source],
            device_id={"tm": t, "row": target, "col": c}, device_id_type=MESH,
        )

    cores = [lax.rem(c + delta, ncol) for delta in range(1, ncol)]
    others = [lax.rem(r + delta, nrow) for delta in range(1, nrow)]

    def to_cores(stage, s):
        send, recv, ssem, rsem = stage
        for core in cores:
            core_copy(send, recv, c, core, s, ssem, rsem).start()

    def to_rows(stage, part, total, stage_b, s):
        send, recv, ssem, rsem = stage
        send_b, recv_b, ssem_b, rsem_b = stage_b
        summed = part[s, c]
        for core in cores:
            core_copy(send, recv, core, c, s, ssem, rsem).wait_recv()
            summed = summed + recv[s, core].astype(jnp.float32)
        total[s] = summed
        send_b[s] = summed.astype(jnp.bfloat16)
        for other in others:
            row_copy(send_b, recv_b, r, other, s, ssem_b, rsem_b).start()

    def from_rows(total, stage_b, s):
        send_b, recv_b, ssem_b, rsem_b = stage_b
        result = total[s, r]
        for other in others:
            row_copy(send_b, recv_b, other, r, s, ssem_b, rsem_b).wait_recv()
            result = result + recv_b[s, other].astype(jnp.float32)
        return result

    def sent_to_cores(stage):
        send, recv, ssem, rsem = stage
        for s in range(2):
            for core in cores:
                core_copy(send, recv, c, core, s, ssem, rsem).wait_send()

    def sent_to_rows(stage):
        send, recv, ssem, rsem = stage
        for s in range(2):
            for other in others:
                row_copy(send, recv, r, other, s, ssem, rsem).wait_send()

    first = (send1, recv1, r1s_sem, r1r_sem)
    first_b = (send1b, recv1b, r1bs_sem, r1br_sem)
    second = (send2, recv2, r2s_sem, r2r_sem)
    second_b = (send2b, recv2b, r2bs_sem, r2br_sem)

    wide = lane_of((half, LANES))
    for s in range(2):
        total = acc[s] + conv1(1, s) + conv1(0, s)
        for d in range(n):
            k = d // 2 * LANES
            one, two = total[:half, k : k + LANES], total[half:, k : k + LANES]
            if d % 2 == 0:
                packed = jnp.where(wide < per2, one, pltpu.roll(two, per2, 1))
            else:
                packed = jnp.where(wide < per2, pltpu.roll(one, per2, 1), two)
            part1[s, d % ncol, d // ncol] = packed
            send1[s, d % ncol, d // ncol] = packed.astype(jnp.bfloat16)
        to_cores(first, s)
    for s in range(2):
        to_rows(first, part1, sum1, first_b, s)

    for delta in range(1, n):
        feat_copy(me, member(delta)).wait_send()
    for dt, di in everyone:
        tile_copy(here, slab(dt), member(di)).wait_send()

    @pl.when(t < slabs - 1)
    def _():
        for delta in range(n):
            feat_next(me, member(delta), t + 1).wait_send()

    def mid_copy(to, s):
        return pltpu.make_async_remote_copy(
            src_ref=midbf.at[s], dst_ref=prevbf.at[s],
            send_sem=ps_sem.at[s], recv_sem=pr_sem.at[s],
            device_id=ident(to, me), device_id_type=MESH,
        )

    def pass_on(s):
        @pl.when(t < slabs - 1)
        def _():
            mid_copy(t + 1, s).start()

    for s in range(2):
        middle = from_rows(sum1, first_b, s) + c1
        midbf[s] = middle.astype(jnp.bfloat16)
        mids[1, s] = middle
        if s == 0:
            pass_on(0)

    stat2[t] = lane_stats(mids[1].reshape(area, LANES))
    for delta in reversed(range(1, slabs)):
        stat_copy(stat2, t, slab(delta), s2s_sem, s2r_sem).start()
    pass_on(1)

    for delta in range(1, slabs):
        stat_copy(stat2, slab(delta), t, s2s_sem, s2r_sem).wait_recv()
    sent_to_cores(first)
    sent_to_rows(first_b)
    stats = stat2[...]
    mean, inv = group_stats(stats[:, 0:1], stats[:, 1:2], same2, 2 * size2, float(area))
    scale = inv * g2

    def normalise_mid(i):
        h = silu((mids[i].reshape(area, LANES) - mean) * scale + b2)
        left, right = side_shifts(h, width)
        for dx, part in enumerate((left, h, right)):
            part = part.astype(jnp.bfloat16).reshape(height, width, LANES)
            lanes = slice(dx * LANES, (dx + 1) * LANES)
            xp2[i, 1 : height + 1, :, lanes] = part
            xp2[i, 0, :, lanes] = part[0]
            xp2[i, height + 1, :, lanes] = part[height - 1]

    def conv2(f, i):
        rows_in = [xp2[i, dy : dy + height].reshape(area, 3 * LANES) for dy in range(3)]
        rhs = wcat[f, i].reshape(9 * LANES, wcat.shape[4])
        return jnp.dot(
            jnp.concatenate(rows_in, axis=1), rhs, preferred_element_type=jnp.float32
        )

    normalise_mid(1)
    for load in loads[2:]:
        load.wait()
    for f in range(2):
        scut[f] = scut[f] + conv2(f, 1)

    @pl.when(t > 0)
    def _():
        for s in range(2):
            mid_copy(t, s).wait_recv()
            mids[0, s] = prevbf[s].astype(jnp.float32)

    @pl.when(t == 0)
    def _():
        for s in range(2):
            middle = mids[1, s]
            mids[0, s] = jnp.where(wide < per2, middle, pltpu.roll(middle, per2, 1))

    normalise_mid(0)
    for f in range(2):
        total = (scut[f] + conv2(f, 0)).reshape(nrow, rows, width, wcat.shape[4])
        for ci in range(ncol):
            piece = total[:, :, ci * cols : (ci + 1) * cols]
            part2[f, ci] = piece
            send2[f, ci] = piece.astype(jnp.bfloat16)
        to_cores(second, f)
    for f in range(2):
        to_rows(second, part2, sum2, second_b, f)
    for delta in range(1, slabs):
        stat_copy(stat2, t, slab(delta), s2s_sem, s2r_sem).wait_send()

    @pl.when(t < slabs - 1)
    def _():
        for s in range(2):
            mid_copy(t + 1, s).wait_send()

    sent_to_cores(second)
    last = bias2[...].reshape(1, 1, -1)
    for f in range(2):
        out[f] = (from_rows(sum2, second_b, f) + last).astype(out.dtype)

    sent_to_rows(second_b)


def per_device(
    features,
    gn1_gain,
    gn1_bias,
    conv1_weight,
    conv1_bias,
    skip_weight,
    gn2_gain,
    gn2_bias,
    conv2_weight,
    conv2_bias,
):
    frames, rows, cols, chans_in = features.shape
    per1, per2 = conv1_weight.shape[1], conv2_weight.shape[1]
    chans_out = conv1_weight.shape[2]
    slabs, nrow, ncol = (lax.axis_size(a) for a in ("tm", "row", "col"))
    n = nrow * ncol
    height, width = nrow * rows, ncol * cols
    area = height * width
    fits = frames == 2 and per1 == LANES and 2 * per2 == LANES and cols % 16 == 0
    fits = fits and n == 4 and width & (width - 1) == 0 and GROUPS % n == 0 and height % 2 == 0
    if not fits:
        return per_device_gathered(
            features, gn1_gain, gn1_bias, conv1_weight, conv1_bias, skip_weight,
            gn2_gain, gn2_bias, conv2_weight, conv2_bias,
        )
    bf16, f32 = jnp.bfloat16, jnp.float32
    vmem, dma = pltpu.VMEM, pltpu.SemaphoreType.DMA
    half = area // 2
    scratch = [
        vmem((1, chans_in), f32),
        vmem((1, chans_in), f32),
        vmem((1, chans_out), f32),
        vmem((1, chans_out), f32),
        vmem((1, chans_out), f32),
        vmem((1, chans_out), f32),
        vmem((frames, rows, cols, chans_in), bf16),
        vmem((4, height, width, LANES), bf16),
        vmem((27 * per1, chans_out), bf16),
        vmem((per1, chans_out), bf16),
        vmem((2, 2, 9, 2 * per2, chans_out), bf16),
        vmem((4, height + 2, width, 3 * LANES), bf16),
        vmem((2, height + 2, width, 3 * LANES), bf16),
        vmem((2, area, chans_out), f32),
        vmem((2, ncol, nrow, half, LANES), f32),
        vmem((2, ncol, nrow, half, LANES), bf16),
        vmem((2, ncol, nrow, half, LANES), bf16),
        vmem((2, nrow, half, LANES), f32),
        vmem((2, nrow, half, LANES), bf16),
        vmem((2, nrow, half, LANES), bf16),
        vmem((slabs * n, 2 * n, LANES), f32),
        vmem((slabs, 8, LANES), f32),
        vmem((2, 2, half, LANES), f32),
        vmem((2, half, LANES), bf16),
        vmem((2, half, LANES), bf16),
        vmem((2, area, chans_out), f32),
        vmem((2, ncol, nrow, rows, cols, chans_out), f32),
        vmem((2, ncol, nrow, rows, cols, chans_out), bf16),
        vmem((2, ncol, nrow, rows, cols, chans_out), bf16),
        vmem((2, nrow, rows, cols, chans_out), f32),
        vmem((2, nrow, rows, cols, chans_out), bf16),
        vmem((2, nrow, rows, cols, chans_out), bf16),
        dma((8,)), dma((6,)), dma((2,)), dma((n,)), dma((n,)), dma((n,)), dma((n,)),
        dma((slabs * n,)), dma((slabs * n,)), dma((slabs,)), dma((slabs,)),
        dma((2, ncol)), dma((2, ncol)), dma((2, nrow)), dma((2, nrow)),
        dma((2, ncol)), dma((2, ncol)), dma((2, nrow)), dma((2, nrow)),
        dma((2,)), dma((2,)),
    ]
    stays = pl.BlockSpec(memory_space=pltpu.HBM)
    inside = pl.BlockSpec(memory_space=pltpu.VMEM)
    sizes = (slabs, nrow, ncol, rows, cols, per1, per2)
    flops = 2 * 2 * area * chans_out * (28 * per1 + 27 * per2)
    return pl.pallas_call(
        functools.partial(block_kernel, sizes),
        out_shape=jax.ShapeDtypeStruct((frames, rows, cols, chans_out), bf16),
        in_specs=[stays] * 10,
        out_specs=inside,
        scratch_shapes=scratch,
        compiler_params=pltpu.CompilerParams(
            collective_id=0, has_side_effects=True, vmem_limit_bytes=64 * 1024 * 1024
        ),
        cost_estimate=pl.CostEstimate(
            flops=flops, bytes_accessed=4 * 1024 * 1024, transcendentals=6 * area * LANES
        ),
        name="residual_block",
    )(
        features,
        gn1_gain.reshape(1, -1),
        gn1_bias.reshape(1, -1),
        conv1_weight.reshape(27 * per1, chans_out),
        conv1_bias.reshape(1, -1),
        skip_weight.reshape(per1, chans_out),
        gn2_gain.reshape(1, -1),
        gn2_bias.reshape(1, -1),
        conv2_weight.reshape(3, 9, per2, chans_out),
        conv2_bias.reshape(1, -1),
    )


def solution(mesh):
    in_specs = (
        P("tm", "row", "col", None),
        P(),
        P(),
        P(None, ("row", "col"), None),
        P(),
        P(None, ("row", "col"), None),
        P(),
        P(),
        P(None, ("row", "col"), None),
        P(),
    )
    out_specs = P("tm", "row", "col", None)
    return jax.shard_map(
        per_device, mesh=mesh, in_specs=in_specs, out_specs=out_specs, check_vma=False
    )
```

```python
import functools

import jax
import jax.numpy as jnp
from jax import lax
from jax.experimental import pallas as pl
from jax.experimental.pallas import tpu as pltpu
from jax.sharding import PartitionSpec as P

GROUPS = 32


def passed_along(block, axis, distance):
    devices = range(lax.axis_size(axis))
    route = [(i - distance, i) for i in devices if i - distance in devices]
    return lax.ppermute(block, axis, route)


def with_halo(array, sides, width):
    for axis, dim in sides:
        size, length = (lax.axis_size(axis), array.shape[dim])
        up = [(i, (i + 1) % size) for i in range(size - 1)]
        down = [(j, i) for i, j in up]
        last = lax.slice_in_dim(array, length - width, length, axis=dim)
        leading = lax.slice_in_dim(array, 0, width, axis=dim)
        before = lax.ppermute(last, axis, up)
        after = lax.ppermute(leading, axis, down)
        array = jnp.concatenate([before, array, after], axis=dim)
    return array


def group_silu(values, gain, shift, groups, total_rows):
    chans = values.shape[-1]
    per_group = chans // groups
    grouped = values.reshape(-1, groups, per_group)
    count = float(total_rows * per_group)
    mean = lax.psum(jnp.sum(grouped, axis=(0, 2)), ("tm", "row", "col")) / count
    centred = grouped - mean[None, :, None]
    spread = lax.psum(jnp.sum(centred * centred, axis=(0, 2)), ("tm", "row", "col")) / count
    normed = (grouped - mean[None, :, None]) * lax.rsqrt(spread + 1e-06)[None, :, None]
    normed = normed.reshape(values.shape) * gain + shift
    return jax.nn.silu(normed).astype(jnp.bfloat16)


def conv_taps(padded, weight, frames, rows, cols):
    chans = padded.shape[3]
    total = jnp.zeros((frames * rows * cols, weight.shape[2]), jnp.float32)
    for dt in range(3):
        pieces = []
        for tap in range(9):
            dy, dx = (tap // 3, tap % 3)
            pieces.append(
                padded[dt : dt + frames, dy : dy + rows, dx : dx + cols].reshape(-1, chans)
            )
        stacked = jnp.concatenate(pieces, axis=1)
        flat_weight = weight[9 * dt : 9 * dt + 9].reshape(9 * chans, weight.shape[2])
        total = total + jnp.dot(stacked, flat_weight, preferred_element_type=jnp.float32)
    return total


def time_edge(earlier, volume):
    first_twice = jnp.concatenate([volume[:1], volume[:1]], axis=0)
    earlier = jnp.where(lax.axis_index("tm") == 0, first_twice, earlier)
    return jnp.concatenate([earlier, volume], axis=0)


def edge_rows(padded):
    place = lax.axis_index("row")
    last = lax.axis_size("row") - 1
    top = jnp.where(place == 0, padded[:, 1:2], padded[:, 0:1])
    bottom = jnp.where(place == last, padded[:, -2:-1], padded[:, -1:])
    return jnp.concatenate([top, padded[:, 1:-1], bottom], axis=1)


def edge_cols(padded):
    place = lax.axis_index("col")
    last = lax.axis_size("col") - 1
    left = jnp.where(place == 0, padded[:, :, 1:2], padded[:, :, 0:1])
    right = jnp.where(place == last, padded[:, :, -2:-1], padded[:, :, -1:])
    return jnp.concatenate([left, padded[:, :, 1:-1], right], axis=2)


def per_device_gathered(
    features,
    gn1_gain,
    gn1_bias,
    conv1_weight,
    conv1_bias,
    skip_weight,
    gn2_gain,
    gn2_bias,
    conv2_weight,
    conv2_bias,
):
    frames, rows, cols, chans_in = features.shape
    chans_out = conv1_weight.shape[2]
    groups = GROUPS
    nrow = lax.axis_size("row")
    ncol = lax.axis_size("col")
    total_rows = lax.axis_size("tm") * nrow * ncol * frames * rows * cols
    flat_features = features.reshape(-1, chans_in)
    hidden1 = group_silu(features.astype(jnp.float32), gn1_gain, gn1_bias, groups, total_rows)
    earlier = passed_along(hidden1, "tm", 1)
    extended = time_edge(earlier, hidden1)
    padded = with_halo(extended, (("row", 1), ("col", 2)), 1)
    padded = edge_cols(edge_rows(padded))
    window = padded
    first = conv_taps(
        window, lax.all_gather(conv1_weight, ("row", "col"), axis=1, tiled=True), frames, rows, cols
    )
    second = jnp.dot(
        flat_features,
        lax.all_gather(skip_weight, ("row", "col"), axis=1, tiled=True)[0],
        preferred_element_type=jnp.float32,
    )
    middle = (first + conv1_bias).reshape(frames, rows, cols, chans_out)
    hidden2 = group_silu(middle, gn2_gain, gn2_bias, groups, total_rows)
    earlier_mid = passed_along(hidden2, "tm", 1)
    extended_mid = time_edge(earlier_mid, hidden2)
    padded_mid = with_halo(extended_mid, (("row", 1), ("col", 2)), 1)
    padded_mid = edge_cols(edge_rows(padded_mid))
    window = padded_mid
    conv_second = conv_taps(
        window, lax.all_gather(conv2_weight, ("row", "col"), axis=1, tiled=True), frames, rows, cols
    )
    block_out = (second + conv_second + conv2_bias).astype(jnp.bfloat16)
    return block_out.reshape(frames, rows, cols, chans_out)


MESH = pl.DeviceIdType.MESH
LANES = 128


def lane_of(shape):
    return lax.broadcasted_iota(jnp.int32, shape, len(shape) - 1)


def silu(a):
    half = 0.5 * a
    return half + half * jnp.tanh(half)


def lane_stats(x):
    mean = jnp.sum(x, axis=0, keepdims=True) * (1.0 / x.shape[0])
    spread = jnp.sum((x - mean) ** 2, axis=0, keepdims=True)
    row = lax.broadcasted_iota(jnp.int32, (8, LANES), 0)
    return jnp.where(row == 0, mean, jnp.where(row == 1, spread, 0.0))


def group_sums(x, same):
    high = x.astype(jnp.bfloat16).astype(jnp.float32)
    rest = x - high
    middle = rest.astype(jnp.bfloat16).astype(jnp.float32)
    row = lax.broadcasted_iota(jnp.int32, (16, LANES), 0)
    parts = jnp.where(row == 0, high, jnp.where(row == 1, middle, rest - middle))
    parts = jnp.where(row < 3, parts, 0.0).astype(jnp.bfloat16)
    sums = jnp.dot(parts, same, preferred_element_type=jnp.float32)
    return jnp.sum(sums, axis=0, keepdims=True)


def group_stats(means, spreads, same, lanes, count):
    parts = means.shape[0]
    mean = jnp.sum(means, axis=0) * (1.0 / parts)
    spread = jnp.sum(spreads, axis=0) + count * jnp.sum((means - mean[None]) ** 2, axis=0)
    group_mean = group_sums(mean, same) * (1.0 / lanes)
    spread = spread + (count * parts) * (mean - group_mean) ** 2
    total = group_sums(spread, same)
    return group_mean, lax.rsqrt(total * (1.0 / (count * parts * lanes)) + 1e-6)


def side_shifts(h, cols):
    col = lax.broadcasted_iota(jnp.int32, h.shape, 0) & (cols - 1)
    length = h.shape[0]
    left = jnp.where(col == 0, h, pltpu.roll(h, 1, 0))
    right = jnp.where(col == cols - 1, h, pltpu.roll(h, length - 1, 0))
    return left, right


def block_kernel(
    sizes,
    feat, gain1_hbm, shift1_hbm, w1, bias1_hbm, wskip, gain2_hbm, shift2_hbm, w2, bias2_hbm,
    out,
    gain1, shift1, bias1, gain2, shift2, bias2, featv, xall, w1v, wsv, wcat, xp1, xp2,
    acc, part1, send1, recv1, sum1, send1b, recv1b, stat0, statg, stat2,
    mids, midbf, prevbf, scut, part2, send2, recv2, sum2, send2b, recv2b,
    w_sem, p_sem, own_sem, fs_sem, fr_sem, fps_sem, fpr_sem,
    s1s_sem, s1r_sem, sgs_sem, sgr_sem, s2s_sem, s2r_sem,
    r1s_sem, r1r_sem, r1bs_sem, r1br_sem, r2s_sem, r2r_sem, r2bs_sem, r2br_sem,
    ps_sem, pr_sem,
):
    slabs, nrow, ncol, rows, cols, per1, per2 = sizes
    n = nrow * ncol
    height, width = nrow * rows, ncol * cols
    area = height * width
    t = lax.axis_index("tm")
    r = lax.axis_index("row")
    c = lax.axis_index("col")
    me = r * ncol + c

    def place(i):
        return lax.div(i, ncol), lax.rem(i, ncol)

    def ident(ti, i):
        ri, ci = place(i)
        return {"tm": ti, "row": ri, "col": ci}

    def member(delta):
        return lax.rem(r + delta // ncol, nrow) * ncol + lax.rem(c + delta % ncol, ncol)

    def slab(delta):
        return lax.rem(t + delta, slabs)

    loads = [
        pltpu.make_async_copy(w1, w1v, w_sem.at[0]),
        pltpu.make_async_copy(wskip, wsv, w_sem.at[1]),
    ]
    for i, (f, p, place_in, dt) in enumerate(
        ((0, 0, 0, 0), (0, 0, 1, 1), (0, 1, 0, 2), (1, 0, 1, 0), (1, 1, 0, 1), (1, 1, 1, 2))
    ):
        lo = place_in * per2
        loads.append(
            pltpu.make_async_copy(
                w2.at[dt], wcat.at[f, p, :, lo : lo + per2, :], w_sem.at[2 + i]
            )
        )
    params = [
        pltpu.make_async_copy(source, target, p_sem.at[i])
        for i, (source, target) in enumerate(
            (
                (gain1_hbm, gain1), (shift1_hbm, shift1), (bias1_hbm, bias1),
                (gain2_hbm, gain2), (shift2_hbm, shift2), (bias2_hbm, bias2),
            )
        )
    ]

    def window(frame0, i):
        ri, ci = place(i)
        top = ri * rows
        left = pl.multiple_of(ci * cols, cols)
        return xall.at[frame0 : frame0 + 2, pl.ds(top, rows), pl.ds(left, cols), :]

    def chunk(i):
        return feat.at[:, :, :, pl.ds(pl.multiple_of(i * LANES, LANES), LANES)]

    whole = pltpu.make_async_copy(feat, featv, own_sem.at[1])
    whole.start()
    own = pltpu.make_async_copy(chunk(me), window(2, me), own_sem.at[0])
    own.start()

    barrier = pltpu.get_barrier_semaphore()
    for delta in range(1, n):
        pl.semaphore_signal(barrier, inc=1, device_id=ident(t, member(delta)), device_id_type=MESH)
    for delta in range(1, slabs):
        pl.semaphore_signal(barrier, inc=1, device_id=ident(slab(delta), me), device_id_type=MESH)

    @pl.when(t > 0)
    def _():
        for delta in range(1, n):
            pl.semaphore_signal(
                barrier, inc=1, device_id=ident(t - 1, member(delta)), device_id_type=MESH
            )

    for load in params + loads:
        load.start()
    blank = jnp.zeros((9, per2, wcat.shape[4]), wcat.dtype)
    wcat[0, 1, :, per2:, :] = blank
    wcat[1, 0, :, :per2, :] = blank

    row8 = lax.broadcasted_iota(jnp.int32, (2 * n, LANES), 0)
    spots = float(2 * rows * cols)
    whole.wait()
    x = featv[...].reshape(2 * rows * cols, n * LANES).astype(jnp.float32)
    lane_mean = jnp.sum(x, axis=0, keepdims=True) * (1.0 / spots)
    lane_spread = jnp.sum((x - lane_mean) ** 2, axis=0, keepdims=True)
    tile = jnp.zeros((2 * n, LANES), jnp.float32)
    for d in range(n):
        at = slice(d * LANES, (d + 1) * LANES)
        tile = jnp.where(row8 == d, lane_mean[:, at], tile)
        tile = jnp.where(row8 == n + d, lane_spread[:, at], tile)
    stat0[t] = tile

    pl.semaphore_wait(barrier, jnp.where(t < slabs - 1, 2 * (n - 1), n - 1) + slabs - 1)

    def stat_copy(buf, source, target, ssem, rsem):
        return pltpu.make_async_remote_copy(
            src_ref=buf.at[source], dst_ref=buf.at[source],
            send_sem=ssem.at[target], recv_sem=rsem.at[source],
            device_id=ident(target, me), device_id_type=MESH,
        )

    def share_copy(source, target):
        return pltpu.make_async_remote_copy(
            src_ref=statg.at[source], dst_ref=statg.at[source],
            send_sem=sgs_sem.at[target], recv_sem=sgr_sem.at[source],
            device_id=ident(t, target), device_id_type=MESH,
        )

    for delta in reversed(range(1, slabs)):
        stat_copy(stat0, t, slab(delta), s1s_sem, s1r_sem).start()

    def feat_copy(source, target):
        return pltpu.make_async_remote_copy(
            src_ref=chunk(target), dst_ref=window(2, source),
            send_sem=fs_sem.at[target], recv_sem=fr_sem.at[source],
            device_id=ident(t, target), device_id_type=MESH,
        )

    def feat_next(source, target, to):
        return pltpu.make_async_remote_copy(
            src_ref=chunk(target), dst_ref=window(0, source),
            send_sem=fps_sem.at[target], recv_sem=fpr_sem.at[source],
            device_id=ident(to, target), device_id_type=MESH,
        )

    @pl.when(t < slabs - 1)
    def _():
        for delta in range(ncol):
            feat_next(me, member(delta), t + 1).start()

    for delta in reversed(range(1, n)):
        feat_copy(me, member(delta)).start()

    @pl.when(t < slabs - 1)
    def _():
        for delta in range(ncol, n):
            feat_next(me, member(delta), t + 1).start()

    lane = lane_of((8, LANES))
    lane_in = lax.broadcasted_iota(jnp.int32, (LANES, LANES), 0)
    lane_to = lane_of((LANES, LANES))
    size1 = per1 // (GROUPS // n)
    size2 = per2 // (GROUPS // n)
    same1 = (lane_in // size1 == lane_to // size1).astype(jnp.bfloat16)
    same2 = ((lane_in % per2) // size2 == (lane_to % per2) // size2).astype(jnp.bfloat16)

    def own_full(ref):
        result = ref[0:1, 0:LANES]
        for d in range(1, n):
            result = jnp.where(me == d, ref[0:1, d * LANES : (d + 1) * LANES], result)
        return result

    def own_twice(ref):
        result = jnp.zeros((8, LANES), jnp.float32)
        for d in range(n):
            k = d // 2 * LANES
            seg = jnp.broadcast_to(ref[0:1, k : k + LANES], (8, LANES))
            turned = pltpu.roll(seg, per2, 1)
            twice = jnp.where((lane < per2) == (d % 2 == 0), seg, turned)
            result = jnp.where(me == d, twice, result)
        return result[0:1]

    for load in params:
        load.wait()
    g1, b1 = own_full(gain1), own_full(shift1)
    g2, b2, c1 = own_twice(gain2), own_twice(shift2), own_twice(bias1)

    for delta in range(1, slabs):
        stat_copy(stat0, slab(delta), t, s1s_sem, s1r_sem).wait_recv()
    stats = stat0[...]
    total = jnp.sum(stats, axis=0)
    mean = total * (1.0 / slabs)
    off = spots * jnp.sum((stats - mean[None]) ** 2, axis=0)
    statg[me] = jnp.where(row8 < n, mean, total + pltpu.roll(off, n, 0))
    for delta in reversed(range(1, n)):
        share_copy(me, member(delta)).start()

    own.wait()
    for delta in range(1, n):
        feat_copy(member(delta), me).wait_recv()
    loads[1].wait()
    for f in range(2):
        x = xall[2 + f].reshape(area, LANES)
        scut[f] = jnp.dot(x, wsv[...], preferred_element_type=jnp.float32)

    for delta in range(1, n):
        share_copy(member(delta), me).wait_recv()
    stats = statg[...]
    pick = lax.broadcasted_iota(jnp.int32, stats.shape, 1)
    means = jnp.sum(jnp.where(pick == me, stats, 0.0), axis=1, keepdims=True)
    spreads = jnp.sum(jnp.where(pick == n + me, stats, 0.0), axis=1, keepdims=True)
    mean, inv = group_stats(means, spreads, same1, size1, spots * slabs)
    scale = inv * g1

    def normalise(f):
        x = xall[f].reshape(area, LANES).astype(jnp.float32)
        h = silu((x - mean) * scale + b1)
        left, right = side_shifts(h, width)
        for dx, part in enumerate((left, h, right)):
            part = part.astype(jnp.bfloat16).reshape(height, width, LANES)
            lanes = slice(dx * LANES, (dx + 1) * LANES)
            xp1[f, 1 : height + 1, :, lanes] = part
            xp1[f, 0, :, lanes] = part[0]
            xp1[f, height + 1, :, lanes] = part[height - 1]

    depth = 9 * LANES
    tall = height // 2
    half = tall * width

    def conv1(dt, s):
        rows_in = [xp1[dt : dt + 2, s * tall + dy : (s + 1) * tall + dy] for dy in range(3)]
        lhs = jnp.concatenate([x.reshape(2 * half, 3 * LANES) for x in rows_in], axis=1)
        rhs = w1v[dt * depth : (dt + 1) * depth, :]
        return jnp.dot(lhs, rhs, preferred_element_type=jnp.float32)

    normalise(2)
    normalise(3)
    loads[0].wait()
    for s in range(2):
        acc[s] = conv1(2, s)

    @pl.when(t > 0)
    def _():
        for delta in range(n):
            feat_next(member(delta), me, t).wait_recv()

    @pl.when(t == 0)
    def _():
        xall[0] = xall[2]
        xall[1] = xall[2]

    normalise(0)
    normalise(1)

    def core_copy(src, dst, source, target, s, ssem, rsem):
        return pltpu.make_async_remote_copy(
            src_ref=src.at[s, target], dst_ref=dst.at[s, source],
            send_sem=ssem.at[s, target], recv_sem=rsem.at[s, source],
            device_id={"tm": t, "row": r, "col": target}, device_id_type=MESH,
        )

    def row_copy(src, dst, source, target, s, ssem, rsem):
        return pltpu.make_async_remote_copy(
            src_ref=src.at[s, target], dst_ref=dst.at[s, source],
            send_sem=ssem.at[s, target], recv_sem=rsem.at[s, source],
            device_id={"tm": t, "row": target, "col": c}, device_id_type=MESH,
        )

    cores = [lax.rem(c + delta, ncol) for delta in range(1, ncol)]
    others = [lax.rem(r + delta, nrow) for delta in range(1, nrow)]

    def to_cores(stage, s):
        send, recv, ssem, rsem = stage
        for core in cores:
            core_copy(send, recv, c, core, s, ssem, rsem).start()

    def to_rows(stage, part, total, stage_b, s):
        send, recv, ssem, rsem = stage
        send_b, recv_b, ssem_b, rsem_b = stage_b
        summed = part[s, c]
        for core in cores:
            core_copy(send, recv, core, c, s, ssem, rsem).wait_recv()
            summed = summed + recv[s, core].astype(jnp.float32)
        total[s] = summed
        send_b[s] = summed.astype(jnp.bfloat16)
        for other in others:
            row_copy(send_b, recv_b, r, other, s, ssem_b, rsem_b).start()

    def from_rows(total, stage_b, s):
        send_b, recv_b, ssem_b, rsem_b = stage_b
        result = total[s, r]
        for other in others:
            row_copy(send_b, recv_b, other, r, s, ssem_b, rsem_b).wait_recv()
            result = result + recv_b[s, other].astype(jnp.float32)
        return result

    def sent_to_cores(stage):
        send, recv, ssem, rsem = stage
        for s in range(2):
            for core in cores:
                core_copy(send, recv, c, core, s, ssem, rsem).wait_send()

    def sent_to_rows(stage):
        send, recv, ssem, rsem = stage
        for s in range(2):
            for other in others:
                row_copy(send, recv, r, other, s, ssem, rsem).wait_send()

    first = (send1, recv1, r1s_sem, r1r_sem)
    first_b = (send1b, recv1b, r1bs_sem, r1br_sem)
    second = (send2, recv2, r2s_sem, r2r_sem)
    second_b = (send2b, recv2b, r2bs_sem, r2br_sem)

    wide = lane_of((half, LANES))
    for s in range(2):
        total = acc[s] + conv1(1, s) + conv1(0, s)
        for d in range(n):
            k = d // 2 * LANES
            one, two = total[:half, k : k + LANES], total[half:, k : k + LANES]
            if d % 2 == 0:
                packed = jnp.where(wide < per2, one, pltpu.roll(two, per2, 1))
            else:
                packed = jnp.where(wide < per2, pltpu.roll(one, per2, 1), two)
            part1[s, d % ncol, d // ncol] = packed
            send1[s, d % ncol, d // ncol] = packed.astype(jnp.bfloat16)
        to_cores(first, s)
    for s in range(2):
        to_rows(first, part1, sum1, first_b, s)

    for delta in range(1, n):
        feat_copy(me, member(delta)).wait_send()
        share_copy(me, member(delta)).wait_send()
    for delta in range(1, slabs):
        stat_copy(stat0, t, slab(delta), s1s_sem, s1r_sem).wait_send()

    @pl.when(t < slabs - 1)
    def _():
        for delta in range(n):
            feat_next(me, member(delta), t + 1).wait_send()

    def mid_copy(to, s):
        return pltpu.make_async_remote_copy(
            src_ref=midbf.at[s], dst_ref=prevbf.at[s],
            send_sem=ps_sem.at[s], recv_sem=pr_sem.at[s],
            device_id=ident(to, me), device_id_type=MESH,
        )

    def pass_on(s):
        @pl.when(t < slabs - 1)
        def _():
            mid_copy(t + 1, s).start()

    for s in range(2):
        middle = from_rows(sum1, first_b, s) + c1
        midbf[s] = middle.astype(jnp.bfloat16)
        mids[1, s] = middle
        if s == 0:
            pass_on(0)

    stat2[t] = lane_stats(mids[1].reshape(area, LANES))
    for delta in reversed(range(1, slabs)):
        stat_copy(stat2, t, slab(delta), s2s_sem, s2r_sem).start()
    pass_on(1)

    for delta in range(1, slabs):
        stat_copy(stat2, slab(delta), t, s2s_sem, s2r_sem).wait_recv()
    sent_to_cores(first)
    sent_to_rows(first_b)
    stats = stat2[...]
    mean, inv = group_stats(stats[:, 0:1], stats[:, 1:2], same2, 2 * size2, float(area))
    scale = inv * g2

    def normalise_mid(i):
        h = silu((mids[i].reshape(area, LANES) - mean) * scale + b2)
        left, right = side_shifts(h, width)
        for dx, part in enumerate((left, h, right)):
            part = part.astype(jnp.bfloat16).reshape(height, width, LANES)
            lanes = slice(dx * LANES, (dx + 1) * LANES)
            xp2[i, 1 : height + 1, :, lanes] = part
            xp2[i, 0, :, lanes] = part[0]
            xp2[i, height + 1, :, lanes] = part[height - 1]

    def conv2(f, i):
        rows_in = [xp2[i, dy : dy + height].reshape(area, 3 * LANES) for dy in range(3)]
        rhs = wcat[f, i].reshape(9 * LANES, wcat.shape[4])
        return jnp.dot(
            jnp.concatenate(rows_in, axis=1), rhs, preferred_element_type=jnp.float32
        )

    normalise_mid(1)
    for load in loads[2:]:
        load.wait()
    for f in range(2):
        scut[f] = scut[f] + conv2(f, 1)

    @pl.when(t > 0)
    def _():
        for s in range(2):
            mid_copy(t, s).wait_recv()
            mids[0, s] = prevbf[s].astype(jnp.float32)

    @pl.when(t == 0)
    def _():
        for s in range(2):
            middle = mids[1, s]
            mids[0, s] = jnp.where(wide < per2, middle, pltpu.roll(middle, per2, 1))

    normalise_mid(0)
    for f in range(2):
        total = (scut[f] + conv2(f, 0)).reshape(nrow, rows, width, wcat.shape[4])
        for ci in range(ncol):
            piece = total[:, :, ci * cols : (ci + 1) * cols]
            part2[f, ci] = piece
            send2[f, ci] = piece.astype(jnp.bfloat16)
        to_cores(second, f)
    for f in range(2):
        to_rows(second, part2, sum2, second_b, f)
    for delta in range(1, slabs):
        stat_copy(stat2, t, slab(delta), s2s_sem, s2r_sem).wait_send()

    @pl.when(t < slabs - 1)
    def _():
        for s in range(2):
            mid_copy(t + 1, s).wait_send()

    sent_to_cores(second)
    last = bias2[...].reshape(1, 1, -1)
    for f in range(2):
        out[f] = (from_rows(sum2, second_b, f) + last).astype(out.dtype)

    sent_to_rows(second_b)


def per_device(
    features,
    gn1_gain,
    gn1_bias,
    conv1_weight,
    conv1_bias,
    skip_weight,
    gn2_gain,
    gn2_bias,
    conv2_weight,
    conv2_bias,
):
    frames, rows, cols, chans_in = features.shape
    per1, per2 = conv1_weight.shape[1], conv2_weight.shape[1]
    chans_out = conv1_weight.shape[2]
    slabs, nrow, ncol = (lax.axis_size(a) for a in ("tm", "row", "col"))
    n = nrow * ncol
    height, width = nrow * rows, ncol * cols
    area = height * width
    fits = frames == 2 and per1 == LANES and 2 * per2 == LANES and cols % 16 == 0
    fits = fits and n == 4 and width & (width - 1) == 0 and GROUPS % n == 0 and height % 2 == 0
    if not fits:
        return per_device_gathered(
            features, gn1_gain, gn1_bias, conv1_weight, conv1_bias, skip_weight,
            gn2_gain, gn2_bias, conv2_weight, conv2_bias,
        )
    bf16, f32 = jnp.bfloat16, jnp.float32
    vmem, dma = pltpu.VMEM, pltpu.SemaphoreType.DMA
    half = area // 2
    scratch = [
        vmem((1, chans_in), f32),
        vmem((1, chans_in), f32),
        vmem((1, chans_out), f32),
        vmem((1, chans_out), f32),
        vmem((1, chans_out), f32),
        vmem((1, chans_out), f32),
        vmem((frames, rows, cols, chans_in), bf16),
        vmem((4, height, width, LANES), bf16),
        vmem((27 * per1, chans_out), bf16),
        vmem((per1, chans_out), bf16),
        vmem((2, 2, 9, 2 * per2, chans_out), bf16),
        vmem((4, height + 2, width, 3 * LANES), bf16),
        vmem((2, height + 2, width, 3 * LANES), bf16),
        vmem((2, area, chans_out), f32),
        vmem((2, ncol, nrow, half, LANES), f32),
        vmem((2, ncol, nrow, half, LANES), bf16),
        vmem((2, ncol, nrow, half, LANES), bf16),
        vmem((2, nrow, half, LANES), f32),
        vmem((2, nrow, half, LANES), bf16),
        vmem((2, nrow, half, LANES), bf16),
        vmem((slabs, 2 * n, LANES), f32),
        vmem((n, 2 * n, LANES), f32),
        vmem((slabs, 8, LANES), f32),
        vmem((2, 2, half, LANES), f32),
        vmem((2, half, LANES), bf16),
        vmem((2, half, LANES), bf16),
        vmem((2, area, chans_out), f32),
        vmem((2, ncol, nrow, rows, cols, chans_out), f32),
        vmem((2, ncol, nrow, rows, cols, chans_out), bf16),
        vmem((2, ncol, nrow, rows, cols, chans_out), bf16),
        vmem((2, nrow, rows, cols, chans_out), f32),
        vmem((2, nrow, rows, cols, chans_out), bf16),
        vmem((2, nrow, rows, cols, chans_out), bf16),
        dma((8,)), dma((6,)), dma((2,)), dma((n,)), dma((n,)), dma((n,)), dma((n,)),
        dma((slabs,)), dma((slabs,)), dma((n,)), dma((n,)), dma((slabs,)), dma((slabs,)),
        dma((2, ncol)), dma((2, ncol)), dma((2, nrow)), dma((2, nrow)),
        dma((2, ncol)), dma((2, ncol)), dma((2, nrow)), dma((2, nrow)),
        dma((2,)), dma((2,)),
    ]
    stays = pl.BlockSpec(memory_space=pltpu.HBM)
    inside = pl.BlockSpec(memory_space=pltpu.VMEM)
    sizes = (slabs, nrow, ncol, rows, cols, per1, per2)
    flops = 2 * 2 * area * chans_out * (28 * per1 + 27 * per2)
    operands = (
        features,
        gn1_gain.reshape(1, -1),
        gn1_bias.reshape(1, -1),
        conv1_weight.reshape(27 * per1, chans_out),
        conv1_bias.reshape(1, -1),
        skip_weight.reshape(per1, chans_out),
        gn2_gain.reshape(1, -1),
        gn2_bias.reshape(1, -1),
        conv2_weight.reshape(3, 9, per2, chans_out),
        conv2_bias.reshape(1, -1),
    )
    return pl.pallas_call(
        functools.partial(block_kernel, sizes),
        out_shape=jax.ShapeDtypeStruct((frames, rows, cols, chans_out), bf16),
        in_specs=[stays] * 10,
        out_specs=inside,
        scratch_shapes=scratch,
        compiler_params=pltpu.CompilerParams(
            collective_id=0, has_side_effects=True, vmem_limit_bytes=48 * 1024 * 1024
        ),
        cost_estimate=pl.CostEstimate(
            flops=flops, bytes_accessed=4 * 1024 * 1024, transcendentals=6 * area * LANES
        ),
        name="residual_block",
    )(*(pltpu.with_memory_space_constraint(x, pltpu.HBM) for x in operands))


def solution(mesh):
    in_specs = (
        P("tm", "row", "col", None),
        P(),
        P(),
        P(None, ("row", "col"), None),
        P(),
        P(None, ("row", "col"), None),
        P(),
        P(),
        P(None, ("row", "col"), None),
        P(),
    )
    out_specs = P("tm", "row", "col", None)
    return jax.shard_map(
        per_device, mesh=mesh, in_specs=in_specs, out_specs=out_specs, check_vma=False
    )
```

```python
import functools

import jax
import jax.numpy as jnp
from jax import lax
from jax.experimental import pallas as pl
from jax.experimental.pallas import tpu as pltpu
from jax.sharding import PartitionSpec as P

GROUPS = 32


def passed_along(block, axis, distance):
    devices = range(lax.axis_size(axis))
    route = [(i - distance, i) for i in devices if i - distance in devices]
    return lax.ppermute(block, axis, route)


def with_halo(array, sides, width):
    for axis, dim in sides:
        size, length = (lax.axis_size(axis), array.shape[dim])
        up = [(i, (i + 1) % size) for i in range(size - 1)]
        down = [(j, i) for i, j in up]
        last = lax.slice_in_dim(array, length - width, length, axis=dim)
        leading = lax.slice_in_dim(array, 0, width, axis=dim)
        before = lax.ppermute(last, axis, up)
        after = lax.ppermute(leading, axis, down)
        array = jnp.concatenate([before, array, after], axis=dim)
    return array


def group_silu(values, gain, shift, groups, total_rows):
    chans = values.shape[-1]
    per_group = chans // groups
    grouped = values.reshape(-1, groups, per_group)
    count = float(total_rows * per_group)
    mean = lax.psum(jnp.sum(grouped, axis=(0, 2)), ("tm", "row", "col")) / count
    centred = grouped - mean[None, :, None]
    spread = lax.psum(jnp.sum(centred * centred, axis=(0, 2)), ("tm", "row", "col")) / count
    normed = (grouped - mean[None, :, None]) * lax.rsqrt(spread + 1e-06)[None, :, None]
    normed = normed.reshape(values.shape) * gain + shift
    return jax.nn.silu(normed).astype(jnp.bfloat16)


def conv_taps(padded, weight, frames, rows, cols):
    chans = padded.shape[3]
    total = jnp.zeros((frames * rows * cols, weight.shape[2]), jnp.float32)
    for dt in range(3):
        pieces = []
        for tap in range(9):
            dy, dx = (tap // 3, tap % 3)
            pieces.append(
                padded[dt : dt + frames, dy : dy + rows, dx : dx + cols].reshape(-1, chans)
            )
        stacked = jnp.concatenate(pieces, axis=1)
        flat_weight = weight[9 * dt : 9 * dt + 9].reshape(9 * chans, weight.shape[2])
        total = total + jnp.dot(stacked, flat_weight, preferred_element_type=jnp.float32)
    return total


def time_edge(earlier, volume):
    first_twice = jnp.concatenate([volume[:1], volume[:1]], axis=0)
    earlier = jnp.where(lax.axis_index("tm") == 0, first_twice, earlier)
    return jnp.concatenate([earlier, volume], axis=0)


def edge_rows(padded):
    place = lax.axis_index("row")
    last = lax.axis_size("row") - 1
    top = jnp.where(place == 0, padded[:, 1:2], padded[:, 0:1])
    bottom = jnp.where(place == last, padded[:, -2:-1], padded[:, -1:])
    return jnp.concatenate([top, padded[:, 1:-1], bottom], axis=1)


def edge_cols(padded):
    place = lax.axis_index("col")
    last = lax.axis_size("col") - 1
    left = jnp.where(place == 0, padded[:, :, 1:2], padded[:, :, 0:1])
    right = jnp.where(place == last, padded[:, :, -2:-1], padded[:, :, -1:])
    return jnp.concatenate([left, padded[:, :, 1:-1], right], axis=2)


def per_device_gathered(
    features,
    gn1_gain,
    gn1_bias,
    conv1_weight,
    conv1_bias,
    skip_weight,
    gn2_gain,
    gn2_bias,
    conv2_weight,
    conv2_bias,
):
    frames, rows, cols, chans_in = features.shape
    chans_out = conv1_weight.shape[2]
    groups = GROUPS
    nrow = lax.axis_size("row")
    ncol = lax.axis_size("col")
    total_rows = lax.axis_size("tm") * nrow * ncol * frames * rows * cols
    flat_features = features.reshape(-1, chans_in)
    hidden1 = group_silu(features.astype(jnp.float32), gn1_gain, gn1_bias, groups, total_rows)
    earlier = passed_along(hidden1, "tm", 1)
    extended = time_edge(earlier, hidden1)
    padded = with_halo(extended, (("row", 1), ("col", 2)), 1)
    padded = edge_cols(edge_rows(padded))
    window = padded
    first = conv_taps(
        window, lax.all_gather(conv1_weight, ("row", "col"), axis=1, tiled=True), frames, rows, cols
    )
    second = jnp.dot(
        flat_features,
        lax.all_gather(skip_weight, ("row", "col"), axis=1, tiled=True)[0],
        preferred_element_type=jnp.float32,
    )
    middle = (first + conv1_bias).reshape(frames, rows, cols, chans_out)
    hidden2 = group_silu(middle, gn2_gain, gn2_bias, groups, total_rows)
    earlier_mid = passed_along(hidden2, "tm", 1)
    extended_mid = time_edge(earlier_mid, hidden2)
    padded_mid = with_halo(extended_mid, (("row", 1), ("col", 2)), 1)
    padded_mid = edge_cols(edge_rows(padded_mid))
    window = padded_mid
    conv_second = conv_taps(
        window, lax.all_gather(conv2_weight, ("row", "col"), axis=1, tiled=True), frames, rows, cols
    )
    block_out = (second + conv_second + conv2_bias).astype(jnp.bfloat16)
    return block_out.reshape(frames, rows, cols, chans_out)


MESH = pl.DeviceIdType.MESH
LANES = 128


def lane_of(shape):
    return lax.broadcasted_iota(jnp.int32, shape, len(shape) - 1)


def silu(a):
    half = 0.5 * a
    return half + half * jnp.tanh(half)


def lane_stats(x):
    mean = jnp.sum(x, axis=0, keepdims=True) * (1.0 / x.shape[0])
    spread = jnp.sum((x - mean) ** 2, axis=0, keepdims=True)
    row = lax.broadcasted_iota(jnp.int32, (8, LANES), 0)
    return jnp.where(row == 0, mean, jnp.where(row == 1, spread, 0.0))


def group_sums(x, same):
    high = x.astype(jnp.bfloat16).astype(jnp.float32)
    rest = x - high
    middle = rest.astype(jnp.bfloat16).astype(jnp.float32)
    row = lax.broadcasted_iota(jnp.int32, (16, LANES), 0)
    parts = jnp.where(row == 0, high, jnp.where(row == 1, middle, rest - middle))
    parts = jnp.where(row < 3, parts, 0.0).astype(jnp.bfloat16)
    sums = jnp.dot(parts, same, preferred_element_type=jnp.float32)
    return jnp.sum(sums, axis=0, keepdims=True)


def group_stats(means, spreads, same, lanes, count):
    parts = means.shape[0]
    mean = jnp.sum(means, axis=0) * (1.0 / parts)
    spread = jnp.sum(spreads, axis=0) + count * jnp.sum((means - mean[None]) ** 2, axis=0)
    group_mean = group_sums(mean, same) * (1.0 / lanes)
    spread = spread + (count * parts) * (mean - group_mean) ** 2
    total = group_sums(spread, same)
    return group_mean, lax.rsqrt(total * (1.0 / (count * parts * lanes)) + 1e-6)


def side_shifts(h, cols):
    col = lax.broadcasted_iota(jnp.int32, h.shape, 0) & (cols - 1)
    length = h.shape[0]
    left = jnp.where(col == 0, h, pltpu.roll(h, 1, 0))
    right = jnp.where(col == cols - 1, h, pltpu.roll(h, length - 1, 0))
    return left, right


def block_kernel(
    sizes,
    feat, gain1_hbm, shift1_hbm, w1, bias1_hbm, wskip, gain2_hbm, shift2_hbm, w2, bias2_hbm,
    out,
    gain1, shift1, bias1, gain2, shift2, bias2, featv, xall, w1v, wsv, wcat, xp1, xp2,
    acc, part1, send1, recv1, sum1, send1b, recv1b, stat0, statg, stat2,
    mids, midbf, prevbf, scut, part2, send2, recv2, sum2, send2b, recv2b,
    w_sem, p_sem, own_sem, fs_sem, fr_sem, fps_sem, fpr_sem,
    s1s_sem, s1r_sem, sgs_sem, sgr_sem, s2s_sem, s2r_sem,
    r1s_sem, r1r_sem, r1bs_sem, r1br_sem, r2s_sem, r2r_sem, r2bs_sem, r2br_sem,
    ps_sem, pr_sem,
):
    slabs, nrow, ncol, rows, cols, per1, per2 = sizes
    n = nrow * ncol
    height, width = nrow * rows, ncol * cols
    area = height * width
    t = lax.axis_index("tm")
    r = lax.axis_index("row")
    c = lax.axis_index("col")
    me = r * ncol + c

    def place(i):
        return lax.div(i, ncol), lax.rem(i, ncol)

    def ident(ti, i):
        ri, ci = place(i)
        return {"tm": ti, "row": ri, "col": ci}

    def member(delta):
        return lax.rem(r + delta // ncol, nrow) * ncol + lax.rem(c + delta % ncol, ncol)

    def slab(delta):
        return lax.rem(t + delta, slabs)

    q = slabs // 2
    side = lax.div(t, q)
    spot = lax.rem(t, q)
    far = slab(q)

    def near(delta):
        return side * q + lax.rem(spot + delta, q)

    loads = [
        pltpu.make_async_copy(w1, w1v, w_sem.at[0]),
        pltpu.make_async_copy(wskip, wsv, w_sem.at[1]),
    ]
    for i, (f, p, place_in, dt) in enumerate(
        ((0, 0, 0, 0), (0, 0, 1, 1), (0, 1, 0, 2), (1, 0, 1, 0), (1, 1, 0, 1), (1, 1, 1, 2))
    ):
        lo = place_in * per2
        loads.append(
            pltpu.make_async_copy(
                w2.at[dt], wcat.at[f, p, :, lo : lo + per2, :], w_sem.at[2 + i]
            )
        )
    params = [
        pltpu.make_async_copy(source, target, p_sem.at[i])
        for i, (source, target) in enumerate(
            (
                (gain1_hbm, gain1), (shift1_hbm, shift1), (bias1_hbm, bias1),
                (gain2_hbm, gain2), (shift2_hbm, shift2), (bias2_hbm, bias2),
            )
        )
    ]

    def window(frame0, i):
        ri, ci = place(i)
        top = ri * rows
        left = pl.multiple_of(ci * cols, cols)
        return xall.at[frame0 : frame0 + 2, pl.ds(top, rows), pl.ds(left, cols), :]

    def chunk(i):
        return feat.at[:, :, :, pl.ds(pl.multiple_of(i * LANES, LANES), LANES)]

    whole = pltpu.make_async_copy(feat, featv, own_sem.at[1])
    whole.start()
    own = pltpu.make_async_copy(chunk(me), window(2, me), own_sem.at[0])
    own.start()

    barrier = pltpu.get_barrier_semaphore()
    for delta in range(1, n):
        pl.semaphore_signal(barrier, inc=1, device_id=ident(t, member(delta)), device_id_type=MESH)
    for delta in range(1, q):
        pl.semaphore_signal(barrier, inc=1, device_id=ident(near(delta), me), device_id_type=MESH)
    for delta in range(n):
        pl.semaphore_signal(barrier, inc=1, device_id=ident(far, member(delta)), device_id_type=MESH)

    @pl.when(t > 0)
    def _():
        for delta in range(n):
            pl.semaphore_signal(
                barrier, inc=1, device_id=ident(t - 1, member(delta)), device_id_type=MESH
            )

    for load in params + loads:
        load.start()
    blank = jnp.zeros((9, per2, wcat.shape[4]), wcat.dtype)
    wcat[0, 1, :, per2:, :] = blank
    wcat[1, 0, :, :per2, :] = blank

    row8 = lax.broadcasted_iota(jnp.int32, (2 * n, LANES), 0)
    spots = float(2 * rows * cols)
    whole.wait()
    x = featv[...].reshape(2 * rows * cols, n * LANES).astype(jnp.float32)
    lane_mean = jnp.sum(x, axis=0, keepdims=True) * (1.0 / spots)
    lane_spread = jnp.sum((x - lane_mean) ** 2, axis=0, keepdims=True)
    tile = jnp.zeros((2 * n, LANES), jnp.float32)
    for d in range(n):
        at = slice(d * LANES, (d + 1) * LANES)
        tile = jnp.where(row8 == d, lane_mean[:, at], tile)
        tile = jnp.where(row8 == n + d, lane_spread[:, at], tile)
    stat0[spot] = tile

    pl.semaphore_wait(barrier, jnp.where(t < slabs - 1, n, 0) + 2 * n + q - 2)

    def stat_copy(buf, source, target, ssem, rsem):
        return pltpu.make_async_remote_copy(
            src_ref=buf.at[source], dst_ref=buf.at[source],
            send_sem=ssem.at[target], recv_sem=rsem.at[source],
            device_id=ident(target, me), device_id_type=MESH,
        )

    def near_copy(source, target):
        return pltpu.make_async_remote_copy(
            src_ref=stat0.at[lax.rem(source, q)], dst_ref=stat0.at[lax.rem(source, q)],
            send_sem=s1s_sem.at[lax.rem(target, q)], recv_sem=s1r_sem.at[lax.rem(source, q)],
            device_id=ident(target, me), device_id_type=MESH,
        )

    def share_copy(t_from, source, t_to, target):
        slot = lax.div(t_from, q) * n + source
        return pltpu.make_async_remote_copy(
            src_ref=statg.at[slot], dst_ref=statg.at[slot],
            send_sem=sgs_sem.at[lax.div(t_to, q) * n + target], recv_sem=sgr_sem.at[slot],
            device_id=ident(t_to, target), device_id_type=MESH,
        )

    sharers = [(far, delta) for delta in reversed(range(n))]
    sharers += [(t, delta) for delta in reversed(range(1, n))]

    for delta in reversed(range(1, q)):
        near_copy(t, near(delta)).start()

    def feat_copy(source, target):
        return pltpu.make_async_remote_copy(
            src_ref=chunk(target), dst_ref=window(2, source),
            send_sem=fs_sem.at[target], recv_sem=fr_sem.at[source],
            device_id=ident(t, target), device_id_type=MESH,
        )

    def feat_next(source, target, to):
        return pltpu.make_async_remote_copy(
            src_ref=chunk(target), dst_ref=window(0, source),
            send_sem=fps_sem.at[target], recv_sem=fpr_sem.at[source],
            device_id=ident(to, target), device_id_type=MESH,
        )

    @pl.when(t < slabs - 1)
    def _():
        for delta in range(ncol):
            feat_next(me, member(delta), t + 1).start()

    for delta in reversed(range(1, n)):
        feat_copy(me, member(delta)).start()

    for delta in range(1, q):
        near_copy(near(delta), t).wait_recv()
    stats = stat0[...]
    total = jnp.sum(stats, axis=0)
    mean = total * (1.0 / q)
    off = spots * jnp.sum((stats - mean[None]) ** 2, axis=0)
    statg[side * n + me] = jnp.where(row8 < n, mean, total + pltpu.roll(off, n, 0))
    for slab_to, delta in sharers:
        share_copy(t, me, slab_to, member(delta)).start()

    @pl.when(t < slabs - 1)
    def _():
        for delta in range(ncol, n):
            feat_next(me, member(delta), t + 1).start()

    lane = lane_of((8, LANES))
    lane_in = lax.broadcasted_iota(jnp.int32, (LANES, LANES), 0)
    lane_to = lane_of((LANES, LANES))
    size1 = per1 // (GROUPS // n)
    size2 = per2 // (GROUPS // n)
    same1 = (lane_in // size1 == lane_to // size1).astype(jnp.bfloat16)
    same2 = ((lane_in % per2) // size2 == (lane_to % per2) // size2).astype(jnp.bfloat16)

    def own_full(ref):
        result = ref[0:1, 0:LANES]
        for d in range(1, n):
            result = jnp.where(me == d, ref[0:1, d * LANES : (d + 1) * LANES], result)
        return result

    def own_twice(ref):
        result = jnp.zeros((8, LANES), jnp.float32)
        for d in range(n):
            k = d // 2 * LANES
            seg = jnp.broadcast_to(ref[0:1, k : k + LANES], (8, LANES))
            turned = pltpu.roll(seg, per2, 1)
            twice = jnp.where((lane < per2) == (d % 2 == 0), seg, turned)
            result = jnp.where(me == d, twice, result)
        return result[0:1]

    for load in params:
        load.wait()
    g1, b1 = own_full(gain1), own_full(shift1)
    g2, b2, c1 = own_twice(gain2), own_twice(shift2), own_twice(bias1)

    own.wait()
    for delta in range(1, n):
        feat_copy(member(delta), me).wait_recv()
    loads[1].wait()
    for f in range(2):
        x = xall[2 + f].reshape(area, LANES)
        scut[f] = jnp.dot(x, wsv[...], preferred_element_type=jnp.float32)

    for slab_from, delta in sharers:
        share_copy(slab_from, member(delta), t, me).wait_recv()
    stats = statg[...]
    pick = lax.broadcasted_iota(jnp.int32, stats.shape, 1)
    means = jnp.sum(jnp.where(pick == me, stats, 0.0), axis=1, keepdims=True)
    spreads = jnp.sum(jnp.where(pick == n + me, stats, 0.0), axis=1, keepdims=True)
    mean, inv = group_stats(means, spreads, same1, size1, spots * q)
    scale = inv * g1

    def normalise(f):
        x = xall[f].reshape(area, LANES).astype(jnp.float32)
        h = silu((x - mean) * scale + b1)
        left, right = side_shifts(h, width)
        for dx, part in enumerate((left, h, right)):
            part = part.astype(jnp.bfloat16).reshape(height, width, LANES)
            lanes = slice(dx * LANES, (dx + 1) * LANES)
            xp1[f, 1 : height + 1, :, lanes] = part
            xp1[f, 0, :, lanes] = part[0]
            xp1[f, height + 1, :, lanes] = part[height - 1]

    depth = 9 * LANES
    tall = height // 2
    half = tall * width

    def conv1(dt, s):
        rows_in = [xp1[dt : dt + 2, s * tall + dy : (s + 1) * tall + dy] for dy in range(3)]
        lhs = jnp.concatenate([x.reshape(2 * half, 3 * LANES) for x in rows_in], axis=1)
        rhs = w1v[dt * depth : (dt + 1) * depth, :]
        return jnp.dot(lhs, rhs, preferred_element_type=jnp.float32)

    normalise(2)
    normalise(3)
    loads[0].wait()
    for s in range(2):
        acc[s] = conv1(2, s)

    @pl.when(t > 0)
    def _():
        for delta in range(n):
            feat_next(member(delta), me, t).wait_recv()

    @pl.when(t == 0)
    def _():
        xall[0] = xall[2]
        xall[1] = xall[2]

    normalise(0)
    normalise(1)

    def core_copy(src, dst, source, target, s, ssem, rsem):
        return pltpu.make_async_remote_copy(
            src_ref=src.at[s, target], dst_ref=dst.at[s, source],
            send_sem=ssem.at[s, target], recv_sem=rsem.at[s, source],
            device_id={"tm": t, "row": r, "col": target}, device_id_type=MESH,
        )

    def row_copy(src, dst, source, target, s, ssem, rsem):
        return pltpu.make_async_remote_copy(
            src_ref=src.at[s, target], dst_ref=dst.at[s, source],
            send_sem=ssem.at[s, target], recv_sem=rsem.at[s, source],
            device_id={"tm": t, "row": target, "col": c}, device_id_type=MESH,
        )

    cores = [lax.rem(c + delta, ncol) for delta in range(1, ncol)]
    others = [lax.rem(r + delta, nrow) for delta in range(1, nrow)]

    def to_cores(stage, s):
        send, recv, ssem, rsem = stage
        for core in cores:
            core_copy(send, recv, c, core, s, ssem, rsem).start()

    def to_rows(stage, part, total, stage_b, s):
        send, recv, ssem, rsem = stage
        send_b, recv_b, ssem_b, rsem_b = stage_b
        summed = part[s, c]
        for core in cores:
            core_copy(send, recv, core, c, s, ssem, rsem).wait_recv()
            summed = summed + recv[s, core].astype(jnp.float32)
        total[s] = summed
        send_b[s] = summed.astype(jnp.bfloat16)
        for other in others:
            row_copy(send_b, recv_b, r, other, s, ssem_b, rsem_b).start()

    def from_rows(total, stage_b, s):
        send_b, recv_b, ssem_b, rsem_b = stage_b
        result = total[s, r]
        for other in others:
            row_copy(send_b, recv_b, other, r, s, ssem_b, rsem_b).wait_recv()
            result = result + recv_b[s, other].astype(jnp.float32)
        return result

    def sent_to_cores(stage):
        send, recv, ssem, rsem = stage
        for s in range(2):
            for core in cores:
                core_copy(send, recv, c, core, s, ssem, rsem).wait_send()

    def sent_to_rows(stage):
        send, recv, ssem, rsem = stage
        for s in range(2):
            for other in others:
                row_copy(send, recv, r, other, s, ssem, rsem).wait_send()

    first = (send1, recv1, r1s_sem, r1r_sem)
    first_b = (send1b, recv1b, r1bs_sem, r1br_sem)
    second = (send2, recv2, r2s_sem, r2r_sem)
    second_b = (send2b, recv2b, r2bs_sem, r2br_sem)

    wide = lane_of((half, LANES))
    for s in range(2):
        total = acc[s] + conv1(1, s) + conv1(0, s)
        for d in range(n):
            k = d // 2 * LANES
            one, two = total[:half, k : k + LANES], total[half:, k : k + LANES]
            if d % 2 == 0:
                packed = jnp.where(wide < per2, one, pltpu.roll(two, per2, 1))
            else:
                packed = jnp.where(wide < per2, pltpu.roll(one, per2, 1), two)
            part1[s, d % ncol, d // ncol] = packed
            send1[s, d % ncol, d // ncol] = packed.astype(jnp.bfloat16)
        to_cores(first, s)
    for s in range(2):
        to_rows(first, part1, sum1, first_b, s)

    for delta in range(1, n):
        feat_copy(me, member(delta)).wait_send()
    for slab_to, delta in sharers:
        share_copy(t, me, slab_to, member(delta)).wait_send()
    for delta in range(1, q):
        near_copy(t, near(delta)).wait_send()

    @pl.when(t < slabs - 1)
    def _():
        for delta in range(n):
            feat_next(me, member(delta), t + 1).wait_send()

    def mid_copy(to, s):
        return pltpu.make_async_remote_copy(
            src_ref=midbf.at[s], dst_ref=prevbf.at[s],
            send_sem=ps_sem.at[s], recv_sem=pr_sem.at[s],
            device_id=ident(to, me), device_id_type=MESH,
        )

    def pass_on(s):
        @pl.when(t < slabs - 1)
        def _():
            mid_copy(t + 1, s).start()

    for s in range(2):
        middle = from_rows(sum1, first_b, s) + c1
        midbf[s] = middle.astype(jnp.bfloat16)
        mids[1, s] = middle
        if s == 0:
            pass_on(0)

    stat2[t] = lane_stats(mids[1].reshape(area, LANES))
    for delta in reversed(range(1, slabs)):
        stat_copy(stat2, t, slab(delta), s2s_sem, s2r_sem).start()
    pass_on(1)

    for delta in range(1, slabs):
        stat_copy(stat2, slab(delta), t, s2s_sem, s2r_sem).wait_recv()
    sent_to_cores(first)
    sent_to_rows(first_b)
    stats = stat2[...]
    mean, inv = group_stats(stats[:, 0:1], stats[:, 1:2], same2, 2 * size2, float(area))
    scale = inv * g2

    def normalise_mid(i):
        h = silu((mids[i].reshape(area, LANES) - mean) * scale + b2)
        left, right = side_shifts(h, width)
        for dx, part in enumerate((left, h, right)):
            part = part.astype(jnp.bfloat16).reshape(height, width, LANES)
            lanes = slice(dx * LANES, (dx + 1) * LANES)
            xp2[i, 1 : height + 1, :, lanes] = part
            xp2[i, 0, :, lanes] = part[0]
            xp2[i, height + 1, :, lanes] = part[height - 1]

    def conv2(f, i):
        rows_in = [xp2[i, dy : dy + height].reshape(area, 3 * LANES) for dy in range(3)]
        rhs = wcat[f, i].reshape(9 * LANES, wcat.shape[4])
        return jnp.dot(
            jnp.concatenate(rows_in, axis=1), rhs, preferred_element_type=jnp.float32
        )

    normalise_mid(1)
    for load in loads[2:]:
        load.wait()
    for f in range(2):
        scut[f] = scut[f] + conv2(f, 1)

    @pl.when(t > 0)
    def _():
        for s in range(2):
            mid_copy(t, s).wait_recv()
            mids[0, s] = prevbf[s].astype(jnp.float32)

    @pl.when(t == 0)
    def _():
        for s in range(2):
            middle = mids[1, s]
            mids[0, s] = jnp.where(wide < per2, middle, pltpu.roll(middle, per2, 1))

    normalise_mid(0)
    for f in range(2):
        total = (scut[f] + conv2(f, 0)).reshape(nrow, rows, width, wcat.shape[4])
        for ci in range(ncol):
            piece = total[:, :, ci * cols : (ci + 1) * cols]
            part2[f, ci] = piece
            send2[f, ci] = piece.astype(jnp.bfloat16)
        to_cores(second, f)
    for f in range(2):
        to_rows(second, part2, sum2, second_b, f)
    for delta in range(1, slabs):
        stat_copy(stat2, t, slab(delta), s2s_sem, s2r_sem).wait_send()

    @pl.when(t < slabs - 1)
    def _():
        for s in range(2):
            mid_copy(t + 1, s).wait_send()

    sent_to_cores(second)
    last = bias2[...].reshape(1, 1, -1)
    for f in range(2):
        out[f] = (from_rows(sum2, second_b, f) + last).astype(out.dtype)

    sent_to_rows(second_b)


def per_device(
    features,
    gn1_gain,
    gn1_bias,
    conv1_weight,
    conv1_bias,
    skip_weight,
    gn2_gain,
    gn2_bias,
    conv2_weight,
    conv2_bias,
):
    frames, rows, cols, chans_in = features.shape
    per1, per2 = conv1_weight.shape[1], conv2_weight.shape[1]
    chans_out = conv1_weight.shape[2]
    slabs, nrow, ncol = (lax.axis_size(a) for a in ("tm", "row", "col"))
    n = nrow * ncol
    height, width = nrow * rows, ncol * cols
    area = height * width
    fits = frames == 2 and per1 == LANES and 2 * per2 == LANES and cols % 16 == 0
    fits = fits and n == 4 and slabs % 2 == 0 and width & (width - 1) == 0 and GROUPS % n == 0 and height % 2 == 0
    if not fits:
        return per_device_gathered(
            features, gn1_gain, gn1_bias, conv1_weight, conv1_bias, skip_weight,
            gn2_gain, gn2_bias, conv2_weight, conv2_bias,
        )
    bf16, f32 = jnp.bfloat16, jnp.float32
    vmem, dma = pltpu.VMEM, pltpu.SemaphoreType.DMA
    half = area // 2
    scratch = [
        vmem((1, chans_in), f32),
        vmem((1, chans_in), f32),
        vmem((1, chans_out), f32),
        vmem((1, chans_out), f32),
        vmem((1, chans_out), f32),
        vmem((1, chans_out), f32),
        vmem((frames, rows, cols, chans_in), bf16),
        vmem((4, height, width, LANES), bf16),
        vmem((27 * per1, chans_out), bf16),
        vmem((per1, chans_out), bf16),
        vmem((2, 2, 9, 2 * per2, chans_out), bf16),
        vmem((4, height + 2, width, 3 * LANES), bf16),
        vmem((2, height + 2, width, 3 * LANES), bf16),
        vmem((2, area, chans_out), f32),
        vmem((2, ncol, nrow, half, LANES), f32),
        vmem((2, ncol, nrow, half, LANES), bf16),
        vmem((2, ncol, nrow, half, LANES), bf16),
        vmem((2, nrow, half, LANES), f32),
        vmem((2, nrow, half, LANES), bf16),
        vmem((2, nrow, half, LANES), bf16),
        vmem((slabs // 2, 2 * n, LANES), f32),
        vmem((2 * n, 2 * n, LANES), f32),
        vmem((slabs, 8, LANES), f32),
        vmem((2, 2, half, LANES), f32),
        vmem((2, half, LANES), bf16),
        vmem((2, half, LANES), bf16),
        vmem((2, area, chans_out), f32),
        vmem((2, ncol, nrow, rows, cols, chans_out), f32),
        vmem((2, ncol, nrow, rows, cols, chans_out), bf16),
        vmem((2, ncol, nrow, rows, cols, chans_out), bf16),
        vmem((2, nrow, rows, cols, chans_out), f32),
        vmem((2, nrow, rows, cols, chans_out), bf16),
        vmem((2, nrow, rows, cols, chans_out), bf16),
        dma((8,)), dma((6,)), dma((2,)), dma((n,)), dma((n,)), dma((n,)), dma((n,)),
        dma((slabs,)), dma((slabs,)), dma((2 * n,)), dma((2 * n,)), dma((slabs,)), dma((slabs,)),
        dma((2, ncol)), dma((2, ncol)), dma((2, nrow)), dma((2, nrow)),
        dma((2, ncol)), dma((2, ncol)), dma((2, nrow)), dma((2, nrow)),
        dma((2,)), dma((2,)),
    ]
    stays = pl.BlockSpec(memory_space=pltpu.HBM)
    inside = pl.BlockSpec(memory_space=pltpu.VMEM)
    sizes = (slabs, nrow, ncol, rows, cols, per1, per2)
    flops = 2 * 2 * area * chans_out * (28 * per1 + 27 * per2)
    operands = (
        features,
        gn1_gain.reshape(1, -1),
        gn1_bias.reshape(1, -1),
        conv1_weight.reshape(27 * per1, chans_out),
        conv1_bias.reshape(1, -1),
        skip_weight.reshape(per1, chans_out),
        gn2_gain.reshape(1, -1),
        gn2_bias.reshape(1, -1),
        conv2_weight.reshape(3, 9, per2, chans_out),
        conv2_bias.reshape(1, -1),
    )
    return pl.pallas_call(
        functools.partial(block_kernel, sizes),
        out_shape=jax.ShapeDtypeStruct((frames, rows, cols, chans_out), bf16),
        in_specs=[stays] * 10,
        out_specs=inside,
        scratch_shapes=scratch,
        compiler_params=pltpu.CompilerParams(
            collective_id=0, has_side_effects=True, vmem_limit_bytes=48 * 1024 * 1024
        ),
        cost_estimate=pl.CostEstimate(
            flops=flops, bytes_accessed=4 * 1024 * 1024, transcendentals=6 * area * LANES
        ),
        name="residual_block",
    )(*(pltpu.with_memory_space_constraint(x, pltpu.HBM) for x in operands))


def solution(mesh):
    in_specs = (
        P("tm", "row", "col", None),
        P(),
        P(),
        P(None, ("row", "col"), None),
        P(),
        P(None, ("row", "col"), None),
        P(),
        P(),
        P(None, ("row", "col"), None),
        P(),
    )
    out_specs = P("tm", "row", "col", None)
    return jax.shard_map(
        per_device, mesh=mesh, in_specs=in_specs, out_specs=out_specs, check_vma=False
    )
```

```python
import functools

import jax
import jax.numpy as jnp
from jax import lax
from jax.experimental import pallas as pl
from jax.experimental.pallas import tpu as pltpu
from jax.sharding import PartitionSpec as P

GROUPS = 32


def passed_along(block, axis, distance):
    devices = range(lax.axis_size(axis))
    route = [(i - distance, i) for i in devices if i - distance in devices]
    return lax.ppermute(block, axis, route)


def with_halo(array, sides, width):
    for axis, dim in sides:
        size, length = (lax.axis_size(axis), array.shape[dim])
        up = [(i, (i + 1) % size) for i in range(size - 1)]
        down = [(j, i) for i, j in up]
        last = lax.slice_in_dim(array, length - width, length, axis=dim)
        leading = lax.slice_in_dim(array, 0, width, axis=dim)
        before = lax.ppermute(last, axis, up)
        after = lax.ppermute(leading, axis, down)
        array = jnp.concatenate([before, array, after], axis=dim)
    return array


def group_silu(values, gain, shift, groups, total_rows):
    chans = values.shape[-1]
    per_group = chans // groups
    grouped = values.reshape(-1, groups, per_group)
    count = float(total_rows * per_group)
    mean = lax.psum(jnp.sum(grouped, axis=(0, 2)), ("tm", "row", "col")) / count
    centred = grouped - mean[None, :, None]
    spread = lax.psum(jnp.sum(centred * centred, axis=(0, 2)), ("tm", "row", "col")) / count
    normed = (grouped - mean[None, :, None]) * lax.rsqrt(spread + 1e-06)[None, :, None]
    normed = normed.reshape(values.shape) * gain + shift
    return jax.nn.silu(normed).astype(jnp.bfloat16)


def conv_taps(padded, weight, frames, rows, cols):
    chans = padded.shape[3]
    total = jnp.zeros((frames * rows * cols, weight.shape[2]), jnp.float32)
    for dt in range(3):
        pieces = []
        for tap in range(9):
            dy, dx = (tap // 3, tap % 3)
            pieces.append(
                padded[dt : dt + frames, dy : dy + rows, dx : dx + cols].reshape(-1, chans)
            )
        stacked = jnp.concatenate(pieces, axis=1)
        flat_weight = weight[9 * dt : 9 * dt + 9].reshape(9 * chans, weight.shape[2])
        total = total + jnp.dot(stacked, flat_weight, preferred_element_type=jnp.float32)
    return total


def time_edge(earlier, volume):
    first_twice = jnp.concatenate([volume[:1], volume[:1]], axis=0)
    earlier = jnp.where(lax.axis_index("tm") == 0, first_twice, earlier)
    return jnp.concatenate([earlier, volume], axis=0)


def edge_rows(padded):
    place = lax.axis_index("row")
    last = lax.axis_size("row") - 1
    top = jnp.where(place == 0, padded[:, 1:2], padded[:, 0:1])
    bottom = jnp.where(place == last, padded[:, -2:-1], padded[:, -1:])
    return jnp.concatenate([top, padded[:, 1:-1], bottom], axis=1)


def edge_cols(padded):
    place = lax.axis_index("col")
    last = lax.axis_size("col") - 1
    left = jnp.where(place == 0, padded[:, :, 1:2], padded[:, :, 0:1])
    right = jnp.where(place == last, padded[:, :, -2:-1], padded[:, :, -1:])
    return jnp.concatenate([left, padded[:, :, 1:-1], right], axis=2)


def per_device_gathered(
    features,
    gn1_gain,
    gn1_bias,
    conv1_weight,
    conv1_bias,
    skip_weight,
    gn2_gain,
    gn2_bias,
    conv2_weight,
    conv2_bias,
):
    frames, rows, cols, chans_in = features.shape
    chans_out = conv1_weight.shape[2]
    groups = GROUPS
    nrow = lax.axis_size("row")
    ncol = lax.axis_size("col")
    total_rows = lax.axis_size("tm") * nrow * ncol * frames * rows * cols
    flat_features = features.reshape(-1, chans_in)
    hidden1 = group_silu(features.astype(jnp.float32), gn1_gain, gn1_bias, groups, total_rows)
    earlier = passed_along(hidden1, "tm", 1)
    extended = time_edge(earlier, hidden1)
    padded = with_halo(extended, (("row", 1), ("col", 2)), 1)
    padded = edge_cols(edge_rows(padded))
    window = padded
    first = conv_taps(
        window, lax.all_gather(conv1_weight, ("row", "col"), axis=1, tiled=True), frames, rows, cols
    )
    second = jnp.dot(
        flat_features,
        lax.all_gather(skip_weight, ("row", "col"), axis=1, tiled=True)[0],
        preferred_element_type=jnp.float32,
    )
    middle = (first + conv1_bias).reshape(frames, rows, cols, chans_out)
    hidden2 = group_silu(middle, gn2_gain, gn2_bias, groups, total_rows)
    earlier_mid = passed_along(hidden2, "tm", 1)
    extended_mid = time_edge(earlier_mid, hidden2)
    padded_mid = with_halo(extended_mid, (("row", 1), ("col", 2)), 1)
    padded_mid = edge_cols(edge_rows(padded_mid))
    window = padded_mid
    conv_second = conv_taps(
        window, lax.all_gather(conv2_weight, ("row", "col"), axis=1, tiled=True), frames, rows, cols
    )
    block_out = (second + conv_second + conv2_bias).astype(jnp.bfloat16)
    return block_out.reshape(frames, rows, cols, chans_out)


MESH = pl.DeviceIdType.MESH
LANES = 128


def lane_of(shape):
    return lax.broadcasted_iota(jnp.int32, shape, len(shape) - 1)


def silu(a):
    half = 0.5 * a
    return half + half * jnp.tanh(half)


def lane_stats(x):
    mean = jnp.sum(x, axis=0, keepdims=True) * (1.0 / x.shape[0])
    spread = jnp.sum((x - mean) ** 2, axis=0, keepdims=True)
    row = lax.broadcasted_iota(jnp.int32, (8, LANES), 0)
    return jnp.where(row == 0, mean, jnp.where(row == 1, spread, 0.0))


def group_sums(x, same):
    high = x.astype(jnp.bfloat16).astype(jnp.float32)
    rest = x - high
    middle = rest.astype(jnp.bfloat16).astype(jnp.float32)
    row = lax.broadcasted_iota(jnp.int32, (16, LANES), 0)
    parts = jnp.where(row == 0, high, jnp.where(row == 1, middle, rest - middle))
    parts = jnp.where(row < 3, parts, 0.0).astype(jnp.bfloat16)
    sums = jnp.dot(parts, same, preferred_element_type=jnp.float32)
    return jnp.sum(sums, axis=0, keepdims=True)


def group_stats(means, spreads, same, lanes, count):
    parts = means.shape[0]
    mean = jnp.sum(means, axis=0) * (1.0 / parts)
    spread = jnp.sum(spreads, axis=0) + count * jnp.sum((means - mean[None]) ** 2, axis=0)
    group_mean = group_sums(mean, same) * (1.0 / lanes)
    spread = spread + (count * parts) * (mean - group_mean) ** 2
    total = group_sums(spread, same)
    return group_mean, lax.rsqrt(total * (1.0 / (count * parts * lanes)) + 1e-6)


def side_shifts(h, cols):
    col = lax.broadcasted_iota(jnp.int32, h.shape, 0) & (cols - 1)
    length = h.shape[0]
    left = jnp.where(col == 0, h, pltpu.roll(h, 1, 0))
    right = jnp.where(col == cols - 1, h, pltpu.roll(h, length - 1, 0))
    return left, right


def block_kernel(
    sizes,
    feat, gain1_hbm, shift1_hbm, w1, bias1_hbm, wskip, gain2_hbm, shift2_hbm, w2, bias2_hbm,
    out,
    gain1, shift1, bias1, gain2, shift2, bias2, featv, xall, w1v, wsv, wcat, xp1, xp2,
    acc, part1, send1, recv1, sum1, send1b, recv1b, stat0, statg, stat2,
    mids, midbf, prevbf, scut, part2, send2, recv2, sum2, send2b, recv2b,
    w_sem, p_sem, own_sem, fs_sem, fr_sem, fps_sem, fpr_sem,
    s1s_sem, s1r_sem, sgs_sem, sgr_sem, s2s_sem, s2r_sem,
    r1s_sem, r1r_sem, r1bs_sem, r1br_sem, r2s_sem, r2r_sem, r2bs_sem, r2br_sem,
    ps_sem, pr_sem,
):
    slabs, nrow, ncol, rows, cols, per1, per2 = sizes
    n = nrow * ncol
    height, width = nrow * rows, ncol * cols
    area = height * width
    t = lax.axis_index("tm")
    r = lax.axis_index("row")
    c = lax.axis_index("col")
    me = r * ncol + c

    def place(i):
        return lax.div(i, ncol), lax.rem(i, ncol)

    def ident(ti, i):
        ri, ci = place(i)
        return {"tm": ti, "row": ri, "col": ci}

    def member(delta):
        return lax.rem(r + delta // ncol, nrow) * ncol + lax.rem(c + delta % ncol, ncol)

    def slab(delta):
        return lax.rem(t + delta, slabs)

    q = slabs // 2
    side = lax.div(t, q)
    spot = lax.rem(t, q)
    far = slab(q)

    def near(delta):
        return side * q + lax.rem(spot + delta, q)

    loads = [
        pltpu.make_async_copy(w1, w1v, w_sem.at[0]),
        pltpu.make_async_copy(wskip, wsv, w_sem.at[1]),
    ]
    for i, (f, p, place_in, dt) in enumerate(
        ((0, 0, 0, 0), (0, 0, 1, 1), (0, 1, 0, 2), (1, 0, 1, 0), (1, 1, 0, 1), (1, 1, 1, 2))
    ):
        lo = place_in * per2
        loads.append(
            pltpu.make_async_copy(
                w2.at[dt], wcat.at[f, p, :, lo : lo + per2, :], w_sem.at[2 + i]
            )
        )
    params = [
        pltpu.make_async_copy(source, target, p_sem.at[i])
        for i, (source, target) in enumerate(
            (
                (gain1_hbm, gain1), (shift1_hbm, shift1), (bias1_hbm, bias1),
                (gain2_hbm, gain2), (shift2_hbm, shift2), (bias2_hbm, bias2),
            )
        )
    ]

    def window(frame0, i):
        ri, ci = place(i)
        top = ri * rows
        left = pl.multiple_of(ci * cols, cols)
        return xall.at[frame0 : frame0 + 2, pl.ds(top, rows), pl.ds(left, cols), :]

    def chunk(i):
        return feat.at[:, :, :, pl.ds(pl.multiple_of(i * LANES, LANES), LANES)]

    whole = pltpu.make_async_copy(feat, featv, own_sem.at[1])
    whole.start()

    barrier = pltpu.get_barrier_semaphore()
    for delta in range(n):
        pl.semaphore_signal(barrier, inc=1, device_id=ident(far, member(delta)), device_id_type=MESH)

    @pl.when(t > 0)
    def _():
        for delta in range(n):
            pl.semaphore_signal(
                barrier, inc=1, device_id=ident(t - 1, member(delta)), device_id_type=MESH
            )

    for delta in range(1, q):
        pl.semaphore_signal(barrier, inc=1, device_id=ident(near(delta), me), device_id_type=MESH)
    for delta in range(1, n):
        pl.semaphore_signal(barrier, inc=1, device_id=ident(t, member(delta)), device_id_type=MESH)
    own = pltpu.make_async_copy(chunk(me), window(2, me), own_sem.at[0])
    own.start()
    blank = jnp.zeros((9, per2, wcat.shape[4]), wcat.dtype)
    wcat[0, 1, :, per2:, :] = blank
    wcat[1, 0, :, :per2, :] = blank

    row8 = lax.broadcasted_iota(jnp.int32, (2 * n, LANES), 0)
    spots = float(2 * rows * cols)
    whole.wait()
    x = featv[...].reshape(2 * rows * cols, n * LANES).astype(jnp.float32)
    lane_mean = jnp.sum(x, axis=0, keepdims=True) * (1.0 / spots)
    lane_spread = jnp.sum((x - lane_mean) ** 2, axis=0, keepdims=True)
    tile = jnp.zeros((2 * n, LANES), jnp.float32)
    for d in range(n):
        at = slice(d * LANES, (d + 1) * LANES)
        tile = jnp.where(row8 == d, lane_mean[:, at], tile)
        tile = jnp.where(row8 == n + d, lane_spread[:, at], tile)
    stat0[spot] = tile

    pl.semaphore_wait(barrier, jnp.where(t < slabs - 1, n, 0) + 2 * n + q - 2)

    def stat_copy(buf, source, target, ssem, rsem):
        return pltpu.make_async_remote_copy(
            src_ref=buf.at[source], dst_ref=buf.at[source],
            send_sem=ssem.at[target], recv_sem=rsem.at[source],
            device_id=ident(target, me), device_id_type=MESH,
        )

    def near_copy(source, target):
        return pltpu.make_async_remote_copy(
            src_ref=stat0.at[lax.rem(source, q)], dst_ref=stat0.at[lax.rem(source, q)],
            send_sem=s1s_sem.at[lax.rem(target, q)], recv_sem=s1r_sem.at[lax.rem(source, q)],
            device_id=ident(target, me), device_id_type=MESH,
        )

    def share_copy(t_from, source, t_to, target):
        slot = lax.div(t_from, q) * n + source
        return pltpu.make_async_remote_copy(
            src_ref=statg.at[slot], dst_ref=statg.at[slot],
            send_sem=sgs_sem.at[lax.div(t_to, q) * n + target], recv_sem=sgr_sem.at[slot],
            device_id=ident(t_to, target), device_id_type=MESH,
        )

    sharers = [(far, delta) for delta in reversed(range(n))]
    sharers += [(t, delta) for delta in reversed(range(1, n))]

    for delta in reversed(range(1, q)):
        near_copy(t, near(delta)).start()

    def feat_copy(source, target):
        return pltpu.make_async_remote_copy(
            src_ref=chunk(target), dst_ref=window(2, source),
            send_sem=fs_sem.at[target], recv_sem=fr_sem.at[source],
            device_id=ident(t, target), device_id_type=MESH,
        )

    def feat_next(source, target, to):
        return pltpu.make_async_remote_copy(
            src_ref=chunk(target), dst_ref=window(0, source),
            send_sem=fps_sem.at[target], recv_sem=fpr_sem.at[source],
            device_id=ident(to, target), device_id_type=MESH,
        )

    @pl.when(t < slabs - 1)
    def _():
        for delta in range(ncol):
            feat_next(me, member(delta), t + 1).start()

    for delta in reversed(range(1, n)):
        feat_copy(me, member(delta)).start()

    for load in params + loads:
        load.start()

    for delta in range(1, q):
        near_copy(near(delta), t).wait_recv()
    stats = stat0[...]
    total = jnp.sum(stats, axis=0)
    mean = total * (1.0 / q)
    off = spots * jnp.sum((stats - mean[None]) ** 2, axis=0)
    statg[side * n + me] = jnp.where(row8 < n, mean, total + pltpu.roll(off, n, 0))
    for slab_to, delta in sharers:
        share_copy(t, me, slab_to, member(delta)).start()

    @pl.when(t < slabs - 1)
    def _():
        for delta in range(ncol, n):
            feat_next(me, member(delta), t + 1).start()

    lane = lane_of((8, LANES))
    lane_in = lax.broadcasted_iota(jnp.int32, (LANES, LANES), 0)
    lane_to = lane_of((LANES, LANES))
    size1 = per1 // (GROUPS // n)
    size2 = per2 // (GROUPS // n)
    same1 = (lane_in // size1 == lane_to // size1).astype(jnp.bfloat16)
    same2 = ((lane_in % per2) // size2 == (lane_to % per2) // size2).astype(jnp.bfloat16)

    def own_full(ref):
        result = ref[0:1, 0:LANES]
        for d in range(1, n):
            result = jnp.where(me == d, ref[0:1, d * LANES : (d + 1) * LANES], result)
        return result

    def own_twice(ref):
        result = jnp.zeros((8, LANES), jnp.float32)
        for d in range(n):
            k = d // 2 * LANES
            seg = jnp.broadcast_to(ref[0:1, k : k + LANES], (8, LANES))
            turned = pltpu.roll(seg, per2, 1)
            twice = jnp.where((lane < per2) == (d % 2 == 0), seg, turned)
            result = jnp.where(me == d, twice, result)
        return result[0:1]

    for load in params:
        load.wait()
    g1, b1 = own_full(gain1), own_full(shift1)
    g2, b2, c1 = own_twice(gain2), own_twice(shift2), own_twice(bias1)

    own.wait()
    for delta in range(1, n):
        feat_copy(member(delta), me).wait_recv()
    loads[1].wait()
    for f in range(2):
        x = xall[2 + f].reshape(area, LANES)
        scut[f] = jnp.dot(x, wsv[...], preferred_element_type=jnp.float32)

    for slab_from, delta in sharers:
        share_copy(slab_from, member(delta), t, me).wait_recv()
    stats = statg[...]
    pick = lax.broadcasted_iota(jnp.int32, stats.shape, 1)
    means = jnp.sum(jnp.where(pick == me, stats, 0.0), axis=1, keepdims=True)
    spreads = jnp.sum(jnp.where(pick == n + me, stats, 0.0), axis=1, keepdims=True)
    mean, inv = group_stats(means, spreads, same1, size1, spots * q)
    scale = inv * g1

    def normalise(f):
        x = xall[f].reshape(area, LANES).astype(jnp.float32)
        h = silu((x - mean) * scale + b1)
        left, right = side_shifts(h, width)
        for dx, part in enumerate((left, h, right)):
            part = part.astype(jnp.bfloat16).reshape(height, width, LANES)
            lanes = slice(dx * LANES, (dx + 1) * LANES)
            xp1[f, 1 : height + 1, :, lanes] = part
            xp1[f, 0, :, lanes] = part[0]
            xp1[f, height + 1, :, lanes] = part[height - 1]

    depth = 9 * LANES
    tall = height // 2
    half = tall * width

    def conv1(dt, s):
        rows_in = [xp1[dt : dt + 2, s * tall + dy : (s + 1) * tall + dy] for dy in range(3)]
        lhs = jnp.concatenate([x.reshape(2 * half, 3 * LANES) for x in rows_in], axis=1)
        rhs = w1v[dt * depth : (dt + 1) * depth, :]
        return jnp.dot(lhs, rhs, preferred_element_type=jnp.float32)

    normalise(2)
    normalise(3)
    loads[0].wait()
    for s in range(2):
        acc[s] = conv1(2, s)

    @pl.when(t > 0)
    def _():
        for delta in range(n):
            feat_next(member(delta), me, t).wait_recv()

    @pl.when(t == 0)
    def _():
        xall[0] = xall[2]
        xall[1] = xall[2]

    normalise(0)
    normalise(1)

    def core_copy(src, dst, source, target, s, ssem, rsem):
        return pltpu.make_async_remote_copy(
            src_ref=src.at[s, target], dst_ref=dst.at[s, source],
            send_sem=ssem.at[s, target], recv_sem=rsem.at[s, source],
            device_id={"tm": t, "row": r, "col": target}, device_id_type=MESH,
        )

    def row_copy(src, dst, source, target, s, ssem, rsem):
        return pltpu.make_async_remote_copy(
            src_ref=src.at[s, target], dst_ref=dst.at[s, source],
            send_sem=ssem.at[s, target], recv_sem=rsem.at[s, source],
            device_id={"tm": t, "row": target, "col": c}, device_id_type=MESH,
        )

    cores = [lax.rem(c + delta, ncol) for delta in range(1, ncol)]
    others = [lax.rem(r + delta, nrow) for delta in range(1, nrow)]

    def to_cores(stage, s):
        send, recv, ssem, rsem = stage
        for core in cores:
            core_copy(send, recv, c, core, s, ssem, rsem).start()

    def to_rows(stage, part, total, stage_b, s):
        send, recv, ssem, rsem = stage
        send_b, recv_b, ssem_b, rsem_b = stage_b
        summed = part[s, c]
        for core in cores:
            core_copy(send, recv, core, c, s, ssem, rsem).wait_recv()
            summed = summed + recv[s, core].astype(jnp.float32)
        total[s] = summed
        send_b[s] = summed.astype(jnp.bfloat16)
        for other in others:
            row_copy(send_b, recv_b, r, other, s, ssem_b, rsem_b).start()

    def from_rows(total, stage_b, s):
        send_b, recv_b, ssem_b, rsem_b = stage_b
        result = total[s, r]
        for other in others:
            row_copy(send_b, recv_b, other, r, s, ssem_b, rsem_b).wait_recv()
            result = result + recv_b[s, other].astype(jnp.float32)
        return result

    def sent_to_cores(stage):
        send, recv, ssem, rsem = stage
        for s in range(2):
            for core in cores:
                core_copy(send, recv, c, core, s, ssem, rsem).wait_send()

    def sent_to_rows(stage):
        send, recv, ssem, rsem = stage
        for s in range(2):
            for other in others:
                row_copy(send, recv, r, other, s, ssem, rsem).wait_send()

    first = (send1, recv1, r1s_sem, r1r_sem)
    first_b = (send1b, recv1b, r1bs_sem, r1br_sem)
    second = (send2, recv2, r2s_sem, r2r_sem)
    second_b = (send2b, recv2b, r2bs_sem, r2br_sem)

    wide = lane_of((half, LANES))
    for s in range(2):
        total = acc[s] + conv1(1, s) + conv1(0, s)
        for d in range(n):
            k = d // 2 * LANES
            one, two = total[:half, k : k + LANES], total[half:, k : k + LANES]
            if d % 2 == 0:
                packed = jnp.where(wide < per2, one, pltpu.roll(two, per2, 1))
            else:
                packed = jnp.where(wide < per2, pltpu.roll(one, per2, 1), two)
            part1[s, d % ncol, d // ncol] = packed
            send1[s, d % ncol, d // ncol] = packed.astype(jnp.bfloat16)
        to_cores(first, s)
    for s in range(2):
        to_rows(first, part1, sum1, first_b, s)

    for delta in range(1, n):
        feat_copy(me, member(delta)).wait_send()
    for slab_to, delta in sharers:
        share_copy(t, me, slab_to, member(delta)).wait_send()
    for delta in range(1, q):
        near_copy(t, near(delta)).wait_send()

    @pl.when(t < slabs - 1)
    def _():
        for delta in range(n):
            feat_next(me, member(delta), t + 1).wait_send()

    def mid_copy(to, s):
        return pltpu.make_async_remote_copy(
            src_ref=midbf.at[s], dst_ref=prevbf.at[s],
            send_sem=ps_sem.at[s], recv_sem=pr_sem.at[s],
            device_id=ident(to, me), device_id_type=MESH,
        )

    def pass_on(s):
        @pl.when(t < slabs - 1)
        def _():
            mid_copy(t + 1, s).start()

    for s in range(2):
        middle = from_rows(sum1, first_b, s) + c1
        midbf[s] = middle.astype(jnp.bfloat16)
        mids[1, s] = middle
        if s == 0:
            pass_on(0)

    stat2[t] = lane_stats(mids[1].reshape(area, LANES))
    for delta in reversed(range(1, slabs)):
        stat_copy(stat2, t, slab(delta), s2s_sem, s2r_sem).start()
    pass_on(1)

    for delta in range(1, slabs):
        stat_copy(stat2, slab(delta), t, s2s_sem, s2r_sem).wait_recv()
    sent_to_cores(first)
    sent_to_rows(first_b)
    stats = stat2[...]
    mean, inv = group_stats(stats[:, 0:1], stats[:, 1:2], same2, 2 * size2, float(area))
    scale = inv * g2

    def normalise_mid(i):
        h = silu((mids[i].reshape(area, LANES) - mean) * scale + b2)
        left, right = side_shifts(h, width)
        for dx, part in enumerate((left, h, right)):
            part = part.astype(jnp.bfloat16).reshape(height, width, LANES)
            lanes = slice(dx * LANES, (dx + 1) * LANES)
            xp2[i, 1 : height + 1, :, lanes] = part
            xp2[i, 0, :, lanes] = part[0]
            xp2[i, height + 1, :, lanes] = part[height - 1]

    def conv2(f, i):
        rows_in = [xp2[i, dy : dy + height].reshape(area, 3 * LANES) for dy in range(3)]
        rhs = wcat[f, i].reshape(9 * LANES, wcat.shape[4])
        return jnp.dot(
            jnp.concatenate(rows_in, axis=1), rhs, preferred_element_type=jnp.float32
        )

    normalise_mid(1)
    for load in loads[2:]:
        load.wait()
    for f in range(2):
        scut[f] = scut[f] + conv2(f, 1)

    @pl.when(t > 0)
    def _():
        for s in range(2):
            mid_copy(t, s).wait_recv()
            mids[0, s] = prevbf[s].astype(jnp.float32)

    @pl.when(t == 0)
    def _():
        for s in range(2):
            middle = mids[1, s]
            mids[0, s] = jnp.where(wide < per2, middle, pltpu.roll(middle, per2, 1))

    normalise_mid(0)
    for f in range(2):
        total = (scut[f] + conv2(f, 0)).reshape(nrow, rows, width, wcat.shape[4])
        for ci in range(ncol):
            piece = total[:, :, ci * cols : (ci + 1) * cols]
            part2[f, ci] = piece
            send2[f, ci] = piece.astype(jnp.bfloat16)
        to_cores(second, f)
    for f in range(2):
        to_rows(second, part2, sum2, second_b, f)
    for delta in range(1, slabs):
        stat_copy(stat2, t, slab(delta), s2s_sem, s2r_sem).wait_send()

    @pl.when(t < slabs - 1)
    def _():
        for s in range(2):
            mid_copy(t + 1, s).wait_send()

    sent_to_cores(second)
    last = bias2[...].reshape(1, 1, -1)
    for f in range(2):
        out[f] = (from_rows(sum2, second_b, f) + last).astype(out.dtype)

    sent_to_rows(second_b)


def per_device(
    features,
    gn1_gain,
    gn1_bias,
    conv1_weight,
    conv1_bias,
    skip_weight,
    gn2_gain,
    gn2_bias,
    conv2_weight,
    conv2_bias,
):
    frames, rows, cols, chans_in = features.shape
    per1, per2 = conv1_weight.shape[1], conv2_weight.shape[1]
    chans_out = conv1_weight.shape[2]
    slabs, nrow, ncol = (lax.axis_size(a) for a in ("tm", "row", "col"))
    n = nrow * ncol
    height, width = nrow * rows, ncol * cols
    area = height * width
    fits = frames == 2 and per1 == LANES and 2 * per2 == LANES and cols % 16 == 0
    fits = fits and n == 4 and slabs % 2 == 0 and width & (width - 1) == 0 and GROUPS % n == 0 and height % 2 == 0
    if not fits:
        return per_device_gathered(
            features, gn1_gain, gn1_bias, conv1_weight, conv1_bias, skip_weight,
            gn2_gain, gn2_bias, conv2_weight, conv2_bias,
        )
    bf16, f32 = jnp.bfloat16, jnp.float32
    vmem, dma = pltpu.VMEM, pltpu.SemaphoreType.DMA
    half = area // 2
    scratch = [
        vmem((1, chans_in), f32),
        vmem((1, chans_in), f32),
        vmem((1, chans_out), f32),
        vmem((1, chans_out), f32),
        vmem((1, chans_out), f32),
        vmem((1, chans_out), f32),
        vmem((frames, rows, cols, chans_in), bf16),
        vmem((4, height, width, LANES), bf16),
        vmem((27 * per1, chans_out), bf16),
        vmem((per1, chans_out), bf16),
        vmem((2, 2, 9, 2 * per2, chans_out), bf16),
        vmem((4, height + 2, width, 3 * LANES), bf16),
        vmem((2, height + 2, width, 3 * LANES), bf16),
        vmem((2, area, chans_out), f32),
        vmem((2, ncol, nrow, half, LANES), f32),
        vmem((2, ncol, nrow, half, LANES), bf16),
        vmem((2, ncol, nrow, half, LANES), bf16),
        vmem((2, nrow, half, LANES), f32),
        vmem((2, nrow, half, LANES), bf16),
        vmem((2, nrow, half, LANES), bf16),
        vmem((slabs // 2, 2 * n, LANES), f32),
        vmem((2 * n, 2 * n, LANES), f32),
        vmem((slabs, 8, LANES), f32),
        vmem((2, 2, half, LANES), f32),
        vmem((2, half, LANES), bf16),
        vmem((2, half, LANES), bf16),
        vmem((2, area, chans_out), f32),
        vmem((2, ncol, nrow, rows, cols, chans_out), f32),
        vmem((2, ncol, nrow, rows, cols, chans_out), bf16),
        vmem((2, ncol, nrow, rows, cols, chans_out), bf16),
        vmem((2, nrow, rows, cols, chans_out), f32),
        vmem((2, nrow, rows, cols, chans_out), bf16),
        vmem((2, nrow, rows, cols, chans_out), bf16),
        dma((8,)), dma((6,)), dma((2,)), dma((n,)), dma((n,)), dma((n,)), dma((n,)),
        dma((slabs,)), dma((slabs,)), dma((2 * n,)), dma((2 * n,)), dma((slabs,)), dma((slabs,)),
        dma((2, ncol)), dma((2, ncol)), dma((2, nrow)), dma((2, nrow)),
        dma((2, ncol)), dma((2, ncol)), dma((2, nrow)), dma((2, nrow)),
        dma((2,)), dma((2,)),
    ]
    stays = pl.BlockSpec(memory_space=pltpu.HBM)
    inside = pl.BlockSpec(memory_space=pltpu.VMEM)
    sizes = (slabs, nrow, ncol, rows, cols, per1, per2)
    flops = 2 * 2 * area * chans_out * (28 * per1 + 27 * per2)
    operands = (
        features,
        gn1_gain.reshape(1, -1),
        gn1_bias.reshape(1, -1),
        conv1_weight.reshape(27 * per1, chans_out),
        conv1_bias.reshape(1, -1),
        skip_weight.reshape(per1, chans_out),
        gn2_gain.reshape(1, -1),
        gn2_bias.reshape(1, -1),
        conv2_weight.reshape(3, 9, per2, chans_out),
        conv2_bias.reshape(1, -1),
    )
    return pl.pallas_call(
        functools.partial(block_kernel, sizes),
        out_shape=jax.ShapeDtypeStruct((frames, rows, cols, chans_out), bf16),
        in_specs=[stays] * 10,
        out_specs=inside,
        scratch_shapes=scratch,
        compiler_params=pltpu.CompilerParams(
            collective_id=0, has_side_effects=True, vmem_limit_bytes=48 * 1024 * 1024
        ),
        cost_estimate=pl.CostEstimate(
            flops=flops, bytes_accessed=4 * 1024 * 1024, transcendentals=6 * area * LANES
        ),
        name="residual_block",
    )(*(pltpu.with_memory_space_constraint(x, pltpu.HBM) for x in operands))


def solution(mesh):
    in_specs = (
        P("tm", "row", "col", None),
        P(),
        P(),
        P(None, ("row", "col"), None),
        P(),
        P(None, ("row", "col"), None),
        P(),
        P(),
        P(None, ("row", "col"), None),
        P(),
    )
    out_specs = P("tm", "row", "col", None)
    return jax.shard_map(
        per_device, mesh=mesh, in_specs=in_specs, out_specs=out_specs, check_vma=False
    )
```
